32 devices in a mesh: groups: 2 (over x), ctx: 16 (over z, y, core).
Axes of the slice: x: 2, y: 2, z: 4, core: 2. Of those that a mesh axis runs over, the one named last changes fastest.
Arguments:
- tokens: bfloat16 [16384, 8192], P(('groups', 'ctx')), parts along dimension 0, may hold values from -6 to 6
- key_down: bfloat16 [8192, 512], P('ctx'), may hold values from -0.0625 to 0.0625
- value_down: bfloat16 [8192, 512], P('ctx'), may hold values from -0.0625 to 0.0625
- key_up: bfloat16 [512, 1024], replicated, may hold values from -0.25 to 0.25
- value_up: bfloat16 [512, 1024], replicated, may hold values from -0.25 to 0.25
- prompt_lens: int32 [8], P('groups'), parts along dimension 0, may hold values from 1 to 4096, 8192 in all
- queries: bfloat16 [4, 8, 8192], P(None, 'groups'), parts along dimension 1, may hold values from -136 to 136
- new_latent: bfloat16 [4, 8, 1024], P(None, 'groups'), parts along dimension 1, may hold values from -6 to 6
Outputs:
- attention: bfloat16 [4, 8, 8192], P(None, 'groups'), parts along dimension 1
The draws below stay inside these ranges and needn't reach their ends.
There are 2 independent parts, one for each index of `groups`. The reference program is written for one: setup_inputs(seed, part) draws one part's arguments, and reference() takes and returns one part's arrays. A program takes and returns all parts, laid end to end along the dimension named above; an argument that names none is the same for every part. Nothing has to cross between parts.
All inputs are finite; a program needn't handle non-finite values.
Results may differ from the reference program's by a relative error of at most 0.015.
The reference program's roundings to bfloat16 on the way count: a program that leaves them out, or rounds other values in their place, can miss the bound.
Values may be sent and summed in bfloat16 or wider, within the bound.
No kernel may reach another device: no remote copies, remote signals or barrier semaphores. Data moves between devices by JAX's collectives and lax.ppermute only.
A program may use at most 192 MiB of HBM per device.

```python
import math
import jax
import jax.numpy as jnp
import numpy as np
from jax import lax

D = 8192
QH = 64
KVH = 8
DH = 128
R = 512
REQS = 4
STEPS = 4
TOKENS = 8192


def draw_queries(key, part):
    key = jax.random.fold_in(key, 11)
    base = jnp.clip(jax.random.normal(key, (STEPS, REQS, QH * DH), jnp.float32), -8.0, 8.0)
    return base.astype(jnp.bfloat16)


def level_of(key, dims, shards, least, largest):
    loudness, own = 1.0, jax.random.fold_in(key, 6)
    for axis_at, blocks in shards:
        draws = jnp.exp(jax.random.uniform(jax.random.fold_in(own, axis_at), (blocks,), jnp.float32, least / len(shards), largest / len(shards)))
        loudness = loudness * jnp.repeat(draws, dims[axis_at] // blocks).reshape([-1 if axis == axis_at else 1 for axis in range(len(dims))])
    return loudness


def split_up(amount, total, limit, lean):
    weights = [(1 << 20) // math.isqrt(standing ** lean) + 1 for standing in range(2, amount + 1)]
    surplus, given = total - limit - (amount - 1), [1] * (amount - 1)
    while surplus > 0:
        free = [i for i in range(amount - 1) if given[i] < limit]
        mass, budget = sum([weights[i] for i in free]), surplus
        for i in free:
            extra = min(limit - given[i], max(1, budget * weights[i] // mass), surplus)
            given[i] = given[i] + extra
            surplus = surplus - extra
    return np.array([limit] + given)


def ragged(rng, amount, total, most, skew):
    if amount == 2:
        one = jax.random.randint(rng, (), max(1, total - most), min(most, total - 1) + 1)
        return jnp.stack([one, total - one])
    lengths = jnp.asarray(split_up(amount, total, most, skew), jnp.int32)
    pairs = (amount - 1) // 2
    giver, taker = lengths[1:1 + 2 * pairs:2], lengths[2:2 + 2 * pairs:2]
    slack = jnp.minimum(giver - 1, most - taker)
    shifted = jax.random.randint(jax.random.fold_in(rng, 1), (pairs,), 0, 1 << 20) % (slack + 1)
    lengths = lengths.at[1:1 + 2 * pairs:2].set(giver - shifted).at[2:2 + 2 * pairs:2].set(taker + shifted)
    return lengths[jax.random.permutation(jax.random.fold_in(rng, 2), amount)]


def scatter_about(key, dims, width, most, split=(), held_as=jnp.bfloat16):
    values = width * jax.random.normal(key, dims, jnp.float32)
    if split:
        values = values * level_of(key, dims, split, -0.22, 0.18)
    return jnp.clip(values, -most, most).astype(held_as)


def setup_inputs(seed: int = 0, part: int = 0) -> dict:
    key_of = jax.random.split(jax.random.key(seed), 9)
    part_splits = jax.random.split(jax.random.fold_in(key_of[8], part), 9)
    return {
        "tokens": scatter_about(part_splits[0], (TOKENS, D), 1.0, 6.0, ((0, 16),)),
        "key_down": scatter_about(key_of[1], (D, R), D ** -0.5, 0.0625, ((0, 16),)),
        "value_down": scatter_about(key_of[2], (D, R), D ** -0.5, 0.0625, ((0, 16),)),
        "key_up": scatter_about(key_of[3], (R, KVH * DH), R ** -0.5, 0.25),
        "value_up": scatter_about(key_of[4], (R, KVH * DH), R ** -0.5, 0.25),
        "prompt_lens": ragged(part_splits[5], REQS, TOKENS, TOKENS // 2, 2).astype(jnp.int32),
        "queries": draw_queries(jax.random.fold_in(jax.random.fold_in(key_of[8], part), 71), part),
        "new_latent": scatter_about(part_splits[7], (STEPS, REQS, 2 * R), 1.0, 6.0),
    }


def reference(tokens, key_down, value_down, key_up, value_up, prompt_lens, queries, new_latent):
    key_latent = jnp.dot(tokens, key_down, preferred_element_type=jnp.float32).astype(jnp.bfloat16)
    value_latent = jnp.dot(tokens, value_down, preferred_element_type=jnp.float32).astype(jnp.bfloat16)
    keys = jnp.dot(key_latent, key_up, preferred_element_type=jnp.float32).astype(jnp.bfloat16).reshape(TOKENS, KVH, DH)
    values = jnp.dot(value_latent, value_up, preferred_element_type=jnp.float32).astype(jnp.bfloat16).reshape(TOKENS, KVH, DH)
    flat_new = new_latent.reshape(STEPS * REQS, 2 * R)
    new_keys = jnp.dot(flat_new[:, :R], key_up, preferred_element_type=jnp.float32).astype(jnp.bfloat16).reshape(STEPS, REQS, KVH, DH)
    new_values = jnp.dot(flat_new[:, R:], value_up, preferred_element_type=jnp.float32).astype(jnp.bfloat16).reshape(STEPS, REQS, KVH, DH)
    offsets = (jnp.cumsum(prompt_lens) - prompt_lens).astype(jnp.int32)
    window = TOKENS // 2
    group = QH // KVH
    scale = 1.0 / (DH ** 0.5)
    causal = jnp.arange(STEPS)[:, None] >= jnp.arange(STEPS)[None, :]

    def one_request(index):
        offset = offsets[index]
        length = prompt_lens[index]
        start = jnp.minimum(offset, TOKENS - window).astype(jnp.int32)
        key_win = lax.dynamic_slice_in_dim(keys, start, window, 0).astype(jnp.float32)
        value_win = lax.dynamic_slice_in_dim(values, start, window, 0).astype(jnp.float32)
        position = start + jnp.arange(window, dtype=jnp.int32)
        member = (position >= offset) & (position < offset + length)
        query = lax.dynamic_index_in_dim(queries, index, 1, keepdims=False).astype(jnp.float32).reshape(STEPS, KVH, group, DH)
        own_keys = lax.dynamic_index_in_dim(new_keys, index, 1, keepdims=False).astype(jnp.float32)
        own_values = lax.dynamic_index_in_dim(new_values, index, 1, keepdims=False).astype(jnp.float32)
        first = jnp.einsum("sgjd,tgd->sgjt", query, key_win) * scale
        first = jnp.where(member[None, None, None, :], first, -1e30)
        second = jnp.einsum("sgjd,ugd->sgju", query, own_keys) * scale
        second = jnp.where(causal[:, None, None, :], second, -1e30)
        top = jnp.maximum(jnp.max(first, -1), jnp.max(second, -1))
        weight_one = jnp.where(member[None, None, None, :], jnp.exp(first - top[..., None]), 0.0)
        weight_two = jnp.where(causal[:, None, None, :], jnp.exp(second - top[..., None]), 0.0)
        total = jnp.sum(weight_one, -1) + jnp.sum(weight_two, -1)
        rounded_one = lax.optimization_barrier(weight_one.astype(jnp.bfloat16)).astype(jnp.float32)
        rounded_two = lax.optimization_barrier(weight_two.astype(jnp.bfloat16)).astype(jnp.float32)
        summed = jnp.einsum("sgjt,tgd->sgjd", rounded_one, value_win) + jnp.einsum("sgju,ugd->sgjd", rounded_two, own_values)
        return (summed / total[..., None]).reshape(STEPS, QH * DH)

    result = lax.map(one_request, jnp.arange(REQS, dtype=jnp.int32))
    return jnp.transpose(result, (1, 0, 2)).astype(jnp.bfloat16)
```

```python
import jax
import jax.numpy as jnp
from jax import lax
from jax.sharding import Mesh, PartitionSpec as P

QH = 64
KVH = 8
DH = 128
BF = jnp.bfloat16
F32 = jnp.float32


def mm(a, b):
    return jnp.dot(a, b, preferred_element_type=F32)


def on_device(tokens, key_down, value_down, key_up, value_up, prompt_lens, queries, new_latent):
    chips = lax.axis_size("chip")
    cores = lax.axis_size("core")
    n_ctx = chips * cores
    core = lax.axis_index("core")
    device = lax.axis_index("chip") * cores + core
    tok_rows, width = tokens.shape
    shard, lat_width = key_down.shape
    group = QH // KVH
    scale = 1.0 / DH**0.5
    steps_count, req_count = (queries.shape[0], queries.shape[1])
    pairs = steps_count * req_count
    rows = pairs * QH
    share = rows // n_ctx

    swap = [(0, 1), (1, 0)]
    key_mine = lax.all_gather(key_down, "chip", axis=0, tiled=True)
    value_mine = lax.all_gather(value_down, "chip", axis=0, tiled=True)
    key_other = lax.ppermute(key_mine, "core", swap)
    value_other = lax.ppermute(value_mine, "core", swap)
    by_core = tokens.reshape(tok_rows, chips, cores, shard)
    tokens_mine = lax.dynamic_index_in_dim(by_core, core, 2, keepdims=False).reshape(tok_rows, -1)
    tokens_other = lax.dynamic_index_in_dim(by_core, 1 - core, 2, keepdims=False).reshape(tok_rows, -1)

    query = queries.reshape(steps_count, req_count, KVH, group, DH)
    flat_new = new_latent.reshape(pairs, 2 * lat_width)
    new_keys = mm(flat_new[:, :lat_width], key_up).astype(BF).reshape(steps_count, req_count, KVH, DH)
    new_values = mm(flat_new[:, lat_width:], value_up).astype(BF).reshape(steps_count, req_count, KVH, DH)
    causal = (jnp.arange(steps_count)[:, None] >= jnp.arange(steps_count)[None, :])[:, None, None, None, :]
    fresh = jnp.einsum("srgjd,urgd->srgju", query, new_keys, preferred_element_type=F32) * scale
    fresh = jnp.where(causal, fresh, -1e30)
    fresh_top = jnp.max(fresh, -1)
    fresh_weights = jnp.where(causal, jnp.exp(fresh - fresh_top[..., None]), 0.0)
    fresh_total = jnp.sum(fresh_weights, -1)
    fresh_summed = jnp.einsum("srgju,urgd->srgjd", fresh_weights.astype(BF), new_values, preferred_element_type=F32)

    def my_share(x):
        return lax.dynamic_slice_in_dim(x, device * share, share, 0)

    fresh_top = my_share(fresh_top.reshape(rows))
    fresh_total = my_share(fresh_total.reshape(rows))
    fresh_summed = my_share(fresh_summed.reshape(rows, DH))

    key_latent = (mm(tokens_mine, key_mine) + mm(tokens_other, key_other)).astype(BF)
    keys = mm(key_latent, key_up).astype(BF)
    position = device * tok_rows + jnp.arange(tok_rows, dtype=jnp.int32)
    offsets = jnp.cumsum(prompt_lens) - prompt_lens
    member = (position[None, :] >= offsets[:, None]) & (position[None, :] < (offsets + prompt_lens)[:, None])
    key_heads = keys.reshape(-1, KVH, DH)
    scores = jnp.einsum("srgjd,tgd->srgjt", query, key_heads, preferred_element_type=F32) * scale
    visible = member[None, :, None, None, :]
    scores = jnp.where(visible, scores, -1e30)
    top = jnp.max(scores, -1)
    weights = jnp.where(visible, jnp.exp(scores - top[..., None]), 0.0)
    total = jnp.sum(weights, -1)

    value_latent = (mm(tokens_mine, value_mine) + mm(tokens_other, value_other)).astype(BF)
    values = mm(value_latent, value_up).astype(BF)
    value_heads = values.reshape(-1, KVH, DH)
    summed = jnp.einsum("srgjt,tgd->srgjd", weights.astype(BF), value_heads, preferred_element_type=F32)

    stats = jnp.stack([top.reshape(n_ctx, share), total.reshape(n_ctx, share)], 1).reshape(n_ctx, 1, 2 * share)
    stats = jnp.pad(stats, ((0, 0), (0, 7), (0, DH - 2 * share)))
    sending = jnp.concatenate([summed.reshape(n_ctx, share, DH), stats], 1)
    arrived = lax.all_to_all(sending, ("chip", "core"), split_axis=0, concat_axis=0, tiled=True)
    tops = arrived[:, share, :share]
    totals = arrived[:, share, share : 2 * share]
    overall = jnp.maximum(jnp.max(tops, 0), fresh_top)
    carried = jnp.exp(tops - overall[None])
    fresh_carried = jnp.exp(fresh_top - overall)
    total = jnp.sum(totals * carried, 0) + fresh_total * fresh_carried
    summed = jnp.sum(arrived[:, :share] * carried[..., None], 0) + fresh_summed * fresh_carried[:, None]
    result = (summed / total[:, None]).astype(BF)
    result = lax.all_gather(result, ("chip", "core"), axis=0, tiled=True)
    return result.reshape(steps_count, req_count, QH * DH)


def solution(mesh):
    cores = 2
    groups, n_ctx = mesh.shape["groups"], mesh.shape["ctx"]
    split = Mesh(mesh.devices.reshape(groups, n_ctx // cores, cores), ("groups", "chip", "core"))
    ctx = ("chip", "core")
    return jax.shard_map(
        on_device,
        mesh=split,
        in_specs=(
            P(("groups",) + ctx, None),
            P(ctx, None),
            P(ctx, None),
            P(),
            P(),
            P("groups"),
            P(None, "groups", None),
            P(None, "groups", None),
        ),
        out_specs=P(None, "groups", None),
        check_vma=False,
    )
```

```python
import jax
import jax.numpy as jnp
from jax import lax
from jax.sharding import Mesh, PartitionSpec as P

QH = 64
KVH = 8
DH = 128
CORES = 2
BF = jnp.bfloat16
F32 = jnp.float32
SWAP = [(0, 1), (1, 0)]


def mm(a, b):
    return jnp.dot(a, b, preferred_element_type=F32)


def project(tokens, theirs, block):
    chips = lax.axis_size("chip")
    chip = lax.axis_index("chip")
    rows = block.shape[0]
    if chips > 8:
        full = lax.all_gather(block, "chip", axis=0, tiled=True)
        return mm(tokens, full), mm(theirs, full)
    cycle = list(range(0, chips, 2)) + list(range(chips - 1, 0, -2))
    last = chips - 1
    place = jnp.where(chip & 1 == 0, chip >> 1, last - (chip >> 1))
    chains = 2
    piece = rows // (2 * chains)
    right = [(cycle[i], cycle[(i + 1) % chips]) for i in range(chips)]
    left = [(b, a) for a, b in right]

    def block_of(spot):
        spot = jnp.where(spot < 0, spot + chips, jnp.where(spot > last, spot - chips, spot))
        return jnp.where(spot < chips // 2, 2 * spot, 2 * (last - spot) + 1) * rows

    def term(x, start, part):
        return mm(lax.dynamic_slice_in_dim(x, start, part.shape[0], 1, allow_negative_indices=False), part)

    held = [block[k * piece : (k + 1) * piece] for k in range(2 * chains)]
    todo = [(chip * rows, block)]
    mine_sum = theirs_sum = 0.0
    for step in range(1, chips):
        for k in range(2 * chains):
            held[k] = lax.ppermute(held[k], "chip", right if k < chains else left)
        if step == min(3, last):
            held, theirs = lax.optimization_barrier((held, theirs))
        for k in range(2 * chains):
            todo.append((block_of(place - step if k < chains else place + step) + k * piece, held[k]))
        if step >= min(3, last):
            for start, part in todo:
                mine_sum = mine_sum + term(tokens, start, part)
                theirs_sum = theirs_sum + term(theirs, start, part)
            todo = []
    return mine_sum, theirs_sum


def on_device(tokens, key_down, value_down, key_up, value_up, prompt_lens, queries, new_latent):
    chips = lax.axis_size("chip")
    chip = lax.axis_index("chip")
    core = lax.axis_index("core")
    first = core == 0
    tok_rows = tokens.shape[0]
    lat_width = key_down.shape[1]
    group = QH // KVH
    heads = KVH // CORES
    scale = 1.0 / DH**0.5
    steps_count, req_count = (queries.shape[0], queries.shape[1])
    pairs = steps_count * req_count
    rows = pairs * heads * group
    share = rows // chips

    theirs = lax.ppermute(tokens, "core", SWAP)
    own_part = jnp.where(first, key_down, value_down)
    got_part = lax.ppermute(jnp.where(first, value_down, key_down), "core", SWAP)
    block = jnp.concatenate([jnp.where(first, own_part, got_part), jnp.where(first, got_part, own_part)], 0)
    mine_sum, theirs_sum = project(tokens, theirs, block)

    query = lax.dynamic_index_in_dim(
        queries.reshape(steps_count, req_count, CORES, heads * group * DH), core, 2, keepdims=False
    ).reshape(steps_count, req_count, heads, group, DH)
    key_up = lax.dynamic_slice_in_dim(key_up, core * heads * DH, heads * DH, 1)
    value_up = lax.dynamic_slice_in_dim(value_up, core * heads * DH, heads * DH, 1)
    flat_new = new_latent.reshape(pairs, 2 * lat_width)
    new_keys = mm(flat_new[:, :lat_width], key_up).astype(BF).reshape(steps_count, req_count, heads, DH)
    new_values = mm(flat_new[:, lat_width:], value_up).astype(BF).reshape(steps_count, req_count, heads, DH)
    causal = (jnp.arange(steps_count)[:, None] >= jnp.arange(steps_count)[None, :])[:, None, None, None, :]
    fresh = jnp.einsum("srgjd,urgd->srgju", query, new_keys, preferred_element_type=F32) * scale
    fresh = jnp.where(causal, fresh, -1e30)
    fresh_top = jnp.max(fresh, -1)
    fresh_weights = jnp.where(causal, jnp.exp(fresh - fresh_top[..., None]), 0.0)
    fresh_total = jnp.sum(fresh_weights, -1)
    fresh_summed = jnp.einsum("srgju,urgd->srgjd", fresh_weights.astype(BF), new_values, preferred_element_type=F32)

    def my_share(x):
        return lax.dynamic_slice_in_dim(x, chip * share, share, 0)

    fresh_top = my_share(fresh_top.reshape(rows))
    fresh_total = my_share(fresh_total.reshape(rows))
    fresh_summed = my_share(fresh_summed.reshape(rows, DH))

    mine = mine_sum.astype(BF)
    other = theirs_sum.astype(BF)
    have = jnp.concatenate([jnp.where(first, mine, other), jnp.where(first, other, mine)], 0)
    got = lax.ppermute(have, "core", SWAP)
    key_latent = jnp.where(first, have, got)
    value_latent = jnp.where(first, got, have)
    keys = mm(key_latent, key_up).astype(BF)
    values = mm(value_latent, value_up).astype(BF)
    position = chip * CORES * tok_rows + jnp.arange(CORES * tok_rows, dtype=jnp.int32)
    offsets = jnp.cumsum(prompt_lens) - prompt_lens
    member = (position[None, :] >= offsets[:, None]) & (position[None, :] < (offsets + prompt_lens)[:, None])
    key_heads = keys.reshape(-1, heads, DH)
    value_heads = values.reshape(-1, heads, DH)
    scores = jnp.einsum("srgjd,tgd->srgjt", query, key_heads, preferred_element_type=F32) * scale
    visible = member[None, :, None, None, :]
    scores = jnp.where(visible, scores, -1e30)
    top = jnp.max(scores, -1)
    weights = jnp.where(visible, jnp.exp(scores - top[..., None]), 0.0)
    total = jnp.sum(weights, -1)
    summed = jnp.einsum("srgjt,tgd->srgjd", weights.astype(BF), value_heads, preferred_element_type=F32)

    stats = jnp.stack([top.reshape(chips, share), total.reshape(chips, share)], 1).reshape(chips, 1, 2 * share)
    stats = jnp.pad(stats, ((0, 0), (0, 7), (0, DH - 2 * share)))
    sending = jnp.concatenate([summed.reshape(chips, share, DH), stats], 1)
    arrived = lax.all_to_all(sending, "chip", split_axis=0, concat_axis=0, tiled=True)
    tops = arrived[:, share, :share]
    totals = arrived[:, share, share : 2 * share]
    overall = jnp.maximum(jnp.max(tops, 0), fresh_top)
    carried = jnp.exp(tops - overall[None])
    fresh_carried = jnp.exp(fresh_top - overall)
    total = jnp.sum(totals * carried, 0) + fresh_total * fresh_carried
    summed = jnp.sum(arrived[:, :share] * carried[..., None], 0) + fresh_summed * fresh_carried[:, None]
    result = (summed / total[:, None]).astype(BF)

    if chips & (chips - 1) == 0:
        whole = result.reshape(1, share, DH)
        span = 1
        while span < chips:
            away = lax.ppermute(whole, "chip", [(c, c ^ span) for c in range(chips)])
            upper = (chip & span) != 0
            whole = jnp.concatenate([jnp.where(upper, away, whole), jnp.where(upper, whole, away)], 0)
            span *= 2
    else:
        whole = lax.all_gather(result, "chip", axis=0, tiled=True)
    whole = whole.reshape(pairs, 1, rows // pairs * DH)
    away = lax.ppermute(whole, "core", SWAP)
    whole = jnp.concatenate([jnp.where(first, whole, away), jnp.where(first, away, whole)], 1)
    return whole.reshape(steps_count, req_count, QH * DH)


def solution(mesh):
    groups, n_ctx = mesh.shape["groups"], mesh.shape["ctx"]
    split = Mesh(mesh.devices.reshape(groups, n_ctx // CORES, CORES), ("groups", "chip", "core"))
    ctx = ("chip", "core")
    return jax.shard_map(
        on_device,
        mesh=split,
        in_specs=(
            P(("groups",) + ctx, None),
            P(ctx, None),
            P(ctx, None),
            P(),
            P(),
            P("groups"),
            P(None, "groups", None),
            P(None, "groups", None),
        ),
        out_specs=P(None, "groups", None),
        check_vma=False,
    )
```

```python
import jax
import jax.numpy as jnp
from jax import lax
from jax.experimental import pallas as pl
from jax.experimental.pallas import tpu as pltpu
from jax.sharding import Mesh, PartitionSpec as P

QH = 64
KVH = 8
DH = 128
CORES = 2
BF = jnp.bfloat16
F32 = jnp.float32
SWAP = [(0, 1), (1, 0)]


def mm(a, b):
    return jnp.dot(a, b, preferred_element_type=F32)


def add_pieces(tokens, theirs, pieces, total, core=None):
    tok_rows = tokens.shape[0]
    depth, width = pieces[0][1].shape
    count = len(pieces)
    last = core is not None
    places = jnp.stack([start for start, _ in pieces] + ([core * tok_rows, (1 - core) * tok_rows] if last else []))

    def kernel(places_ref, mine_ref, theirs_ref, *refs):
        parts = refs[:count]
        total_ref, out_ref, mark_ref, columns, sems = refs[count:] if total is not None else (None,) + refs[count:]
        copies = []
        for k in range(count):
            for j, source in enumerate((mine_ref, theirs_ref)):
                start = pl.multiple_of(places_ref[k], 128)
                copy = pltpu.make_async_copy(source.at[:, pl.ds(start, depth)], columns.at[j, k], sems.at[j, k])
                copy.start()
                copies.append(copy)
        sums = [None, None]
        for k in range(count):
            for j in range(2):
                copies[2 * k + j].wait()
                term = mm(columns[j, k], parts[k][...])
                rows = pl.ds(j * tok_rows, tok_rows)
                if k == 0:
                    before = None if total is None else total_ref[rows, :]
                else:
                    before = sums[j]
                sums[j] = term if before is None else before + term
        for j in range(2):
            if last:
                out_ref[pl.ds(pl.multiple_of(places_ref[count + j], tok_rows), tok_rows), :] = sums[j].astype(BF)
            else:
                out_ref[pl.ds(j * tok_rows, tok_rows), :] = sums[j]
        mark_ref[...] = jnp.zeros_like(mark_ref)

    in_vmem = pl.BlockSpec(memory_space=pltpu.VMEM)
    in_hbm = pl.BlockSpec(memory_space=pltpu.HBM)
    sums = [] if total is None else [total]
    return pl.pallas_call(
        kernel,
        out_shape=(
            jax.ShapeDtypeStruct((2 * tok_rows, width), BF if last else F32),
            jax.ShapeDtypeStruct((8, 128), F32),
        ),
        in_specs=[pl.BlockSpec(memory_space=pltpu.SMEM), in_hbm, in_hbm] + [in_vmem] * (count + len(sums)),
        out_specs=(in_vmem, in_vmem),
        scratch_shapes=[
            pltpu.VMEM((2, count, tok_rows, depth), BF),
            pltpu.SemaphoreType.DMA((2, count)),
        ],
        compiler_params=pltpu.CompilerParams(vmem_limit_bytes=48 * 2**20),
        cost_estimate=pl.CostEstimate(
            flops=4 * tok_rows * depth * width * count,
            bytes_accessed=4 * tok_rows * depth * count,
            transcendentals=0,
        ),
    )(places, tokens, theirs, *[part for _, part in pieces], *sums)


def project(tokens, key_down, value_down):
    chips = lax.axis_size("chip")
    chip = lax.axis_index("chip")
    core = lax.axis_index("core")
    first = core == 0
    shard = key_down.shape[0]
    rows = CORES * shard
    own = jnp.where(first, key_down, value_down)
    got = lax.ppermute(jnp.where(first, value_down, key_down), "core", SWAP)
    if chips > 8:
        theirs = lax.ppermute(tokens, "core", SWAP)
        block = jnp.concatenate([jnp.where(first, own, got), jnp.where(first, got, own)], 0)
        full = lax.all_gather(block, "chip", axis=0, tiled=True)
        mine, other = mm(tokens, full).astype(BF), mm(theirs, full).astype(BF)
        return jnp.concatenate([jnp.where(first, mine, other), jnp.where(first, other, mine)], 0)
    cycle = list(range(0, chips, 2)) + list(range(chips - 1, 0, -2))
    last = chips - 1
    place = jnp.where(chip & 1 == 0, chip >> 1, last - (chip >> 1))
    chains = 2
    piece = shard // chains
    right = [(cycle[i], cycle[(i + 1) % chips]) for i in range(chips)]
    left = [(b, a) for a, b in right]
    ways = [right] * chains + [left] * chains

    def start_of(k, step):
        spot = place - step if k < chains else place + step
        spot = jnp.where(spot < 0, spot + chips, jnp.where(spot > last, spot - chips, spot))
        source = jnp.where(spot < chips // 2, 2 * spot, 2 * (last - spot) + 1)
        return source * rows + (core if k < chains else 1 - core) * shard + k % chains * piece

    held = [own[k * piece : (k + 1) * piece] for k in range(chains)]
    got, tokens_later = lax.optimization_barrier((got, tokens))
    held += [got[k * piece : (k + 1) * piece] for k in range(chains)]
    theirs = lax.ppermute(tokens_later, "core", SWAP)
    steps = [[(start_of(k, 0), held[k]) for k in range(2 * chains)]]
    total = None
    mark = None
    for step in range(1, chips):
        for k in range(2 * chains):
            if mark is not None:
                held[k], _ = lax.optimization_barrier((held[k], mark))
            held[k] = lax.ppermute(held[k], "chip", ways[k])
        steps.append([(start_of(k, step), held[k]) for k in range(2 * chains)])
        while steps and (step >= 3 and len(steps) > 1):
            total, mark = add_pieces(tokens, theirs, steps.pop(0), total)
    return add_pieces(tokens, theirs, steps.pop(0), total, core)[0]


def on_device(tokens, key_down, value_down, key_up, value_up, prompt_lens, queries, new_latent):
    chips = lax.axis_size("chip")
    chip = lax.axis_index("chip")
    core = lax.axis_index("core")
    first = core == 0
    tok_rows = tokens.shape[0]
    lat_width = key_down.shape[1]
    group = QH // KVH
    heads = KVH // CORES
    scale = 1.0 / DH**0.5
    steps_count, req_count = (queries.shape[0], queries.shape[1])
    pairs = steps_count * req_count
    rows = pairs * heads * group
    share = rows // chips

    have = project(tokens, key_down, value_down)

    query = lax.dynamic_index_in_dim(
        queries.reshape(steps_count, req_count, CORES, heads * group * DH), core, 2, keepdims=False
    ).reshape(steps_count, req_count, heads, group, DH)
    key_up = lax.dynamic_slice_in_dim(key_up, core * heads * DH, heads * DH, 1)
    value_up = lax.dynamic_slice_in_dim(value_up, core * heads * DH, heads * DH, 1)
    flat_new = new_latent.reshape(pairs, 2 * lat_width)
    new_keys = mm(flat_new[:, :lat_width], key_up).astype(BF).reshape(steps_count, req_count, heads, DH)
    new_values = mm(flat_new[:, lat_width:], value_up).astype(BF).reshape(steps_count, req_count, heads, DH)
    causal = (jnp.arange(steps_count)[:, None] >= jnp.arange(steps_count)[None, :])[:, None, None, None, :]
    fresh = jnp.einsum("srgjd,urgd->srgju", query, new_keys, preferred_element_type=F32) * scale
    fresh = jnp.where(causal, fresh, -1e30)
    fresh_top = jnp.max(fresh, -1)
    fresh_weights = jnp.where(causal, jnp.exp(fresh - fresh_top[..., None]), 0.0)
    fresh_total = jnp.sum(fresh_weights, -1)
    fresh_summed = jnp.einsum("srgju,urgd->srgjd", fresh_weights.astype(BF), new_values, preferred_element_type=F32)

    def my_share(x):
        return lax.dynamic_slice_in_dim(x, chip * share, share, 0)

    fresh_top = my_share(fresh_top.reshape(rows))
    fresh_total = my_share(fresh_total.reshape(rows))
    fresh_summed = my_share(fresh_summed.reshape(rows, DH))

    got = lax.ppermute(have, "core", SWAP)
    key_latent = jnp.where(first, have, got)
    value_latent = jnp.where(first, got, have)
    keys = mm(key_latent, key_up).astype(BF)
    values = mm(value_latent, value_up).astype(BF)
    position = chip * CORES * tok_rows + jnp.arange(CORES * tok_rows, dtype=jnp.int32)
    offsets = jnp.cumsum(prompt_lens) - prompt_lens
    member = (position[None, :] >= offsets[:, None]) & (position[None, :] < (offsets + prompt_lens)[:, None])
    key_heads = keys.reshape(-1, heads, DH)
    value_heads = values.reshape(-1, heads, DH)
    scores = jnp.einsum("srgjd,tgd->srgjt", query, key_heads, preferred_element_type=F32) * scale
    visible = member[None, :, None, None, :]
    scores = jnp.where(visible, scores, -1e30)
    top = jnp.max(scores, -1)
    weights = jnp.where(visible, jnp.exp(scores - top[..., None]), 0.0)
    total = jnp.sum(weights, -1)
    summed = jnp.einsum("srgjt,tgd->srgjd", weights.astype(BF), value_heads, preferred_element_type=F32)

    stats = jnp.stack([top.reshape(chips, share), total.reshape(chips, share)], 1).reshape(chips, 1, 2 * share)
    stats = jnp.pad(stats, ((0, 0), (0, 7), (0, DH - 2 * share)))
    sending = jnp.concatenate([summed.reshape(chips, share, DH), stats], 1)
    arrived = lax.all_to_all(sending, "chip", split_axis=0, concat_axis=0, tiled=True)
    tops = arrived[:, share, :share]
    totals = arrived[:, share, share : 2 * share]
    overall = jnp.maximum(jnp.max(tops, 0), fresh_top)
    carried = jnp.exp(tops - overall[None])
    fresh_carried = jnp.exp(fresh_top - overall)
    total = jnp.sum(totals * carried, 0) + fresh_total * fresh_carried
    summed = jnp.sum(arrived[:, :share] * carried[..., None], 0) + fresh_summed * fresh_carried[:, None]
    result = (summed / total[:, None]).astype(BF)

    if chips & (chips - 1) == 0:
        whole = result.reshape(1, share, DH)
        span = 1
        while span < chips:
            away = lax.ppermute(whole, "chip", [(c, c ^ span) for c in range(chips)])
            upper = (chip & span) != 0
            whole = jnp.concatenate([jnp.where(upper, away, whole), jnp.where(upper, whole, away)], 0)
            span *= 2
    else:
        whole = lax.all_gather(result, "chip", axis=0, tiled=True)
    whole = whole.reshape(pairs, 1, rows // pairs * DH)
    away = lax.ppermute(whole, "core", SWAP)
    whole = jnp.concatenate([jnp.where(first, whole, away), jnp.where(first, away, whole)], 1)
    return whole.reshape(steps_count, req_count, QH * DH)


def solution(mesh):
    groups, n_ctx = mesh.shape["groups"], mesh.shape["ctx"]
    split = Mesh(mesh.devices.reshape(groups, n_ctx // CORES, CORES), ("groups", "chip", "core"))
    ctx = ("chip", "core")
    return jax.shard_map(
        on_device,
        mesh=split,
        in_specs=(
            P(("groups",) + ctx, None),
            P(ctx, None),
            P(ctx, None),
            P(),
            P(),
            P("groups"),
            P(None, "groups", None),
            P(None, "groups", None),
        ),
        out_specs=P(None, "groups", None),
        check_vma=False,
    )
```

```python
import jax
import jax.numpy as jnp
from jax import lax
from jax.experimental import pallas as pl
from jax.experimental.pallas import tpu as pltpu
from jax.sharding import Mesh, PartitionSpec as P

QH = 64
KVH = 8
DH = 128
CORES = 2
BF = jnp.bfloat16
F32 = jnp.float32
SWAP = [(0, 1), (1, 0)]


def mm(a, b):
    return jnp.dot(a, b, preferred_element_type=F32)


def add_pieces(tokens, theirs, groups, total, core=None):
    tok_rows = tokens.shape[0]
    width = groups[0][1][0].shape[1]
    depths = [[part.shape[0] for part in parts] for _, parts in groups]
    span = sum(depths[0])
    deep = span * len(groups)
    flat = [part for _, parts in groups for part in parts]
    count = len(flat)
    last = core is not None
    places = jnp.stack([start for start, _ in groups] + ([core * tok_rows, (1 - core) * tok_rows] if last else []))

    def kernel(places_ref, mine_ref, theirs_ref, *refs):
        parts = refs[:count]
        total_ref, out_ref, mark_ref, columns, weights, sems = (
            refs[count:] if total is not None else (None,) + refs[count:]
        )
        copies = []
        for j, source in enumerate((mine_ref, theirs_ref)):
            for g in range(len(groups)):
                start = pl.multiple_of(places_ref[g], 128)
                copy = pltpu.make_async_copy(
                    source.at[:, pl.ds(start, span)], columns.at[j, :, pl.ds(g * span, span)], sems.at[j, g]
                )
                copy.start()
                copies.append(copy)
        at = 0
        for part in parts:
            weights[at : at + part.shape[0], :] = part[...]
            at += part.shape[0]
        mark_ref[...] = jnp.zeros_like(mark_ref)
        for j in range(2):
            for g in range(len(groups)):
                copies[j * len(groups) + g].wait()
            rows = pl.ds(j * tok_rows, tok_rows)
            term = mm(columns[j], weights[...])
            if total is not None:
                term = total_ref[rows, :] + term
            if last:
                rows = pl.ds(pl.multiple_of(places_ref[len(groups) + j], tok_rows), tok_rows)
            out_ref[rows, :] = term.astype(out_ref.dtype)

    in_vmem = pl.BlockSpec(memory_space=pltpu.VMEM)
    in_any = pl.BlockSpec(memory_space=pl.ANY)
    sums = [] if total is None else [total]
    return pl.pallas_call(
        kernel,
        out_shape=(
            jax.ShapeDtypeStruct((2 * tok_rows, width), BF if last else F32),
            jax.ShapeDtypeStruct((8, 128), F32),
        ),
        in_specs=[pl.BlockSpec(memory_space=pltpu.SMEM), in_any, in_any] + [in_vmem] * (count + len(sums)),
        out_specs=(in_vmem, in_vmem),
        scratch_shapes=[
            pltpu.VMEM((2, tok_rows, deep), BF),
            pltpu.VMEM((deep, width), BF),
            pltpu.SemaphoreType.DMA((2, len(groups))),
        ],
        input_output_aliases={} if total is None or last else {3 + count: 0},
        compiler_params=pltpu.CompilerParams(vmem_limit_bytes=48 * 2**20),
        cost_estimate=pl.CostEstimate(
            flops=4 * tok_rows * deep * width, bytes_accessed=4 * tok_rows * deep, transcendentals=0
        ),
    )(places, tokens, theirs, *flat, *sums)


def project(tokens, key_down, value_down):
    chips = lax.axis_size("chip")
    chip = lax.axis_index("chip")
    core = lax.axis_index("core")
    first = core == 0
    shard = key_down.shape[0]
    rows = CORES * shard
    own = jnp.where(first, key_down, value_down)
    got = lax.ppermute(jnp.where(first, value_down, key_down), "core", SWAP)
    if chips > 8:
        theirs = lax.ppermute(tokens, "core", SWAP)
        block = jnp.concatenate([jnp.where(first, own, got), jnp.where(first, got, own)], 0)
        full = lax.all_gather(block, "chip", axis=0, tiled=True)
        mine, other = mm(tokens, full).astype(BF), mm(theirs, full).astype(BF)
        return jnp.concatenate([jnp.where(first, mine, other), jnp.where(first, other, mine)], 0)
    cycle = list(range(0, chips, 2)) + list(range(chips - 1, 0, -2))
    last = chips - 1
    place = jnp.where(chip & 1 == 0, chip >> 1, last - (chip >> 1))
    chains = 2
    piece = shard // chains
    right = [(cycle[i], cycle[(i + 1) % chips]) for i in range(chips)]
    left = [(b, a) for a, b in right]
    ways = [right] * chains + [left] * chains

    def start_of(way, step):
        spot = place - step if way == 0 else place + step
        spot = jnp.where(spot < 0, spot + chips, jnp.where(spot > last, spot - chips, spot))
        source = jnp.where(spot < chips // 2, 2 * spot, 2 * (last - spot) + 1)
        return source * rows + (core if way == 0 else 1 - core) * shard

    held = [own[k * piece : (k + 1) * piece] for k in range(chains)]
    got, tokens_later = lax.optimization_barrier((got, tokens))
    held += [got[k * piece : (k + 1) * piece] for k in range(chains)]
    theirs = lax.ppermute(tokens_later, "core", SWAP)
    todo = [(start_of(0, 0), [own]), (start_of(1, 0), [got])]
    total = None
    mark = None
    for step in range(1, chips):
        ready = todo
        for k in range(2 * chains):
            if mark is not None:
                held[k], _ = lax.optimization_barrier((held[k], mark))
            held[k] = lax.ppermute(held[k], "chip", ways[k])
        arriving = [(start_of(w, step), held[w * chains : (w + 1) * chains]) for w in range(2)]
        if step == 1:
            todo = todo + arriving
        else:
            total, mark = add_pieces(tokens, theirs, ready, total)
            todo = arriving
    return add_pieces(tokens, theirs, todo, total, core)[0]


def on_device(tokens, key_down, value_down, key_up, value_up, prompt_lens, queries, new_latent):
    chips = lax.axis_size("chip")
    chip = lax.axis_index("chip")
    core = lax.axis_index("core")
    first = core == 0
    tok_rows = tokens.shape[0]
    lat_width = key_down.shape[1]
    group = QH // KVH
    heads = KVH // CORES
    scale = 1.0 / DH**0.5
    steps_count, req_count = (queries.shape[0], queries.shape[1])
    pairs = steps_count * req_count
    rows = pairs * heads * group
    share = rows // chips

    have = project(tokens, key_down, value_down)

    query = lax.dynamic_index_in_dim(
        queries.reshape(steps_count, req_count, CORES, heads * group * DH), core, 2, keepdims=False
    ).reshape(steps_count, req_count, heads, group, DH)
    key_up = lax.dynamic_slice_in_dim(key_up, core * heads * DH, heads * DH, 1)
    value_up = lax.dynamic_slice_in_dim(value_up, core * heads * DH, heads * DH, 1)
    flat_new = new_latent.reshape(pairs, 2 * lat_width)
    new_keys = mm(flat_new[:, :lat_width], key_up).astype(BF).reshape(steps_count, req_count, heads, DH)
    new_values = mm(flat_new[:, lat_width:], value_up).astype(BF).reshape(steps_count, req_count, heads, DH)
    causal = (jnp.arange(steps_count)[:, None] >= jnp.arange(steps_count)[None, :])[:, None, None, None, :]
    fresh = jnp.einsum("srgjd,urgd->srgju", query, new_keys, preferred_element_type=F32) * scale
    fresh = jnp.where(causal, fresh, -1e30)
    fresh_top = jnp.max(fresh, -1)
    fresh_weights = jnp.where(causal, jnp.exp(fresh - fresh_top[..., None]), 0.0)
    fresh_total = jnp.sum(fresh_weights, -1)
    fresh_summed = jnp.einsum("srgju,urgd->srgjd", fresh_weights.astype(BF), new_values, preferred_element_type=F32)

    def my_share(x):
        return lax.dynamic_slice_in_dim(x, chip * share, share, 0)

    fresh_top = my_share(fresh_top.reshape(rows))
    fresh_total = my_share(fresh_total.reshape(rows))
    fresh_summed = my_share(fresh_summed.reshape(rows, DH))

    got = lax.ppermute(have, "core", SWAP)
    key_latent = jnp.where(first, have, got)
    value_latent = jnp.where(first, got, have)
    keys = mm(key_latent, key_up).astype(BF)
    values = mm(value_latent, value_up).astype(BF)
    position = chip * CORES * tok_rows + jnp.arange(CORES * tok_rows, dtype=jnp.int32)
    offsets = jnp.cumsum(prompt_lens) - prompt_lens
    member = (position[None, :] >= offsets[:, None]) & (position[None, :] < (offsets + prompt_lens)[:, None])
    key_heads = keys.reshape(-1, heads, DH)
    value_heads = values.reshape(-1, heads, DH)
    scores = jnp.einsum("srgjd,tgd->srgjt", query, key_heads, preferred_element_type=F32) * scale
    visible = member[None, :, None, None, :]
    scores = jnp.where(visible, scores, -1e30)
    top = jnp.max(scores, -1)
    weights = jnp.where(visible, jnp.exp(scores - top[..., None]), 0.0)
    total = jnp.sum(weights, -1)
    summed = jnp.einsum("srgjt,tgd->srgjd", weights.astype(BF), value_heads, preferred_element_type=F32)

    stats = jnp.stack([top.reshape(chips, share), total.reshape(chips, share)], 1).reshape(chips, 1, 2 * share)
    stats = jnp.pad(stats, ((0, 0), (0, 7), (0, DH - 2 * share)))
    sending = jnp.concatenate([summed.reshape(chips, share, DH), stats], 1)
    arrived = lax.all_to_all(sending, "chip", split_axis=0, concat_axis=0, tiled=True)
    tops = arrived[:, share, :share]
    totals = arrived[:, share, share : 2 * share]
    overall = jnp.maximum(jnp.max(tops, 0), fresh_top)
    carried = jnp.exp(tops - overall[None])
    fresh_carried = jnp.exp(fresh_top - overall)
    total = jnp.sum(totals * carried, 0) + fresh_total * fresh_carried
    summed = jnp.sum(arrived[:, :share] * carried[..., None], 0) + fresh_summed * fresh_carried[:, None]
    result = (summed / total[:, None]).astype(BF)

    if chips & (chips - 1) == 0:
        whole = result.reshape(1, share, DH)
        span = 1
        while span < chips:
            away = lax.ppermute(whole, "chip", [(c, c ^ span) for c in range(chips)])
            upper = (chip & span) != 0
            whole = jnp.concatenate([jnp.where(upper, away, whole), jnp.where(upper, whole, away)], 0)
            span *= 2
    else:
        whole = lax.all_gather(result, "chip", axis=0, tiled=True)
    whole = whole.reshape(pairs, 1, rows // pairs * DH)
    away = lax.ppermute(whole, "core", SWAP)
    whole = jnp.concatenate([jnp.where(first, whole, away), jnp.where(first, away, whole)], 1)
    return whole.reshape(steps_count, req_count, QH * DH)


def solution(mesh):
    groups, n_ctx = mesh.shape["groups"], mesh.shape["ctx"]
    split = Mesh(mesh.devices.reshape(groups, n_ctx // CORES, CORES), ("groups", "chip", "core"))
    ctx = ("chip", "core")
    return jax.shard_map(
        on_device,
        mesh=split,
        in_specs=(
            P(("groups",) + ctx, None),
            P(ctx, None),
            P(ctx, None),
            P(),
            P(),
            P("groups"),
            P(None, "groups", None),
            P(None, "groups", None),
        ),
        out_specs=P(None, "groups", None),
        check_vma=False,
    )
```

```python
import jax
import jax.numpy as jnp
from jax import lax
from jax.experimental import pallas as pl
from jax.experimental.pallas import tpu as pltpu
from jax.sharding import Mesh, PartitionSpec as P

QH = 64
KVH = 8
DH = 128
CORES = 2
BF = jnp.bfloat16
F32 = jnp.float32
SWAP = [(0, 1), (1, 0)]


def mm(a, b):
    return jnp.dot(a, b, preferred_element_type=F32)


def add_pieces(tokens, theirs, groups, total, core=None):
    tok_rows = tokens.shape[0]
    width = groups[0][1][0].shape[1]
    depths = [[part.shape[0] for part in parts] for _, parts in groups]
    span = sum(depths[0])
    deep = span * len(groups)
    flat = [part for _, parts in groups for part in parts]
    count = len(flat)
    last = core is not None
    places = jnp.stack([start for start, _ in groups] + ([core * tok_rows, (1 - core) * tok_rows] if last else []))

    def kernel(places_ref, mine_ref, theirs_ref, *refs):
        parts = refs[:count]
        total_ref, out_ref, mark_ref, columns, weights, sems = (
            refs[count:] if total is not None else (None,) + refs[count:]
        )
        copies = []
        for j, source in enumerate((mine_ref, theirs_ref)):
            for g in range(len(groups)):
                start = pl.multiple_of(places_ref[g], 128)
                copy = pltpu.make_async_copy(
                    source.at[:, pl.ds(start, span)], columns.at[j, :, pl.ds(g * span, span)], sems.at[j, g]
                )
                copy.start()
                copies.append(copy)
        at = 0
        for part in parts:
            weights[at : at + part.shape[0], :] = part[...]
            at += part.shape[0]
        mark_ref[...] = jnp.zeros_like(mark_ref)
        for j in range(2):
            for g in range(len(groups)):
                copies[j * len(groups) + g].wait()
            rows = pl.ds(j * tok_rows, tok_rows)
            term = mm(columns[j], weights[...])
            if total is not None:
                term = total_ref[rows, :] + term
            if last:
                rows = pl.ds(pl.multiple_of(places_ref[len(groups) + j], tok_rows), tok_rows)
            out_ref[rows, :] = term.astype(out_ref.dtype)

    in_vmem = pl.BlockSpec(memory_space=pltpu.VMEM)
    in_any = pl.BlockSpec(memory_space=pl.ANY)
    sums = [] if total is None else [total]
    return pl.pallas_call(
        kernel,
        out_shape=(
            jax.ShapeDtypeStruct((2 * tok_rows, width), BF if last else F32),
            jax.ShapeDtypeStruct((8, 128), F32),
        ),
        in_specs=[pl.BlockSpec(memory_space=pltpu.SMEM), in_any, in_any] + [in_vmem] * (count + len(sums)),
        out_specs=(in_vmem, in_vmem),
        scratch_shapes=[
            pltpu.VMEM((2, tok_rows, deep), BF),
            pltpu.VMEM((deep, width), BF),
            pltpu.SemaphoreType.DMA((2, len(groups))),
        ],
        input_output_aliases={} if total is None or last else {3 + count: 0},
        compiler_params=pltpu.CompilerParams(vmem_limit_bytes=48 * 2**20),
        cost_estimate=pl.CostEstimate(
            flops=4 * tok_rows * deep * width, bytes_accessed=4 * tok_rows * deep, transcendentals=0
        ),
    )(places, tokens, theirs, *flat, *sums)


def project(tokens, key_down, value_down, early):
    chips = lax.axis_size("chip")
    chip = lax.axis_index("chip")
    core = lax.axis_index("core")
    first = core == 0
    shard = key_down.shape[0]
    rows = CORES * shard
    own = jnp.where(first, key_down, value_down)
    got = lax.ppermute(jnp.where(first, value_down, key_down), "core", SWAP)
    if chips > 8:
        theirs = lax.ppermute(tokens, "core", SWAP)
        block = jnp.concatenate([jnp.where(first, own, got), jnp.where(first, got, own)], 0)
        full = lax.all_gather(block, "chip", axis=0, tiled=True)
        mine, other = mm(tokens, full).astype(BF), mm(theirs, full).astype(BF)
        return jnp.concatenate([jnp.where(first, mine, other), jnp.where(first, other, mine)], 0), early
    cycle = list(range(0, chips, 2)) + list(range(chips - 1, 0, -2))
    last = chips - 1
    place = jnp.where(chip & 1 == 0, chip >> 1, last - (chip >> 1))
    chains = 2
    piece = shard // chains
    right = [(cycle[i], cycle[(i + 1) % chips]) for i in range(chips)]
    left = [(b, a) for a, b in right]
    ways = [right] * chains + [left] * chains

    def start_of(way, step):
        spot = place - step if way == 0 else place + step
        spot = jnp.where(spot < 0, spot + chips, jnp.where(spot > last, spot - chips, spot))
        source = jnp.where(spot < chips // 2, 2 * spot, 2 * (last - spot) + 1)
        return source * rows + (core if way == 0 else 1 - core) * shard

    held = [own[k * piece : (k + 1) * piece] for k in range(chains)]
    got, tokens_later = lax.optimization_barrier((got, tokens))
    held += [got[k * piece : (k + 1) * piece] for k in range(chains)]
    theirs = lax.ppermute(tokens_later, "core", SWAP)
    todo = [(start_of(0, 0), [own]), (start_of(1, 0), [got])]
    total = None
    mark = None
    for step in range(1, chips):
        ready = todo
        if step == 2:
            held[0], early = lax.optimization_barrier((held[0], early))
        for k in range(2 * chains):
            if mark is not None:
                held[k], _ = lax.optimization_barrier((held[k], mark))
            held[k] = lax.ppermute(held[k], "chip", ways[k])
        arriving = [(start_of(w, step), held[w * chains : (w + 1) * chains]) for w in range(2)]
        if step == 1:
            todo = todo + arriving
        else:
            total, mark = add_pieces(tokens, theirs, ready, total)
            todo = arriving
    return add_pieces(tokens, theirs, todo, total, core)[0], early


def attend(have, got, core, key_up, value_up, query, bounds, chips):
    heads, rows = query.shape[:2]
    tokens = have.shape[0]
    pairs = rows // 8
    blocks = pairs * heads // chips
    scale = 1.0 / DH**0.5

    def kernel(core_ref, have_ref, got_ref, key_up_ref, value_up_ref, query_ref, bounds_ref, out_ref):
        first = core_ref[0] == 0
        have, got = have_ref[...], got_ref[...]
        keys = mm(jnp.where(first, have, got), key_up_ref[...]).astype(BF)
        values = mm(jnp.where(first, got, have), value_up_ref[...]).astype(BF)
        position = lax.broadcasted_iota(jnp.int32, (tokens, rows), 0)
        visible = (position >= bounds_ref[0:1, :]) & (position < bounds_ref[1:2, :])
        tops, totals = [], []
        for g in range(heads):
            lanes = slice(g * DH, (g + 1) * DH)
            scores = scale * lax.dot_general(
                keys[:, lanes], query_ref[g], (((1,), (1,)), ((), ())), preferred_element_type=F32
            )
            scores = jnp.where(visible, scores, -1e30)
            top = jnp.max(scores, 0, keepdims=True)
            weights = jnp.where(visible, jnp.exp(scores - top), 0.0)
            tops.append(top)
            totals.append(jnp.sum(weights, 0, keepdims=True))
            summed = lax.dot_general(
                weights.astype(BF), values[:, lanes], (((0,), (0,)), ((), ())), preferred_element_type=F32
            )
            for pair in range(pairs):
                block = pair * heads + g
                out_ref[block // blocks, block % blocks] = summed[pair * 8 : (pair + 1) * 8]
        stats = jnp.transpose(jnp.concatenate(tops + totals, 0))
        stride = min(blocks, heads)
        for chip in range(chips):
            spots = [divmod(b, heads) for b in range(chip * blocks, (chip + 1) * blocks, stride)]
            sides = [
                stats[pair * 8 : (pair + 1) * 8, side + g : side + g + stride] for side in (0, heads) for pair, g in spots
            ]
            out_ref[chip, blocks] = jnp.zeros((8, DH), F32)
            out_ref[chip, blocks, :, : 2 * blocks] = jnp.concatenate(sides, 1)

    in_vmem = pl.BlockSpec(memory_space=pltpu.VMEM)
    return pl.pallas_call(
        kernel,
        out_shape=jax.ShapeDtypeStruct((chips, blocks + 1, 8, DH), F32),
        in_specs=[pl.BlockSpec(memory_space=pltpu.SMEM)] + [in_vmem] * 6,
        out_specs=in_vmem,
        compiler_params=pltpu.CompilerParams(vmem_limit_bytes=40 * 2**20),
        cost_estimate=pl.CostEstimate(
            flops=4 * tokens * (have.shape[1] * heads * DH + heads * rows * DH),
            bytes_accessed=4 * tokens * have.shape[1],
            transcendentals=tokens * heads * rows,
        ),
    )(core.reshape(1), have, got, key_up, value_up, query, bounds)


def merge(arrived, fresh_stats, fresh_summed):
    chips, blocks = arrived.shape[0], arrived.shape[1] - 1

    def kernel(arrived_ref, stats_ref, summed_ref, out_ref):
        results = []
        for b in range(blocks):
            top = arrived_ref[:, blocks, :, b : b + 1]
            total = arrived_ref[:, blocks, :, blocks + b : blocks + b + 1]
            fresh_top = stats_ref[:, b : b + 1]
            overall = jnp.maximum(jnp.max(top, 0), fresh_top)
            carried = jnp.exp(top - overall[None])
            fresh_carried = jnp.exp(fresh_top - overall)
            total = jnp.sum(total * carried, 0) + stats_ref[:, blocks + b : blocks + b + 1] * fresh_carried
            summed = jnp.sum(arrived_ref[:, b] * carried, 0) + summed_ref[b * 8 : (b + 1) * 8, :] * fresh_carried
            results.append(summed / total)
        out_ref[...] = jnp.concatenate(results, 0).astype(BF)

    in_vmem = pl.BlockSpec(memory_space=pltpu.VMEM)
    return pl.pallas_call(
        kernel,
        out_shape=jax.ShapeDtypeStruct((blocks * 8, DH), BF),
        in_specs=[in_vmem] * 3,
        out_specs=in_vmem,
        cost_estimate=pl.CostEstimate(
            flops=2 * chips * blocks * 8 * DH, bytes_accessed=4 * arrived.size, transcendentals=chips * blocks * 8
        ),
    )(arrived, fresh_stats, fresh_summed)


def on_device(tokens, key_down, value_down, key_up, value_up, prompt_lens, queries, new_latent):
    chips = lax.axis_size("chip")
    chip = lax.axis_index("chip")
    core = lax.axis_index("core")
    first = core == 0
    tok_rows = tokens.shape[0]
    lat_width = key_down.shape[1]
    group = QH // KVH
    heads = KVH // CORES
    scale = 1.0 / DH**0.5
    steps_count, req_count = (queries.shape[0], queries.shape[1])
    pairs = steps_count * req_count
    rows = pairs * heads * group
    share = rows // chips

    query = lax.dynamic_index_in_dim(
        queries.reshape(steps_count, req_count, CORES, heads * group * DH), core, 2, keepdims=False
    ).reshape(steps_count, req_count, heads, group, DH)
    key_up = lax.dynamic_slice_in_dim(key_up, core * heads * DH, heads * DH, 1)
    value_up = lax.dynamic_slice_in_dim(value_up, core * heads * DH, heads * DH, 1)
    flat_new = new_latent.reshape(pairs, 2 * lat_width)
    new_keys = mm(flat_new[:, :lat_width], key_up).astype(BF).reshape(steps_count, req_count, heads, DH)
    new_values = mm(flat_new[:, lat_width:], value_up).astype(BF).reshape(steps_count, req_count, heads, DH)
    causal = (jnp.arange(steps_count)[:, None] >= jnp.arange(steps_count)[None, :])[:, None, None, None, :]
    fresh = jnp.einsum("srgjd,urgd->srgju", query, new_keys, preferred_element_type=F32) * scale
    fresh = jnp.where(causal, fresh, -1e30)
    fresh_top = jnp.max(fresh, -1)
    fresh_weights = jnp.where(causal, jnp.exp(fresh - fresh_top[..., None]), 0.0)
    fresh_total = jnp.sum(fresh_weights, -1)
    fresh_summed = jnp.einsum("srgju,urgd->srgjd", fresh_weights.astype(BF), new_values, preferred_element_type=F32)

    def my_share(x):
        return lax.dynamic_slice_in_dim(x, chip * share, share, 0)

    fresh_summed = my_share(fresh_summed.reshape(rows, DH))
    fresh_stats = [my_share(x.reshape(rows)).reshape(-1, group).T for x in (fresh_top, fresh_total)]
    fresh_stats = jnp.pad(jnp.concatenate(fresh_stats, 1), ((0, 0), (0, DH - 2 * share // group)))

    offsets = jnp.cumsum(prompt_lens) - prompt_lens
    bounds = jnp.stack([offsets, offsets + prompt_lens]) - chip * CORES * tok_rows
    bounds = jnp.broadcast_to(bounds[:, None, :, None], (2, steps_count, req_count, group)).reshape(2, -1)
    by_head = query.transpose(2, 0, 1, 3, 4).reshape(heads, pairs * group, DH)

    early = (by_head, bounds, key_up, value_up, fresh_stats, fresh_summed)
    have, early = project(tokens, key_down, value_down, early)
    by_head, bounds, key_up, value_up, fresh_stats, fresh_summed = early
    got = lax.ppermute(have, "core", SWAP)
    sending = attend(have, got, core, key_up, value_up, by_head, bounds, chips)

    arrived = lax.all_to_all(sending, "chip", split_axis=0, concat_axis=0, tiled=True)
    result = merge(arrived, fresh_stats, fresh_summed)

    if chips == 8:
        near = lax.ppermute(result, "chip", [(c, c ^ 1) for c in range(chips)])
        upper = chip & 1 == 1
        couple = jnp.concatenate([jnp.where(upper, near, result), jnp.where(upper, result, near)], 0)
        far = [couple] + [lax.ppermute(couple, "chip", [(c, c ^ (2 * d)) for c in range(chips)]) for d in range(1, 4)]
        odd, high = chip & 2 != 0, chip & 4 != 0

        def of(z):
            return jnp.where(high, jnp.where(odd, far[z ^ 3], far[z ^ 2]), jnp.where(odd, far[z ^ 1], far[z]))

        whole = jnp.concatenate([of(z) for z in range(4)], 0)
    else:
        whole = lax.all_gather(result, "chip", axis=0, tiled=True)
    whole = whole.reshape(pairs, 1, rows // pairs * DH)
    away = lax.ppermute(whole, "core", SWAP)
    whole = jnp.concatenate([jnp.where(first, whole, away), jnp.where(first, away, whole)], 1)
    return whole.reshape(steps_count, req_count, QH * DH)


def solution(mesh):
    groups, n_ctx = mesh.shape["groups"], mesh.shape["ctx"]
    split = Mesh(mesh.devices.reshape(groups, n_ctx // CORES, CORES), ("groups", "chip", "core"))
    ctx = ("chip", "core")
    return jax.shard_map(
        on_device,
        mesh=split,
        in_specs=(
            P(("groups",) + ctx, None),
            P(ctx, None),
            P(ctx, None),
            P(),
            P(),
            P("groups"),
            P(None, "groups", None),
            P(None, "groups", None),
        ),
        out_specs=P(None, "groups", None),
        check_vma=False,
    )
```

```python
import jax
import jax.numpy as jnp
from jax import lax
from jax.experimental import pallas as pl
from jax.experimental.pallas import tpu as pltpu
from jax.sharding import Mesh, PartitionSpec as P

QH = 64
KVH = 8
DH = 128
CORES = 2
BF = jnp.bfloat16
F32 = jnp.float32
SWAP = [(0, 1), (1, 0)]


def mm(a, b):
    return jnp.dot(a, b, preferred_element_type=F32)


def add_pieces(tokens, theirs, halves, total, part, core=None):
    tok_rows = tokens.shape[0]
    span = sum(x.shape[0] for x in halves[0][1:])
    width = halves[0][1].shape[1]
    deep = span * len(halves)
    flat = [x for half in halves for x in half[1:]]
    count = len(flat)
    last = core is not None
    places = jnp.stack([half[0] for half in halves] + [part] + ([core, 1 - core] if last else []))

    def kernel(places_ref, mine_ref, theirs_ref, *refs):
        parts = list(refs[:count])
        total_ref, out_ref, mark_ref, columns, weights, sems = (
            refs[count:] if total is not None else (None,) + refs[count:]
        )
        copies = []
        for j, source in enumerate((mine_ref, theirs_ref)):
            for h in range(len(halves)):
                start = pl.multiple_of(places_ref[h], 128)
                copy = pltpu.make_async_copy(
                    source.at[:, pl.ds(start, span)], columns.at[j, :, pl.ds(h * span, span)], sems.at[j, h]
                )
                copy.start()
                copies.append(copy)
        for h, half in enumerate(halves):
            at = h * span
            shared = half[1].shape[0]
            weights[at : at + shared, :] = parts.pop(0)[...]
            if len(half) > 2:
                rest = half[2].shape[0]
                for turn in (places_ref[len(halves)], 1 - places_ref[len(halves)]):
                    weights[pl.ds(pl.multiple_of(at + shared + turn * rest, rest), rest), :] = parts.pop(0)[...]
        mark_ref[...] = jnp.zeros_like(mark_ref)
        for j in range(2):
            for h in range(len(halves)):
                copies[j * len(halves) + h].wait()
            rows = pl.ds(j * tok_rows, tok_rows)
            term = mm(columns[j], weights[...])
            if total is not None:
                term = total_ref[rows, :] + term
            if last:
                rows = pl.ds(pl.multiple_of(places_ref[len(halves) + 1 + j] * tok_rows, tok_rows), tok_rows)
            out_ref[rows, :] = term.astype(out_ref.dtype)

    in_vmem = pl.BlockSpec(memory_space=pltpu.VMEM)
    in_any = pl.BlockSpec(memory_space=pl.ANY)
    sums = [] if total is None else [total]
    return pl.pallas_call(
        kernel,
        out_shape=(
            jax.ShapeDtypeStruct((2 * tok_rows, width), BF if last else F32),
            jax.ShapeDtypeStruct((8, 128), F32),
        ),
        in_specs=[pl.BlockSpec(memory_space=pltpu.SMEM), in_any, in_any] + [in_vmem] * (count + len(sums)),
        out_specs=(in_vmem, in_vmem),
        scratch_shapes=[
            pltpu.VMEM((2, tok_rows, deep), BF),
            pltpu.VMEM((deep, width), BF),
            pltpu.SemaphoreType.DMA((2, len(halves))),
        ],
        input_output_aliases={} if total is None or last else {3 + count: 0},
        compiler_params=pltpu.CompilerParams(vmem_limit_bytes=48 * 2**20),
        cost_estimate=pl.CostEstimate(
            flops=4 * tok_rows * deep * width, bytes_accessed=4 * tok_rows * deep, transcendentals=0
        ),
    )(places, tokens, theirs, *flat, *sums)


def project(tokens, key_down, value_down, prepare, inputs):
    chips = lax.axis_size("chip")
    chip = lax.axis_index("chip")
    core = lax.axis_index("core")
    part = lax.axis_index("groups")
    first = core == 0
    shard = key_down.shape[0]
    rows = CORES * shard
    own = jnp.where(first, key_down, value_down)
    got = lax.ppermute(jnp.where(first, value_down, key_down), "core", SWAP)
    if chips != 8 or lax.axis_size("groups") != 2:
        theirs = lax.ppermute(tokens, "core", SWAP)
        block = jnp.concatenate([jnp.where(first, own, got), jnp.where(first, got, own)], 0)
        full = lax.all_gather(block, "chip", axis=0, tiled=True)
        mine, other = mm(tokens, full).astype(BF), mm(theirs, full).astype(BF)
        return jnp.concatenate([jnp.where(first, mine, other), jnp.where(first, other, mine)], 0), prepare(*inputs)
    cycle = list(range(0, chips, 2)) + list(range(chips - 1, 0, -2))
    last = chips - 1
    place = jnp.where(chip & 1 == 0, chip >> 1, last - (chip >> 1))
    right = [(cycle[i], cycle[(i + 1) % chips]) for i in range(chips)]
    ways = (right, [(b, a) for a, b in right])

    def start_of(way, step):
        spot = place - step if way == 0 else place + step
        spot = jnp.where(spot < 0, spot + chips, jnp.where(spot > last, spot - chips, spot))
        source = jnp.where(spot < chips // 2, 2 * spot, 2 * (last - spot) + 1)
        return source * rows + (core if way == 0 else 1 - core) * shard

    rest = shard // 4
    shared = shard - 2 * rest

    def turns(half):
        return jnp.where(part == 0, half[shared : shared + rest], half[shared + rest :])

    both, single = [own[:shared]], [turns(own)]
    got, tokens_later = lax.optimization_barrier((got, tokens))
    both.append(got[:shared])
    single.append(turns(got))
    theirs = lax.ppermute(tokens_later, "core", SWAP)
    todo = [(start_of(0, 0), own), (start_of(1, 0), got)]
    calls = {3: 4, 5: 4, 7: 4}
    total = mark = others = None
    for step in range(1, chips):
        if step == 2:
            both, single, inputs = lax.optimization_barrier((both, single, inputs))
            early = prepare(*inputs)
        if step == 4:
            both[0], early = lax.optimization_barrier((both[0], early))
        if mark is not None:
            both = [lax.optimization_barrier((x, mark))[0] for x in both]
            single = [lax.optimization_barrier((x, mark))[0] for x in single]
            mark = None
        passed = single
        both = [lax.ppermute(x, "chip", way) for x, way in zip(both, ways)]
        single = [lax.ppermute(x, "chip", way) for x, way in zip(single, ways)]
        if step > 1:
            crossed = lax.ppermute(jnp.concatenate(passed, 0), "groups", SWAP)
            others = [crossed[:rest], crossed[rest:]]
            todo += [(start_of(w, step - 1), before[w], passed[w], others[w]) for w in range(2)]
        before = both
        if step in calls:
            ready, todo = todo[: calls[step]], todo[calls[step] :]
            total, mark = add_pieces(tokens, theirs, ready, total, part)
    others = [lax.ppermute(x, "chip", way) for x, way in zip(others, ways)]
    total, _ = add_pieces(tokens, theirs, todo, total, part)
    final = [(start_of(w, last), both[w], single[w], others[w]) for w in range(2)]
    return add_pieces(tokens, theirs, final, total, part, core)[0], early


def attend(have, got, core, key_up, value_up, query, bounds, chips):
    heads, rows = query.shape[:2]
    tokens = have.shape[0]
    pairs = rows // 8
    blocks = pairs * heads // chips
    scale = 1.0 / DH**0.5

    def kernel(core_ref, have_ref, got_ref, key_up_ref, value_up_ref, query_ref, bounds_ref, out_ref):
        first = core_ref[0] == 0
        have, got = have_ref[...], got_ref[...]
        keys = mm(jnp.where(first, have, got), key_up_ref[...]).astype(BF)
        values = mm(jnp.where(first, got, have), value_up_ref[...]).astype(BF)
        position = lax.broadcasted_iota(jnp.int32, (tokens, rows), 0)
        visible = (position >= bounds_ref[0:1, :]) & (position < bounds_ref[1:2, :])
        tops, totals = [], []
        for g in range(heads):
            lanes = slice(g * DH, (g + 1) * DH)
            scores = scale * lax.dot_general(
                keys[:, lanes], query_ref[g], (((1,), (1,)), ((), ())), preferred_element_type=F32
            )
            scores = jnp.where(visible, scores, -1e30)
            top = jnp.max(scores, 0, keepdims=True)
            weights = jnp.where(visible, jnp.exp(scores - top), 0.0)
            tops.append(top)
            totals.append(jnp.sum(weights, 0, keepdims=True))
            summed = lax.dot_general(
                weights.astype(BF), values[:, lanes], (((0,), (0,)), ((), ())), preferred_element_type=F32
            )
            for pair in range(pairs):
                block = pair * heads + g
                out_ref[block // blocks, block % blocks] = summed[pair * 8 : (pair + 1) * 8]
        stats = jnp.transpose(jnp.concatenate(tops + totals, 0))
        stride = min(blocks, heads)
        for chip in range(chips):
            spots = [divmod(b, heads) for b in range(chip * blocks, (chip + 1) * blocks, stride)]
            sides = [
                stats[pair * 8 : (pair + 1) * 8, side + g : side + g + stride] for side in (0, heads) for pair, g in spots
            ]
            out_ref[chip, blocks] = jnp.zeros((8, DH), F32)
            out_ref[chip, blocks, :, : 2 * blocks] = jnp.concatenate(sides, 1)

    in_vmem = pl.BlockSpec(memory_space=pltpu.VMEM)
    return pl.pallas_call(
        kernel,
        out_shape=jax.ShapeDtypeStruct((chips, blocks + 1, 8, DH), F32),
        in_specs=[pl.BlockSpec(memory_space=pltpu.SMEM)] + [in_vmem] * 6,
        out_specs=in_vmem,
        compiler_params=pltpu.CompilerParams(vmem_limit_bytes=40 * 2**20),
        cost_estimate=pl.CostEstimate(
            flops=4 * tokens * (have.shape[1] * heads * DH + heads * rows * DH),
            bytes_accessed=4 * tokens * have.shape[1],
            transcendentals=tokens * heads * rows,
        ),
    )(core.reshape(1), have, got, key_up, value_up, query, bounds)


def merge(arrived, fresh_stats, fresh_summed):
    chips, blocks = arrived.shape[0], arrived.shape[1] - 1

    def kernel(arrived_ref, stats_ref, summed_ref, out_ref):
        results = []
        for b in range(blocks):
            top = arrived_ref[:, blocks, :, b : b + 1]
            total = arrived_ref[:, blocks, :, blocks + b : blocks + b + 1]
            fresh_top = stats_ref[:, b : b + 1]
            overall = jnp.maximum(jnp.max(top, 0), fresh_top)
            carried = jnp.exp(top - overall[None])
            fresh_carried = jnp.exp(fresh_top - overall)
            total = jnp.sum(total * carried, 0) + stats_ref[:, blocks + b : blocks + b + 1] * fresh_carried
            summed = jnp.sum(arrived_ref[:, b] * carried, 0) + summed_ref[b * 8 : (b + 1) * 8, :] * fresh_carried
            results.append(summed / total)
        out_ref[...] = jnp.concatenate(results, 0).astype(BF)

    in_vmem = pl.BlockSpec(memory_space=pltpu.VMEM)
    return pl.pallas_call(
        kernel,
        out_shape=jax.ShapeDtypeStruct((blocks * 8, DH), BF),
        in_specs=[in_vmem] * 3,
        out_specs=in_vmem,
        cost_estimate=pl.CostEstimate(
            flops=2 * chips * blocks * 8 * DH, bytes_accessed=4 * arrived.size, transcendentals=chips * blocks * 8
        ),
    )(arrived, fresh_stats, fresh_summed)


def on_device(tokens, key_down, value_down, key_up, value_up, prompt_lens, queries, new_latent):
    chips = lax.axis_size("chip")
    chip = lax.axis_index("chip")
    core = lax.axis_index("core")
    first = core == 0
    tok_rows = tokens.shape[0]
    lat_width = key_down.shape[1]
    group = QH // KVH
    heads = KVH // CORES
    scale = 1.0 / DH**0.5
    steps_count, req_count = (queries.shape[0], queries.shape[1])
    pairs = steps_count * req_count
    rows = pairs * heads * group
    share = rows // chips

    def prepare(queries, new_latent, key_up, value_up):
        query = lax.dynamic_index_in_dim(
            queries.reshape(steps_count, req_count, CORES, heads * group * DH), core, 2, keepdims=False
        ).reshape(steps_count, req_count, heads, group, DH)
        key_up = lax.dynamic_slice_in_dim(key_up, core * heads * DH, heads * DH, 1)
        value_up = lax.dynamic_slice_in_dim(value_up, core * heads * DH, heads * DH, 1)
        flat_new = new_latent.reshape(pairs, 2 * lat_width)
        new_keys = mm(flat_new[:, :lat_width], key_up).astype(BF).reshape(steps_count, req_count, heads, DH)
        new_values = mm(flat_new[:, lat_width:], value_up).astype(BF).reshape(steps_count, req_count, heads, DH)
        causal = (jnp.arange(steps_count)[:, None] >= jnp.arange(steps_count)[None, :])[:, None, None, None, :]
        fresh = jnp.einsum("srgjd,urgd->srgju", query, new_keys, preferred_element_type=F32) * scale
        fresh = jnp.where(causal, fresh, -1e30)
        fresh_top = jnp.max(fresh, -1)
        fresh_weights = jnp.where(causal, jnp.exp(fresh - fresh_top[..., None]), 0.0)
        fresh_total = jnp.sum(fresh_weights, -1)
        fresh_summed = jnp.einsum("srgju,urgd->srgjd", fresh_weights.astype(BF), new_values, preferred_element_type=F32)

        def my_share(x):
            return lax.dynamic_slice_in_dim(x, chip * share, share, 0)

        fresh_summed = my_share(fresh_summed.reshape(rows, DH))
        fresh_stats = [my_share(x.reshape(rows)).reshape(-1, group).T for x in (fresh_top, fresh_total)]
        fresh_stats = jnp.pad(jnp.concatenate(fresh_stats, 1), ((0, 0), (0, DH - 2 * share // group)))

        offsets = jnp.cumsum(prompt_lens) - prompt_lens
        bounds = jnp.stack([offsets, offsets + prompt_lens]) - chip * CORES * tok_rows
        bounds = jnp.broadcast_to(bounds[:, None, :, None], (2, steps_count, req_count, group)).reshape(2, -1)
        by_head = query.transpose(2, 0, 1, 3, 4).reshape(heads, pairs * group, DH)
        return by_head, bounds, key_up, value_up, fresh_stats, fresh_summed

    have, early = project(tokens, key_down, value_down, prepare, (queries, new_latent, key_up, value_up))
    by_head, bounds, key_up, value_up, fresh_stats, fresh_summed = early
    got = lax.ppermute(have, "core", SWAP)
    sending = attend(have, got, core, key_up, value_up, by_head, bounds, chips)

    arrived = lax.all_to_all(sending, "chip", split_axis=0, concat_axis=0, tiled=True)
    result = merge(arrived, fresh_stats, fresh_summed)

    if chips == 8:
        near = lax.ppermute(result, "chip", [(c, c ^ 1) for c in range(chips)])
        upper = chip & 1 == 1
        couple = jnp.concatenate([jnp.where(upper, near, result), jnp.where(upper, result, near)], 0)
        far = [couple] + [lax.ppermute(couple, "chip", [(c, c ^ (2 * d)) for c in range(chips)]) for d in range(1, 4)]
        odd, high = chip & 2 != 0, chip & 4 != 0

        def of(z):
            return jnp.where(high, jnp.where(odd, far[z ^ 3], far[z ^ 2]), jnp.where(odd, far[z ^ 1], far[z]))

        whole = jnp.concatenate([of(z) for z in range(4)], 0)
    else:
        whole = lax.all_gather(result, "chip", axis=0, tiled=True)
    whole = whole.reshape(pairs, 1, rows // pairs * DH)
    away = lax.ppermute(whole, "core", SWAP)
    whole = jnp.concatenate([jnp.where(first, whole, away), jnp.where(first, away, whole)], 1)
    return whole.reshape(steps_count, req_count, QH * DH)


def solution(mesh):
    groups, n_ctx = mesh.shape["groups"], mesh.shape["ctx"]
    split = Mesh(mesh.devices.reshape(groups, n_ctx // CORES, CORES), ("groups", "chip", "core"))
    ctx = ("chip", "core")
    return jax.shard_map(
        on_device,
        mesh=split,
        in_specs=(
            P(("groups",) + ctx, None),
            P(ctx, None),
            P(ctx, None),
            P(),
            P(),
            P("groups"),
            P(None, "groups", None),
            P(None, "groups", None),
        ),
        out_specs=P(None, "groups", None),
        check_vma=False,
    )
```

```python
import jax
import jax.numpy as jnp
from jax import lax
from jax.experimental import pallas as pl
from jax.experimental.pallas import tpu as pltpu
from jax.sharding import Mesh, PartitionSpec as P

QH = 64
KVH = 8
DH = 128
CORES = 2
BF = jnp.bfloat16
F32 = jnp.float32
SWAP = [(0, 1), (1, 0)]


def mm(a, b):
    return jnp.dot(a, b, preferred_element_type=F32)


def add_pieces(tokens, theirs, halves, total, part, core=None):
    tok_rows = tokens.shape[0]
    span, width = tokens.shape[1] // lax.axis_size("chip") // CORES, halves[0][1].shape[1]
    deep = span * len(halves)
    flat = [x for half in halves for x in half[1:4]]
    count = len(flat)
    last = core is not None
    places = jnp.stack([half[0] for half in halves] + [part] + ([core, 1 - core] if last else []))

    def kernel(places_ref, mine_ref, theirs_ref, *refs):
        parts = list(refs[:count])
        total_ref, out_ref, mark_ref, columns, weights, sems = (
            refs[count:] if total is not None else (None,) + refs[count:]
        )
        copies = []
        for j, source in enumerate((mine_ref, theirs_ref)):
            for h in range(len(halves)):
                start = pl.multiple_of(places_ref[h], 128)
                copy = pltpu.make_async_copy(
                    source.at[:, pl.ds(start, span)], columns.at[j, :, pl.ds(h * span, span)], sems.at[j, h]
                )
                copy.start()
                copies.append(copy)
        for h, half in enumerate(halves):
            at = h * span
            shared = half[1].shape[0]
            weights[at : at + shared, :] = parts.pop(0)[...]
            if len(half) > 2:
                rest = half[2].shape[0]
                turn = places_ref[len(halves)]
                for turn, skip in ((turn, 0), (1 - turn, half[4] * rest)):
                    rows = pl.ds(pl.multiple_of(at + shared + turn * rest, rest), rest)
                    weights[rows, :] = parts.pop(0)[skip : skip + rest, :]
        mark_ref[...] = jnp.zeros_like(mark_ref)
        for j in range(2):
            for h in range(len(halves)):
                copies[j * len(halves) + h].wait()
            rows = pl.ds(j * tok_rows, tok_rows)
            term = mm(columns[j], weights[...])
            if total is not None:
                term = total_ref[rows, :] + term
            if last:
                rows = pl.ds(pl.multiple_of(places_ref[len(halves) + 1 + j] * tok_rows, tok_rows), tok_rows)
            out_ref[rows, :] = term.astype(out_ref.dtype)

    in_vmem = pl.BlockSpec(memory_space=pltpu.VMEM)
    in_any = pl.BlockSpec(memory_space=pl.ANY)
    sums = [] if total is None else [total]
    return pl.pallas_call(
        kernel,
        out_shape=(
            jax.ShapeDtypeStruct((2 * tok_rows, width), BF if last else F32),
            jax.ShapeDtypeStruct((8, 128), F32),
        ),
        in_specs=[pl.BlockSpec(memory_space=pltpu.SMEM), in_any, in_any] + [in_vmem] * (count + len(sums)),
        out_specs=(in_vmem, in_vmem),
        scratch_shapes=[
            pltpu.VMEM((2, tok_rows, deep), BF),
            pltpu.VMEM((deep, width), BF),
            pltpu.SemaphoreType.DMA((2, len(halves))),
        ],
        input_output_aliases={} if total is None or last else {3 + count: 0},
        compiler_params=pltpu.CompilerParams(vmem_limit_bytes=48 * 2**20),
        cost_estimate=pl.CostEstimate(
            flops=4 * tok_rows * deep * width, bytes_accessed=4 * tok_rows * deep, transcendentals=0
        ),
    )(places, tokens, theirs, *flat, *sums)


def project(tokens, key_down, value_down, prepare, inputs):
    chips = lax.axis_size("chip")
    chip = lax.axis_index("chip")
    core = lax.axis_index("core")
    part = lax.axis_index("groups")
    first = core == 0
    shard = key_down.shape[0]
    rows = CORES * shard
    own = jnp.where(first, key_down, value_down)
    got = lax.ppermute(jnp.where(first, value_down, key_down), "core", SWAP)
    if chips != 8 or lax.axis_size("groups") != 2:
        theirs = lax.ppermute(tokens, "core", SWAP)
        block = jnp.concatenate([jnp.where(first, own, got), jnp.where(first, got, own)], 0)
        full = lax.all_gather(block, "chip", axis=0, tiled=True)
        mine, other = mm(tokens, full).astype(BF), mm(theirs, full).astype(BF)
        return jnp.concatenate([jnp.where(first, mine, other), jnp.where(first, other, mine)], 0), prepare(*inputs)
    cycle = list(range(0, chips, 2)) + list(range(chips - 1, 0, -2))
    last = chips - 1
    place = jnp.where(chip & 1 == 0, chip >> 1, last - (chip >> 1))
    right = [(cycle[i], cycle[(i + 1) % chips]) for i in range(chips)]
    ways = (right, [(b, a) for a, b in right])

    def start_of(way, step):
        spot = place - step if way == 0 else place + step
        spot = jnp.where(spot < 0, spot + chips, jnp.where(spot > last, spot - chips, spot))
        source = jnp.where(spot < chips // 2, 2 * spot, 2 * (last - spot) + 1)
        return source * rows + (core if way == 0 else 1 - core) * shard

    rest = shard // 4
    shared = shard - 2 * rest

    def turns(half):
        return jnp.where(part == 0, half[shared : shared + rest], half[shared + rest :])

    both, single = [own[:shared]], [turns(own)]
    got, tokens_later = lax.optimization_barrier((got, tokens))
    both.append(got[:shared])
    single.append(turns(got))
    theirs = lax.ppermute(tokens_later, "core", SWAP)
    todo = [(start_of(0, 0), own), (start_of(1, 0), got)]
    calls = {3: 4, 5: 4, 7: 4}
    total = mark = crossed = None
    for step in range(1, chips):
        if step == 2:
            both, single = lax.optimization_barrier((both, single))
        if step == last:
            _, inputs = lax.optimization_barrier((both[0], inputs))
        if mark is not None:
            both = [lax.optimization_barrier((x, mark))[0] for x in both]
            single = [lax.optimization_barrier((x, mark))[0] for x in single]
            mark = None
        passed = single
        both = [lax.ppermute(x, "chip", way) for x, way in zip(both, ways)]
        single = [lax.ppermute(x, "chip", way) for x, way in zip(single, ways)]
        if step > 1:
            crossed = lax.ppermute(jnp.concatenate(passed, 0), "groups", SWAP)
            todo += [(start_of(w, step - 1), before[w], passed[w], crossed, w) for w in range(2)]
        before = both
        if step in calls:
            ready, todo = todo[: calls[step]], todo[calls[step] :]
            total, mark = add_pieces(tokens, theirs, ready, total, part)
    crossed, _ = lax.optimization_barrier((crossed, mark))
    others = [lax.ppermute(crossed[w * rest : (w + 1) * rest], "chip", ways[w]) for w in range(2)]
    total, _ = add_pieces(tokens, theirs, todo, total, part)
    final = [(start_of(w, last), both[w], single[w], others[w], 0) for w in range(2)]
    return add_pieces(tokens, theirs, final, total, part, core)[0], prepare(*inputs)


def attend(have, got, core, key_up, value_up, query, bounds, chips):
    heads, rows = query.shape[:2]
    tokens = have.shape[0]
    pairs = rows // 8
    blocks = pairs * heads // chips
    scale = 1.0 / DH**0.5

    def kernel(core_ref, have_ref, got_ref, key_up_ref, value_up_ref, query_ref, bounds_ref, out_ref):
        first = core_ref[0] == 0
        have, got = have_ref[...], got_ref[...]
        lanes = pl.ds(pl.multiple_of(core_ref[0] * heads * DH, heads * DH), heads * DH)
        keys = mm(jnp.where(first, have, got), key_up_ref[:, lanes]).astype(BF)
        values = mm(jnp.where(first, got, have), value_up_ref[:, lanes]).astype(BF)
        position = lax.broadcasted_iota(jnp.int32, (tokens, rows), 0)
        visible = (position >= bounds_ref[0:1, :]) & (position < bounds_ref[1:2, :])
        tops, totals = [], []
        for g in range(heads):
            lanes = slice(g * DH, (g + 1) * DH)
            scores = scale * lax.dot_general(
                keys[:, lanes], query_ref[g], (((1,), (1,)), ((), ())), preferred_element_type=F32
            )
            scores = jnp.where(visible, scores, -1e30)
            top = jnp.max(scores, 0, keepdims=True)
            weights = jnp.where(visible, jnp.exp(scores - top), 0.0)
            tops.append(top)
            totals.append(jnp.sum(weights, 0, keepdims=True))
            summed = lax.dot_general(
                weights.astype(BF), values[:, lanes], (((0,), (0,)), ((), ())), preferred_element_type=F32
            )
            for pair in range(pairs):
                block = pair * heads + g
                out_ref[block // blocks, block % blocks] = summed[pair * 8 : (pair + 1) * 8]
        stats = jnp.transpose(jnp.concatenate(tops + totals, 0))
        stride = min(blocks, heads)
        for chip in range(chips):
            spots = [divmod(b, heads) for b in range(chip * blocks, (chip + 1) * blocks, stride)]
            sides = [
                stats[pair * 8 : (pair + 1) * 8, side + g : side + g + stride] for side in (0, heads) for pair, g in spots
            ]
            out_ref[chip, blocks] = jnp.zeros((8, DH), F32)
            out_ref[chip, blocks, :, : 2 * blocks] = jnp.concatenate(sides, 1)

    in_vmem = pl.BlockSpec(memory_space=pltpu.VMEM)
    return pl.pallas_call(
        kernel,
        out_shape=jax.ShapeDtypeStruct((chips, blocks + 1, 8, DH), F32),
        in_specs=[pl.BlockSpec(memory_space=pltpu.SMEM)] + [in_vmem] * 6,
        out_specs=in_vmem,
        compiler_params=pltpu.CompilerParams(vmem_limit_bytes=40 * 2**20),
        cost_estimate=pl.CostEstimate(
            flops=4 * tokens * (have.shape[1] * heads * DH + heads * rows * DH),
            bytes_accessed=4 * tokens * have.shape[1],
            transcendentals=tokens * heads * rows,
        ),
    )(core.reshape(1), have, got, key_up, value_up, query, bounds)


def merge(arrived, fresh_stats, fresh_summed):
    chips, blocks = arrived.shape[0], arrived.shape[1] - 1

    def kernel(arrived_ref, stats_ref, summed_ref, out_ref):
        results = []
        for b in range(blocks):
            top = arrived_ref[:, blocks, :, b : b + 1]
            total = arrived_ref[:, blocks, :, blocks + b : blocks + b + 1]
            fresh_top = stats_ref[:, b : b + 1]
            overall = jnp.maximum(jnp.max(top, 0), fresh_top)
            carried = jnp.exp(top - overall[None])
            fresh_carried = jnp.exp(fresh_top - overall)
            total = jnp.sum(total * carried, 0) + stats_ref[:, blocks + b : blocks + b + 1] * fresh_carried
            summed = jnp.sum(arrived_ref[:, b] * carried, 0) + summed_ref[b * 8 : (b + 1) * 8, :] * fresh_carried
            results.append(summed / total)
        out_ref[...] = jnp.concatenate(results, 0).astype(BF)

    in_vmem = pl.BlockSpec(memory_space=pltpu.VMEM)
    return pl.pallas_call(
        kernel,
        out_shape=jax.ShapeDtypeStruct((blocks * 8, DH), BF),
        in_specs=[in_vmem] * 3,
        out_specs=in_vmem,
        cost_estimate=pl.CostEstimate(
            flops=2 * chips * blocks * 8 * DH, bytes_accessed=4 * arrived.size, transcendentals=chips * blocks * 8
        ),
    )(arrived, fresh_stats, fresh_summed)


def on_device(tokens, key_down, value_down, key_up, value_up, prompt_lens, queries, new_latent):
    chips = lax.axis_size("chip")
    chip = lax.axis_index("chip")
    core = lax.axis_index("core")
    first = core == 0
    tok_rows = tokens.shape[0]
    lat_width = key_down.shape[1]
    group = QH // KVH
    heads = KVH // CORES
    scale = 1.0 / DH**0.5
    steps_count, req_count = (queries.shape[0], queries.shape[1])
    pairs = steps_count * req_count
    rows = pairs * heads * group
    share = rows // chips

    def by_head(queries):
        mine = lax.dynamic_slice_in_dim(queries, core * heads * group * DH, heads * group * DH, 2)
        return mine.reshape(steps_count, req_count, heads, group, DH).transpose(2, 0, 1, 3, 4)

    have, query = project(tokens, key_down, value_down, by_head, (queries,))
    got = lax.ppermute(have, "core", SWAP)

    offsets = jnp.cumsum(prompt_lens) - prompt_lens
    bounds = jnp.stack([offsets, offsets + prompt_lens]) - chip * CORES * tok_rows
    bounds = jnp.broadcast_to(bounds[:, None, :, None], (2, steps_count, req_count, group)).reshape(2, -1)
    sending = attend(have, got, core, key_up, value_up, query.reshape(heads, -1, DH), bounds, chips)

    sending, query, new_latent = lax.optimization_barrier((sending, query, new_latent))
    flat_new = new_latent.reshape(pairs, 2 * lat_width)

    def my_heads(latent, up):
        full = lax.dynamic_slice_in_dim(mm(latent, up), core * heads * DH, heads * DH, 1)
        return full.astype(BF).reshape(steps_count, req_count, heads, DH)

    new_keys = my_heads(flat_new[:, :lat_width], key_up)
    new_values = my_heads(flat_new[:, lat_width:], value_up)
    causal = (jnp.arange(steps_count)[:, None] >= jnp.arange(steps_count)[None, :])[:, None, None, None, :]
    fresh = jnp.einsum("gsrjd,urgd->srgju", query, new_keys, preferred_element_type=F32) * scale
    fresh = jnp.where(causal, fresh, -1e30)
    fresh_top = jnp.max(fresh, -1)
    fresh_weights = jnp.where(causal, jnp.exp(fresh - fresh_top[..., None]), 0.0)
    fresh_total = jnp.sum(fresh_weights, -1)
    fresh_summed = jnp.einsum("srgju,urgd->srgjd", fresh_weights.astype(BF), new_values, preferred_element_type=F32)

    def my_share(x):
        return lax.dynamic_slice_in_dim(x, chip * share, share, 0)

    fresh_summed = my_share(fresh_summed.reshape(rows, DH))
    fresh_stats = [my_share(x.reshape(rows)).reshape(-1, group).T for x in (fresh_top, fresh_total)]
    fresh_stats = jnp.pad(jnp.concatenate(fresh_stats, 1), ((0, 0), (0, DH - 2 * share // group)))

    flat = sending.reshape(chips, -1, DH)
    arrived = lax.all_to_all(flat, "chip", split_axis=0, concat_axis=0, tiled=True).reshape(sending.shape)
    result = merge(arrived, fresh_stats, fresh_summed)

    if chips == 8:
        near = lax.ppermute(result, "chip", [(c, c ^ 1) for c in range(chips)])
        upper = chip & 1 == 1
        couple = jnp.concatenate([jnp.where(upper, near, result), jnp.where(upper, result, near)], 0)
        far = [couple] + [lax.ppermute(couple, "chip", [(c, c ^ (2 * d)) for c in range(chips)]) for d in range(1, 4)]
        odd, high = chip & 2 != 0, chip & 4 != 0

        def of(z):
            return jnp.where(high, jnp.where(odd, far[z ^ 3], far[z ^ 2]), jnp.where(odd, far[z ^ 1], far[z]))

        whole = jnp.concatenate([of(z) for z in range(4)], 0)
    else:
        whole = lax.all_gather(result, "chip", axis=0, tiled=True)
    whole = whole.reshape(pairs, 1, rows // pairs * DH)
    away = lax.ppermute(whole, "core", SWAP)
    whole = jnp.concatenate([jnp.where(first, whole, away), jnp.where(first, away, whole)], 1)
    return whole.reshape(steps_count, req_count, QH * DH)


def solution(mesh):
    groups, n_ctx = mesh.shape["groups"], mesh.shape["ctx"]
    split = Mesh(mesh.devices.reshape(groups, n_ctx // CORES, CORES), ("groups", "chip", "core"))
    ctx = ("chip", "core")
    return jax.shard_map(
        on_device,
        mesh=split,
        in_specs=(
            P(("groups",) + ctx, None),
            P(ctx, None),
            P(ctx, None),
            P(),
            P(),
            P("groups"),
            P(None, "groups", None),
            P(None, "groups", None),
        ),
        out_specs=P(None, "groups", None),
        check_vma=False,
    )
```

```python
import jax
import jax.numpy as jnp
from jax import lax
from jax.experimental import pallas as pl
from jax.experimental.pallas import tpu as pltpu
from jax.sharding import Mesh, PartitionSpec as P

QH = 64
KVH = 8
DH = 128
CORES = 2
BF = jnp.bfloat16
F32 = jnp.float32
SWAP = [(0, 1), (1, 0)]


def mm(a, b):
    return jnp.dot(a, b, preferred_element_type=F32)


def add_pieces(tokens, theirs, groups, total, core=None):
    tok_rows = tokens.shape[0]
    width = groups[0][1][0].shape[1]
    depths = [[part.shape[0] for part in parts] for _, parts in groups]
    span = sum(depths[0])
    deep = span * len(groups)
    flat = [part for _, parts in groups for part in parts]
    count = len(flat)
    last = core is not None
    places = jnp.stack([start for start, _ in groups] + ([core * tok_rows, (1 - core) * tok_rows] if last else []))

    def kernel(places_ref, mine_ref, theirs_ref, *refs):
        parts = refs[:count]
        total_ref, out_ref, mark_ref, columns, weights, sems = (
            refs[count:] if total is not None else (None,) + refs[count:]
        )
        copies = []
        for j, source in enumerate((mine_ref, theirs_ref)):
            for g in range(len(groups)):
                start = pl.multiple_of(places_ref[g], 128)
                copy = pltpu.make_async_copy(
                    source.at[:, pl.ds(start, span)], columns.at[j, :, pl.ds(g * span, span)], sems.at[j, g]
                )
                copy.start()
                copies.append(copy)
        at = 0
        for part in parts:
            weights[at : at + part.shape[0], :] = part[...]
            at += part.shape[0]
        mark_ref[...] = jnp.zeros_like(mark_ref)
        for j in range(2):
            for g in range(len(groups)):
                copies[j * len(groups) + g].wait()
            rows = pl.ds(j * tok_rows, tok_rows)
            term = mm(columns[j], weights[...])
            if total is not None:
                term = total_ref[rows, :] + term
            if last:
                rows = pl.ds(pl.multiple_of(places_ref[len(groups) + j], tok_rows), tok_rows)
            out_ref[rows, :] = term.astype(out_ref.dtype)

    tokens = pltpu.with_memory_space_constraint(tokens, pltpu.HBM)
    in_vmem = pl.BlockSpec(memory_space=pltpu.VMEM)
    in_any = pl.BlockSpec(memory_space=pl.ANY)
    sums = [] if total is None else [total]
    return pl.pallas_call(
        kernel,
        out_shape=(
            jax.ShapeDtypeStruct((2 * tok_rows, width), BF if last else F32),
            jax.ShapeDtypeStruct((8, 128), F32),
        ),
        in_specs=[pl.BlockSpec(memory_space=pltpu.SMEM), in_any, in_any] + [in_vmem] * (count + len(sums)),
        out_specs=(in_vmem, in_vmem),
        scratch_shapes=[
            pltpu.VMEM((2, tok_rows, deep), BF),
            pltpu.VMEM((deep, width), BF),
            pltpu.SemaphoreType.DMA((2, len(groups))),
        ],
        input_output_aliases={} if total is None or last else {3 + count: 0},
        compiler_params=pltpu.CompilerParams(vmem_limit_bytes=30 * 2**20),
        cost_estimate=pl.CostEstimate(
            flops=4 * tok_rows * deep * width, bytes_accessed=4 * tok_rows * deep, transcendentals=0
        ),
    )(places, tokens, theirs, *flat, *sums)


def project(tokens, key_down, value_down, prepare, inputs):
    chips = lax.axis_size("chip")
    chip = lax.axis_index("chip")
    core = lax.axis_index("core")
    first = core == 0
    shard = key_down.shape[0]
    rows = CORES * shard
    own = jnp.where(first, key_down, value_down)
    got = lax.ppermute(jnp.where(first, value_down, key_down), "core", SWAP)
    if chips > 8:
        theirs = lax.ppermute(tokens, "core", SWAP)
        block = jnp.concatenate([jnp.where(first, own, got), jnp.where(first, got, own)], 0)
        full = lax.all_gather(block, "chip", axis=0, tiled=True)
        mine, other = mm(tokens, full).astype(BF), mm(theirs, full).astype(BF)
        return jnp.concatenate([jnp.where(first, mine, other), jnp.where(first, other, mine)], 0), prepare(*inputs)
    cycle = list(range(0, chips, 2)) + list(range(chips - 1, 0, -2))
    last = chips - 1
    place = jnp.where(chip & 1 == 0, chip >> 1, last - (chip >> 1))
    chains = 2
    piece = shard // chains
    right = [(cycle[i], cycle[(i + 1) % chips]) for i in range(chips)]
    left = [(b, a) for a, b in right]
    ways = [right] * chains + [left] * chains

    def start_of(way, step):
        spot = place - step if way == 0 else place + step
        spot = jnp.where(spot < 0, spot + chips, jnp.where(spot > last, spot - chips, spot))
        source = jnp.where(spot < chips // 2, 2 * spot, 2 * (last - spot) + 1)
        return source * rows + (core if way == 0 else 1 - core) * shard

    held = [own[k * piece : (k + 1) * piece] for k in range(chains)]
    got, tokens_later = lax.optimization_barrier((got, tokens))
    held += [got[k * piece : (k + 1) * piece] for k in range(chains)]
    theirs = lax.ppermute(tokens_later, "core", SWAP)
    todo = [(start_of(0, 0), [own]), (start_of(1, 0), [got])]
    total = None
    mark = None
    for step in range(1, chips):
        ready = todo
        if step == 2:
            held = lax.optimization_barrier(held)
        if step == last:
            _, inputs = lax.optimization_barrier((held[0], inputs))
        for k in range(2 * chains):
            if mark is not None:
                held[k], _ = lax.optimization_barrier((held[k], mark))
            held[k] = lax.ppermute(held[k], "chip", ways[k])
        arriving = [(start_of(w, step), held[w * chains : (w + 1) * chains]) for w in range(2)]
        if step == 1:
            todo = todo + arriving
        else:
            total, mark = add_pieces(tokens, theirs, ready, total)
            todo = arriving
    return add_pieces(tokens, theirs, todo, total, core)[0], prepare(*inputs)


def attend(have, got, core, key_up, value_up, query, bounds, chips):
    heads, rows = query.shape[:2]
    tokens = have.shape[0]
    pairs = rows // 8
    blocks = pairs * heads // chips
    scale = 1.0 / DH**0.5

    def kernel(core_ref, have_ref, got_ref, key_up_ref, value_up_ref, query_ref, bounds_ref, out_ref):
        first = core_ref[0] == 0
        have, got = have_ref[...], got_ref[...]
        lanes = pl.ds(pl.multiple_of(core_ref[0] * heads * DH, heads * DH), heads * DH)
        keys = mm(jnp.where(first, have, got), key_up_ref[:, lanes]).astype(BF)
        values = mm(jnp.where(first, got, have), value_up_ref[:, lanes]).astype(BF)
        position = lax.broadcasted_iota(jnp.int32, (tokens, rows), 0)
        visible = (position >= bounds_ref[0:1, :]) & (position < bounds_ref[1:2, :])
        tops, totals = [], []
        for g in range(heads):
            lanes = slice(g * DH, (g + 1) * DH)
            scores = scale * lax.dot_general(
                keys[:, lanes], query_ref[g], (((1,), (1,)), ((), ())), preferred_element_type=F32
            )
            scores = jnp.where(visible, scores, -1e30)
            top = jnp.max(scores, 0, keepdims=True)
            weights = jnp.where(visible, jnp.exp(scores - top), 0.0)
            tops.append(top)
            totals.append(jnp.sum(weights, 0, keepdims=True))
            summed = lax.dot_general(
                weights.astype(BF), values[:, lanes], (((0,), (0,)), ((), ())), preferred_element_type=F32
            )
            for pair in range(pairs):
                block = pair * heads + g
                out_ref[block // blocks, block % blocks] = summed[pair * 8 : (pair + 1) * 8]
        stats = jnp.transpose(jnp.concatenate(tops + totals, 0))
        stride = min(blocks, heads)
        for chip in range(chips):
            spots = [divmod(b, heads) for b in range(chip * blocks, (chip + 1) * blocks, stride)]
            sides = [
                stats[pair * 8 : (pair + 1) * 8, side + g : side + g + stride] for side in (0, heads) for pair, g in spots
            ]
            out_ref[chip, blocks] = jnp.zeros((8, DH), F32)
            out_ref[chip, blocks, :, : 2 * blocks] = jnp.concatenate(sides, 1)

    in_vmem = pl.BlockSpec(memory_space=pltpu.VMEM)
    return pl.pallas_call(
        kernel,
        out_shape=jax.ShapeDtypeStruct((chips, blocks + 1, 8, DH), F32),
        in_specs=[pl.BlockSpec(memory_space=pltpu.SMEM)] + [in_vmem] * 6,
        out_specs=in_vmem,
        compiler_params=pltpu.CompilerParams(vmem_limit_bytes=24 * 2**20),
        cost_estimate=pl.CostEstimate(
            flops=4 * tokens * (have.shape[1] * heads * DH + heads * rows * DH),
            bytes_accessed=4 * tokens * have.shape[1],
            transcendentals=tokens * heads * rows,
        ),
    )(core.reshape(1), have, got, key_up, value_up, query, bounds)


def merge(arrived, fresh_stats, fresh_summed):
    chips, blocks = arrived.shape[0], arrived.shape[1] - 1

    def kernel(arrived_ref, stats_ref, summed_ref, out_ref):
        results = []
        for b in range(blocks):
            top = arrived_ref[:, blocks, :, b : b + 1]
            total = arrived_ref[:, blocks, :, blocks + b : blocks + b + 1]
            fresh_top = stats_ref[:, b : b + 1]
            overall = jnp.maximum(jnp.max(top, 0), fresh_top)
            carried = jnp.exp(top - overall[None])
            fresh_carried = jnp.exp(fresh_top - overall)
            total = jnp.sum(total * carried, 0) + stats_ref[:, blocks + b : blocks + b + 1] * fresh_carried
            summed = jnp.sum(arrived_ref[:, b] * carried, 0) + summed_ref[b * 8 : (b + 1) * 8, :] * fresh_carried
            results.append(summed / total)
        out_ref[...] = jnp.concatenate(results, 0).astype(BF)

    in_vmem = pl.BlockSpec(memory_space=pltpu.VMEM)
    return pl.pallas_call(
        kernel,
        out_shape=jax.ShapeDtypeStruct((blocks * 8, DH), BF),
        in_specs=[in_vmem] * 3,
        out_specs=in_vmem,
        cost_estimate=pl.CostEstimate(
            flops=2 * chips * blocks * 8 * DH, bytes_accessed=4 * arrived.size, transcendentals=chips * blocks * 8
        ),
    )(arrived, fresh_stats, fresh_summed)


def on_device(tokens, key_down, value_down, key_up, value_up, prompt_lens, queries, new_latent):
    chips = lax.axis_size("chip")
    chip = lax.axis_index("chip")
    core = lax.axis_index("core")
    first = core == 0
    tok_rows = tokens.shape[0]
    lat_width = key_down.shape[1]
    group = QH // KVH
    heads = KVH // CORES
    scale = 1.0 / DH**0.5
    steps_count, req_count = (queries.shape[0], queries.shape[1])
    pairs = steps_count * req_count
    rows = pairs * heads * group
    share = rows // chips

    def by_head(queries):
        mine = lax.dynamic_slice_in_dim(queries, core * heads * group * DH, heads * group * DH, 2)
        return mine.reshape(steps_count, req_count, heads, group, DH).transpose(2, 0, 1, 3, 4)

    have, query = project(tokens, key_down, value_down, by_head, (queries,))
    got = lax.ppermute(have, "core", SWAP)

    offsets = jnp.cumsum(prompt_lens) - prompt_lens
    bounds = jnp.stack([offsets, offsets + prompt_lens]) - chip * CORES * tok_rows
    bounds = jnp.broadcast_to(bounds[:, None, :, None], (2, steps_count, req_count, group)).reshape(2, -1)
    sending = attend(have, got, core, key_up, value_up, query.reshape(heads, -1, DH), bounds, chips)

    sending, query, new_latent = lax.optimization_barrier((sending, query, new_latent))
    flat_new = new_latent.reshape(pairs, 2 * lat_width)

    def my_heads(latent, up):
        full = lax.dynamic_slice_in_dim(mm(latent, up), core * heads * DH, heads * DH, 1)
        return full.astype(BF).reshape(steps_count, req_count, heads, DH)

    new_keys = my_heads(flat_new[:, :lat_width], key_up)
    new_values = my_heads(flat_new[:, lat_width:], value_up)
    causal = (jnp.arange(steps_count)[:, None] >= jnp.arange(steps_count)[None, :])[:, None, None, None, :]
    fresh = jnp.einsum("gsrjd,urgd->srgju", query, new_keys, preferred_element_type=F32) * scale
    fresh = jnp.where(causal, fresh, -1e30)
    fresh_top = jnp.max(fresh, -1)
    fresh_weights = jnp.where(causal, jnp.exp(fresh - fresh_top[..., None]), 0.0)
    fresh_total = jnp.sum(fresh_weights, -1)
    fresh_summed = jnp.einsum("srgju,urgd->srgjd", fresh_weights.astype(BF), new_values, preferred_element_type=F32)

    def my_share(x):
        return lax.dynamic_slice_in_dim(x, chip * share, share, 0)

    fresh_summed = my_share(fresh_summed.reshape(rows, DH))
    fresh_stats = [my_share(x.reshape(rows)).reshape(-1, group).T for x in (fresh_top, fresh_total)]
    fresh_stats = jnp.pad(jnp.concatenate(fresh_stats, 1), ((0, 0), (0, DH - 2 * share // group)))

    flat = sending.reshape(chips, -1, DH)
    arrived = lax.all_to_all(flat, "chip", split_axis=0, concat_axis=0, tiled=True).reshape(sending.shape)
    result = merge(arrived, fresh_stats, fresh_summed)

    if chips == 8:
        near = lax.ppermute(result, "chip", [(c, c ^ 1) for c in range(chips)])
        upper = chip & 1 == 1
        couple = jnp.concatenate([jnp.where(upper, near, result), jnp.where(upper, result, near)], 0)
        far = [couple] + [lax.ppermute(couple, "chip", [(c, c ^ (2 * d)) for c in range(chips)]) for d in range(1, 4)]
        odd, high = chip & 2 != 0, chip & 4 != 0

        def of(z):
            return jnp.where(high, jnp.where(odd, far[z ^ 3], far[z ^ 2]), jnp.where(odd, far[z ^ 1], far[z]))

        whole = jnp.concatenate([of(z) for z in range(4)], 0)
    else:
        whole = lax.all_gather(result, "chip", axis=0, tiled=True)
    whole = whole.reshape(pairs, 1, rows // pairs * DH)
    away = lax.ppermute(whole, "core", SWAP)
    whole = jnp.concatenate([jnp.where(first, whole, away), jnp.where(first, away, whole)], 1)
    return whole.reshape(steps_count, req_count, QH * DH)


def solution(mesh):
    groups, n_ctx = mesh.shape["groups"], mesh.shape["ctx"]
    split = Mesh(mesh.devices.reshape(groups, n_ctx // CORES, CORES), ("groups", "chip", "core"))
    ctx = ("chip", "core")
    return jax.shard_map(
        on_device,
        mesh=split,
        in_specs=(
            P(("groups",) + ctx, None),
            P(ctx, None),
            P(ctx, None),
            P(),
            P(),
            P("groups"),
            P(None, "groups", None),
            P(None, "groups", None),
        ),
        out_specs=P(None, "groups", None),
        check_vma=False,
    )
```

```python
import jax
import jax.numpy as jnp
from jax import lax
from jax.experimental import pallas as pl
from jax.experimental.pallas import tpu as pltpu
from jax.sharding import Mesh, PartitionSpec as P

QH = 64
KVH = 8
DH = 128
CORES = 2
BF = jnp.bfloat16
F32 = jnp.float32
SWAP = [(0, 1), (1, 0)]


def mm(a, b):
    return jnp.dot(a, b, preferred_element_type=F32)


def add_pieces(tokens, theirs, groups, total, core=None):
    tok_rows = tokens.shape[0]
    width = groups[0][1][0].shape[1]
    depths = [[part.shape[0] for part in parts] for _, parts in groups]
    span = sum(depths[0])
    deep = span * len(groups)
    flat = [part for _, parts in groups for part in parts]
    count = len(flat)
    last = core is not None
    places = jnp.stack([start for start, _ in groups] + ([core * tok_rows, (1 - core) * tok_rows] if last else []))

    def kernel(places_ref, mine_ref, theirs_ref, *refs):
        parts = refs[:count]
        total_ref, out_ref, mark_ref, columns, weights, sems, loaded = (
            refs[count:] if total is not None else (None,) + refs[count:]
        )
        copies = []
        for j, source in enumerate((mine_ref, theirs_ref)):
            for g in range(len(groups)):
                start = pl.multiple_of(places_ref[g], 128)
                copy = pltpu.make_async_copy(
                    source.at[:, pl.ds(start, span)], columns.at[j, :, pl.ds(g * span, span)], sems.at[j, g]
                )
                copy.start()
                copies.append(copy)
        at = 0
        loads = []
        for k, part in enumerate(parts):
            load = pltpu.make_async_copy(part, weights.at[pl.ds(at, part.shape[0])], loaded.at[k])
            load.start()
            loads.append(load)
            at += part.shape[0]
        mark_ref[...] = jnp.zeros_like(mark_ref)
        for load in loads:
            load.wait()
        for j in range(2):
            for g in range(len(groups)):
                copies[j * len(groups) + g].wait()
            rows = pl.ds(j * tok_rows, tok_rows)
            term = mm(columns[j], weights[...])
            if total is not None:
                term = total_ref[rows, :] + term
            if last:
                rows = pl.ds(pl.multiple_of(places_ref[len(groups) + j], tok_rows), tok_rows)
            out_ref[rows, :] = term.astype(out_ref.dtype)

    tokens = pltpu.with_memory_space_constraint(tokens, pltpu.HBM)
    in_vmem = pl.BlockSpec(memory_space=pltpu.VMEM)
    in_any = pl.BlockSpec(memory_space=pl.ANY)
    sums = [] if total is None else [total]
    return pl.pallas_call(
        kernel,
        out_shape=(
            jax.ShapeDtypeStruct((2 * tok_rows, width), BF if last else F32),
            jax.ShapeDtypeStruct((8, 128), F32),
        ),
        in_specs=[pl.BlockSpec(memory_space=pltpu.SMEM)] + [in_any] * (2 + count) + [in_vmem] * len(sums),
        out_specs=(in_vmem, in_vmem),
        scratch_shapes=[
            pltpu.VMEM((2, tok_rows, deep), BF),
            pltpu.VMEM((deep, width), BF),
            pltpu.SemaphoreType.DMA((2, len(groups))),
            pltpu.SemaphoreType.DMA((count,)),
        ],
        input_output_aliases={} if total is None or last else {3 + count: 0},
        compiler_params=pltpu.CompilerParams(vmem_limit_bytes=30 * 2**20),
        cost_estimate=pl.CostEstimate(
            flops=4 * tok_rows * deep * width, bytes_accessed=4 * tok_rows * deep, transcendentals=0
        ),
    )(places, tokens, theirs, *flat, *sums)


def project(tokens, key_down, value_down, prepare, inputs):
    chips = lax.axis_size("chip")
    chip = lax.axis_index("chip")
    core = lax.axis_index("core")
    first = core == 0
    shard = key_down.shape[0]
    rows = CORES * shard
    own = jnp.where(first, key_down, value_down)
    got = lax.ppermute(jnp.where(first, value_down, key_down), "core", SWAP)
    if chips > 8:
        theirs = lax.ppermute(tokens, "core", SWAP)
        block = jnp.concatenate([jnp.where(first, own, got), jnp.where(first, got, own)], 0)
        full = lax.all_gather(block, "chip", axis=0, tiled=True)
        mine, other = mm(tokens, full).astype(BF), mm(theirs, full).astype(BF)
        return jnp.concatenate([jnp.where(first, mine, other), jnp.where(first, other, mine)], 0), prepare(*inputs)
    cycle = list(range(0, chips, 2)) + list(range(chips - 1, 0, -2))
    last = chips - 1
    place = jnp.where(chip & 1 == 0, chip >> 1, last - (chip >> 1))
    chains = 2
    piece = shard // chains
    right = [(cycle[i], cycle[(i + 1) % chips]) for i in range(chips)]
    left = [(b, a) for a, b in right]
    ways = [right] * chains + [left] * chains

    def start_of(way, step):
        spot = place - step if way == 0 else place + step
        spot = jnp.where(spot < 0, spot + chips, jnp.where(spot > last, spot - chips, spot))
        source = jnp.where(spot < chips // 2, 2 * spot, 2 * (last - spot) + 1)
        return source * rows + (core if way == 0 else 1 - core) * shard

    held = [own[k * piece : (k + 1) * piece] for k in range(chains)]
    got, tokens_later = lax.optimization_barrier((got, tokens))
    held += [got[k * piece : (k + 1) * piece] for k in range(chains)]
    theirs = lax.ppermute(tokens_later, "core", SWAP)
    todo = [(start_of(0, 0), [own]), (start_of(1, 0), [got])]
    total = None
    mark = None
    for step in range(1, chips):
        ready = todo
        if step == 2:
            held = lax.optimization_barrier(held)
        if step == last:
            _, inputs = lax.optimization_barrier((held[0], inputs))
        for k in range(2 * chains):
            if mark is not None:
                held[k], _ = lax.optimization_barrier((held[k], mark))
            held[k] = lax.ppermute(held[k], "chip", ways[k])
        arriving = [(start_of(w, step), held[w * chains : (w + 1) * chains]) for w in range(2)]
        if step == 1:
            todo = todo + arriving
        else:
            total, mark = add_pieces(tokens, theirs, ready, total)
            todo = arriving
    return add_pieces(tokens, theirs, todo, total, core)[0], prepare(*inputs)


def attend(have, got, core, key_up, value_up, query, bounds, chips):
    heads, rows = query.shape[:2]
    tokens = have.shape[0]
    pairs = rows // 8
    blocks = pairs * heads // chips
    scale = 1.0 / DH**0.5

    def kernel(core_ref, have_any, got_any, key_any, value_any, query_any, bounds_ref, out_ref, *scratch):
        latents, ups, query_ref, sems = scratch
        core = core_ref[0]
        lanes = pl.ds(pl.multiple_of(core * heads * DH, heads * DH), heads * DH)
        pairs_of = [
            (have_any, latents.at[core]),
            (got_any, latents.at[1 - core]),
            (key_any.at[:, lanes], ups.at[0]),
            (value_any.at[:, lanes], ups.at[1]),
            (query_any, query_ref),
        ]
        copies = [pltpu.make_async_copy(source, target, sems.at[k]) for k, (source, target) in enumerate(pairs_of)]
        for copy in copies:
            copy.start()
        for copy in copies:
            copy.wait()
        keys = mm(latents[0], ups[0]).astype(BF)
        values = mm(latents[1], ups[1]).astype(BF)
        position = lax.broadcasted_iota(jnp.int32, (tokens, rows), 0)
        visible = (position >= bounds_ref[0:1, :]) & (position < bounds_ref[1:2, :])
        tops, totals = [], []
        for g in range(heads):
            lanes = slice(g * DH, (g + 1) * DH)
            scores = scale * lax.dot_general(
                keys[:, lanes], query_ref[g], (((1,), (1,)), ((), ())), preferred_element_type=F32
            )
            scores = jnp.where(visible, scores, -1e30)
            top = jnp.max(scores, 0, keepdims=True)
            weights = jnp.where(visible, jnp.exp(scores - top), 0.0)
            tops.append(top)
            totals.append(jnp.sum(weights, 0, keepdims=True))
            summed = lax.dot_general(
                weights.astype(BF), values[:, lanes], (((0,), (0,)), ((), ())), preferred_element_type=F32
            )
            for pair in range(pairs):
                block = pair * heads + g
                out_ref[block // blocks, block % blocks] = summed[pair * 8 : (pair + 1) * 8]
        stats = jnp.transpose(jnp.concatenate(tops + totals, 0))
        stride = min(blocks, heads)
        for chip in range(chips):
            spots = [divmod(b, heads) for b in range(chip * blocks, (chip + 1) * blocks, stride)]
            sides = [
                stats[pair * 8 : (pair + 1) * 8, side + g : side + g + stride] for side in (0, heads) for pair, g in spots
            ]
            out_ref[chip, blocks] = jnp.zeros((8, DH), F32)
            out_ref[chip, blocks, :, : 2 * blocks] = jnp.concatenate(sides, 1)

    in_vmem = pl.BlockSpec(memory_space=pltpu.VMEM)
    return pl.pallas_call(
        kernel,
        out_shape=jax.ShapeDtypeStruct((chips, blocks + 1, 8, DH), F32),
        in_specs=[pl.BlockSpec(memory_space=pltpu.SMEM)] + [pl.BlockSpec(memory_space=pl.ANY)] * 5 + [in_vmem],
        out_specs=in_vmem,
        scratch_shapes=[
            pltpu.VMEM((2,) + have.shape, BF),
            pltpu.VMEM((2, have.shape[1], heads * DH), BF),
            pltpu.VMEM(query.shape, BF),
            pltpu.SemaphoreType.DMA((5,)),
        ],
        compiler_params=pltpu.CompilerParams(vmem_limit_bytes=24 * 2**20),
        cost_estimate=pl.CostEstimate(
            flops=4 * tokens * (have.shape[1] * heads * DH + heads * rows * DH),
            bytes_accessed=4 * tokens * have.shape[1],
            transcendentals=tokens * heads * rows,
        ),
    )(core.reshape(1), have, got, key_up, value_up, query, bounds)


def merge(arrived, fresh_stats, fresh_summed):
    chips, blocks = arrived.shape[0], arrived.shape[1] - 1

    def kernel(arrived_ref, stats_ref, summed_ref, out_ref):
        results = []
        for b in range(blocks):
            top = arrived_ref[:, blocks, :, b : b + 1]
            total = arrived_ref[:, blocks, :, blocks + b : blocks + b + 1]
            fresh_top = stats_ref[:, b : b + 1]
            overall = jnp.maximum(jnp.max(top, 0), fresh_top)
            carried = jnp.exp(top - overall[None])
            fresh_carried = jnp.exp(fresh_top - overall)
            total = jnp.sum(total * carried, 0) + stats_ref[:, blocks + b : blocks + b + 1] * fresh_carried
            summed = jnp.sum(arrived_ref[:, b] * carried, 0) + summed_ref[b * 8 : (b + 1) * 8, :] * fresh_carried
            results.append(summed / total)
        out_ref[...] = jnp.concatenate(results, 0).astype(BF)

    in_vmem = pl.BlockSpec(memory_space=pltpu.VMEM)
    return pl.pallas_call(
        kernel,
        out_shape=jax.ShapeDtypeStruct((blocks * 8, DH), BF),
        in_specs=[in_vmem] * 3,
        out_specs=in_vmem,
        compiler_params=pltpu.CompilerParams(vmem_limit_bytes=8 * 2**20),
        cost_estimate=pl.CostEstimate(
            flops=2 * chips * blocks * 8 * DH, bytes_accessed=4 * arrived.size, transcendentals=chips * blocks * 8
        ),
    )(arrived, fresh_stats, fresh_summed)


def on_device(tokens, key_down, value_down, key_up, value_up, prompt_lens, queries, new_latent):
    chips = lax.axis_size("chip")
    chip = lax.axis_index("chip")
    core = lax.axis_index("core")
    first = core == 0
    tok_rows = tokens.shape[0]
    lat_width = key_down.shape[1]
    group = QH // KVH
    heads = KVH // CORES
    scale = 1.0 / DH**0.5
    steps_count, req_count = (queries.shape[0], queries.shape[1])
    pairs = steps_count * req_count
    rows = pairs * heads * group
    share = rows // chips

    def by_head(queries):
        mine = lax.dynamic_slice_in_dim(queries, core * heads * group * DH, heads * group * DH, 2)
        return mine.reshape(steps_count, req_count, heads, group, DH).transpose(2, 0, 1, 3, 4)

    have, query = project(tokens, key_down, value_down, by_head, (queries,))
    got = lax.ppermute(have, "core", SWAP)

    offsets = jnp.cumsum(prompt_lens) - prompt_lens
    bounds = jnp.stack([offsets, offsets + prompt_lens]) - chip * CORES * tok_rows
    bounds = jnp.broadcast_to(bounds[:, None, :, None], (2, steps_count, req_count, group)).reshape(2, -1)
    sending = attend(have, got, core, key_up, value_up, query.reshape(heads, -1, DH), bounds, chips)

    sending, query, new_latent = lax.optimization_barrier((sending, query, new_latent))
    flat_new = new_latent.reshape(pairs, 2 * lat_width)

    def my_heads(latent, up):
        full = lax.dynamic_slice_in_dim(mm(latent, up), core * heads * DH, heads * DH, 1)
        return full.astype(BF).reshape(steps_count, req_count, heads, DH)

    new_keys = my_heads(flat_new[:, :lat_width], key_up)
    new_values = my_heads(flat_new[:, lat_width:], value_up)
    causal = (jnp.arange(steps_count)[:, None] >= jnp.arange(steps_count)[None, :])[:, None, None, None, :]
    fresh = jnp.einsum("gsrjd,urgd->srgju", query, new_keys, preferred_element_type=F32) * scale
    fresh = jnp.where(causal, fresh, -1e30)
    fresh_top = jnp.max(fresh, -1)
    fresh_weights = jnp.where(causal, jnp.exp(fresh - fresh_top[..., None]), 0.0)
    fresh_total = jnp.sum(fresh_weights, -1)
    fresh_summed = jnp.einsum("srgju,urgd->srgjd", fresh_weights.astype(BF), new_values, preferred_element_type=F32)

    def my_share(x):
        return lax.dynamic_slice_in_dim(x, chip * share, share, 0)

    fresh_summed = my_share(fresh_summed.reshape(rows, DH))
    fresh_stats = [my_share(x.reshape(rows)).reshape(-1, group).T for x in (fresh_top, fresh_total)]
    fresh_stats = jnp.pad(jnp.concatenate(fresh_stats, 1), ((0, 0), (0, DH - 2 * share // group)))

    flat = sending.reshape(chips, -1, DH)
    arrived = lax.all_to_all(flat, "chip", split_axis=0, concat_axis=0, tiled=True).reshape(sending.shape)
    result = merge(arrived, fresh_stats, fresh_summed)

    if chips == 8:
        near = lax.ppermute(result, "chip", [(c, c ^ 1) for c in range(chips)])
        upper = chip & 1 == 1
        couple = jnp.concatenate([jnp.where(upper, near, result), jnp.where(upper, result, near)], 0)
        far = [couple] + [lax.ppermute(couple, "chip", [(c, c ^ (2 * d)) for c in range(chips)]) for d in range(1, 4)]
        odd, high = chip & 2 != 0, chip & 4 != 0

        def of(z):
            return jnp.where(high, jnp.where(odd, far[z ^ 3], far[z ^ 2]), jnp.where(odd, far[z ^ 1], far[z]))

        whole = jnp.concatenate([of(z) for z in range(4)], 0)
    else:
        whole = lax.all_gather(result, "chip", axis=0, tiled=True)
    whole = whole.reshape(pairs, 1, rows // pairs * DH)
    away = lax.ppermute(whole, "core", SWAP)
    whole = jnp.concatenate([jnp.where(first, whole, away), jnp.where(first, away, whole)], 1)
    return whole.reshape(steps_count, req_count, QH * DH)


def solution(mesh):
    groups, n_ctx = mesh.shape["groups"], mesh.shape["ctx"]
    split = Mesh(mesh.devices.reshape(groups, n_ctx // CORES, CORES), ("groups", "chip", "core"))
    ctx = ("chip", "core")
    return jax.shard_map(
        on_device,
        mesh=split,
        in_specs=(
            P(("groups",) + ctx, None),
            P(ctx, None),
            P(ctx, None),
            P(),
            P(),
            P("groups"),
            P(None, "groups", None),
            P(None, "groups", None),
        ),
        out_specs=P(None, "groups", None),
        check_vma=False,
    )
```

```python
import jax
import jax.numpy as jnp
from jax import lax
from jax.experimental import pallas as pl
from jax.experimental.pallas import tpu as pltpu
from jax.sharding import Mesh, PartitionSpec as P

QH = 64
KVH = 8
DH = 128
CORES = 2
BF = jnp.bfloat16
F32 = jnp.float32
SWAP = [(0, 1), (1, 0)]


def mm(a, b):
    return jnp.dot(a, b, preferred_element_type=F32)


def add_pieces(tokens, theirs, groups, total, core=None):
    tok_rows = tokens.shape[0]
    width = groups[0][1][0].shape[1]
    depths = [[part.shape[0] for part in parts] for _, parts in groups]
    span = sum(depths[0])
    deep = span * len(groups)
    flat = [part for _, parts in groups for part in parts]
    count = len(flat)
    last = core is not None
    places = jnp.stack([start for start, _ in groups] + ([core * tok_rows, (1 - core) * tok_rows] if last else []))

    def kernel(places_ref, mine_ref, theirs_ref, *refs):
        parts = refs[:count]
        total_ref, out_ref, mark_ref, columns, weights, sems, loaded = (
            refs[count:] if total is not None else (None,) + refs[count:]
        )
        copies = []
        for j, source in enumerate((mine_ref, theirs_ref)):
            for g in range(len(groups)):
                start = pl.multiple_of(places_ref[g], 128)
                copy = pltpu.make_async_copy(
                    source.at[:, pl.ds(start, span)], columns.at[j, :, pl.ds(g * span, span)], sems.at[j, g]
                )
                copy.start()
                copies.append(copy)
        at = 0
        loads = []
        for k, part in enumerate(parts):
            load = pltpu.make_async_copy(part, weights.at[pl.ds(at, part.shape[0])], loaded.at[k])
            load.start()
            loads.append(load)
            at += part.shape[0]
        mark_ref[...] = jnp.zeros_like(mark_ref)
        for load in loads:
            load.wait()
        for j in range(2):
            for g in range(len(groups)):
                copies[j * len(groups) + g].wait()
            rows = pl.ds(j * tok_rows, tok_rows)
            term = mm(columns[j], weights[...])
            if total is not None:
                term = total_ref[rows, :] + term
            if last:
                rows = pl.ds(pl.multiple_of(places_ref[len(groups) + j], tok_rows), tok_rows)
            out_ref[rows, :] = term.astype(out_ref.dtype)

    tokens = pltpu.with_memory_space_constraint(tokens, pltpu.HBM)
    in_vmem = pl.BlockSpec(memory_space=pltpu.VMEM)
    in_any = pl.BlockSpec(memory_space=pl.ANY)
    sums = [] if total is None else [total]
    return pl.pallas_call(
        kernel,
        out_shape=(
            jax.ShapeDtypeStruct((2 * tok_rows, width), BF if last else F32),
            jax.ShapeDtypeStruct((8, 128), F32),
        ),
        in_specs=[pl.BlockSpec(memory_space=pltpu.SMEM)] + [in_any] * (2 + count) + [in_vmem] * len(sums),
        out_specs=(in_vmem, in_vmem),
        scratch_shapes=[
            pltpu.VMEM((2, tok_rows, deep), BF),
            pltpu.VMEM((deep, width), BF),
            pltpu.SemaphoreType.DMA((2, len(groups))),
            pltpu.SemaphoreType.DMA((count,)),
        ],
        input_output_aliases={} if total is None or last else {3 + count: 0},
        compiler_params=pltpu.CompilerParams(vmem_limit_bytes=20 * 2**20),
        cost_estimate=pl.CostEstimate(
            flops=4 * tok_rows * deep * width, bytes_accessed=4 * tok_rows * deep, transcendentals=0
        ),
    )(places, tokens, theirs, *flat, *sums)


def project(tokens, key_down, value_down, prepare, inputs):
    chips = lax.axis_size("chip")
    chip = lax.axis_index("chip")
    core = lax.axis_index("core")
    first = core == 0
    shard = key_down.shape[0]
    rows = CORES * shard
    own = jnp.where(first, key_down, value_down)
    got = lax.ppermute(jnp.where(first, value_down, key_down), "core", SWAP)
    if chips > 8:
        theirs = lax.ppermute(tokens, "core", SWAP)
        block = jnp.concatenate([jnp.where(first, own, got), jnp.where(first, got, own)], 0)
        full = lax.all_gather(block, "chip", axis=0, tiled=True)
        mine, other = mm(tokens, full).astype(BF), mm(theirs, full).astype(BF)
        return jnp.concatenate([jnp.where(first, mine, other), jnp.where(first, other, mine)], 0), prepare(*inputs)
    cycle = list(range(0, chips, 2)) + list(range(chips - 1, 0, -2))
    last = chips - 1
    place = jnp.where(chip & 1 == 0, chip >> 1, last - (chip >> 1))
    chains = 2
    piece = shard // chains
    right = [(cycle[i], cycle[(i + 1) % chips]) for i in range(chips)]
    left = [(b, a) for a, b in right]
    ways = [right] * chains + [left] * chains

    def start_of(way, step):
        spot = place - step if way == 0 else place + step
        spot = jnp.where(spot < 0, spot + chips, jnp.where(spot > last, spot - chips, spot))
        source = jnp.where(spot < chips // 2, 2 * spot, 2 * (last - spot) + 1)
        return source * rows + (core if way == 0 else 1 - core) * shard

    held = [own[k * piece : (k + 1) * piece] for k in range(chains)]
    got, tokens_later = lax.optimization_barrier((got, tokens))
    held += [got[k * piece : (k + 1) * piece] for k in range(chains)]
    theirs = lax.ppermute(tokens_later, "core", SWAP)
    todo = [(start_of(0, 0), [own]), (start_of(1, 0), [got])]
    total = None
    mark = None
    for step in range(1, chips):
        ready = todo
        if step == 2:
            held = lax.optimization_barrier(held)
        if step == last:
            _, inputs = lax.optimization_barrier((held[0], inputs))
        for k in range(2 * chains):
            if mark is not None:
                held[k], _ = lax.optimization_barrier((held[k], mark))
            held[k] = lax.ppermute(held[k], "chip", ways[k])
        arriving = [(start_of(w, step), held[w * chains : (w + 1) * chains]) for w in range(2)]
        if step == 1:
            todo = todo + arriving
        else:
            total, mark = add_pieces(tokens, theirs, ready, total)
            todo = arriving
    return add_pieces(tokens, theirs, todo, total, core)[0], prepare(*inputs)


def attend(have, got, core, key_up, value_up, query, bounds, chips):
    heads, rows = query.shape[:2]
    tokens = have.shape[0]
    pairs = rows // 8
    blocks = pairs * heads // chips
    scale = 1.0 / DH**0.5

    def kernel(core_ref, have_any, got_any, key_any, value_any, query_any, bounds_ref, out_ref, *scratch):
        latents, ups, query_ref, sems = scratch
        core = core_ref[0]
        lanes = pl.ds(pl.multiple_of(core * heads * DH, heads * DH), heads * DH)
        pairs_of = [
            (have_any, latents.at[core]),
            (got_any, latents.at[1 - core]),
            (key_any.at[:, lanes], ups.at[0]),
            (value_any.at[:, lanes], ups.at[1]),
            (query_any, query_ref),
        ]
        copies = [pltpu.make_async_copy(source, target, sems.at[k]) for k, (source, target) in enumerate(pairs_of)]
        for copy in copies:
            copy.start()
        for copy in copies[:3]:
            copy.wait()
        keys = mm(latents[0], ups[0]).astype(BF)
        for copy in copies[3:]:
            copy.wait()
        values = mm(latents[1], ups[1]).astype(BF)
        position = lax.broadcasted_iota(jnp.int32, (tokens, rows), 0)
        visible = (position >= bounds_ref[0:1, :]) & (position < bounds_ref[1:2, :])
        tops, totals = [], []
        for g in range(heads):
            lanes = slice(g * DH, (g + 1) * DH)
            scores = scale * lax.dot_general(
                keys[:, lanes], query_ref[g], (((1,), (1,)), ((), ())), preferred_element_type=F32
            )
            scores = jnp.where(visible, scores, -1e30)
            top = jnp.max(scores, 0, keepdims=True)
            weights = jnp.where(visible, jnp.exp(scores - top), 0.0)
            tops.append(top)
            totals.append(jnp.sum(weights, 0, keepdims=True))
            summed = lax.dot_general(
                weights.astype(BF), values[:, lanes], (((0,), (0,)), ((), ())), preferred_element_type=F32
            )
            for pair in range(pairs):
                block = pair * heads + g
                out_ref[block // blocks, block % blocks] = summed[pair * 8 : (pair + 1) * 8]
        stats = jnp.transpose(jnp.concatenate(tops + totals, 0))
        stride = min(blocks, heads)
        for chip in range(chips):
            spots = [divmod(b, heads) for b in range(chip * blocks, (chip + 1) * blocks, stride)]
            sides = [
                stats[pair * 8 : (pair + 1) * 8, side + g : side + g + stride] for side in (0, heads) for pair, g in spots
            ]
            out_ref[chip, blocks] = jnp.zeros((8, DH), F32)
            out_ref[chip, blocks, :, : 2 * blocks] = jnp.concatenate(sides, 1)

    ups = [pltpu.with_memory_space_constraint(x, pltpu.HBM) for x in (key_up, value_up)]
    in_vmem = pl.BlockSpec(memory_space=pltpu.VMEM)
    return pl.pallas_call(
        kernel,
        out_shape=jax.ShapeDtypeStruct((chips, blocks + 1, 8, DH), F32),
        in_specs=[pl.BlockSpec(memory_space=pltpu.SMEM)] + [pl.BlockSpec(memory_space=pl.ANY)] * 5 + [in_vmem],
        out_specs=in_vmem,
        scratch_shapes=[
            pltpu.VMEM((2,) + have.shape, BF),
            pltpu.VMEM((2, have.shape[1], heads * DH), BF),
            pltpu.VMEM(query.shape, BF),
            pltpu.SemaphoreType.DMA((5,)),
        ],
        compiler_params=pltpu.CompilerParams(vmem_limit_bytes=16 * 2**20),
        cost_estimate=pl.CostEstimate(
            flops=4 * tokens * (have.shape[1] * heads * DH + heads * rows * DH),
            bytes_accessed=4 * tokens * have.shape[1],
            transcendentals=tokens * heads * rows,
        ),
    )(core.reshape(1), have, got, *ups, query, bounds)


def merge(arrived, fresh_stats, fresh_summed):
    chips, blocks = arrived.shape[0], arrived.shape[1] - 1

    def kernel(arrived_ref, stats_ref, summed_ref, out_ref):
        results = []
        for b in range(blocks):
            top = arrived_ref[:, blocks, :, b : b + 1]
            total = arrived_ref[:, blocks, :, blocks + b : blocks + b + 1]
            fresh_top = stats_ref[:, b : b + 1]
            overall = jnp.maximum(jnp.max(top, 0), fresh_top)
            carried = jnp.exp(top - overall[None])
            fresh_carried = jnp.exp(fresh_top - overall)
            total = jnp.sum(total * carried, 0) + stats_ref[:, blocks + b : blocks + b + 1] * fresh_carried
            summed = jnp.sum(arrived_ref[:, b] * carried, 0) + summed_ref[b * 8 : (b + 1) * 8, :] * fresh_carried
            results.append(summed / total)
        out_ref[...] = jnp.concatenate(results, 0).astype(BF)

    in_vmem = pl.BlockSpec(memory_space=pltpu.VMEM)
    return pl.pallas_call(
        kernel,
        out_shape=jax.ShapeDtypeStruct((blocks * 8, DH), BF),
        in_specs=[in_vmem] * 3,
        out_specs=in_vmem,
        compiler_params=pltpu.CompilerParams(vmem_limit_bytes=8 * 2**20),
        cost_estimate=pl.CostEstimate(
            flops=2 * chips * blocks * 8 * DH, bytes_accessed=4 * arrived.size, transcendentals=chips * blocks * 8
        ),
    )(arrived, fresh_stats, fresh_summed)


def on_device(tokens, key_down, value_down, key_up, value_up, prompt_lens, queries, new_latent):
    chips = lax.axis_size("chip")
    chip = lax.axis_index("chip")
    core = lax.axis_index("core")
    first = core == 0
    tok_rows = tokens.shape[0]
    lat_width = key_down.shape[1]
    group = QH // KVH
    heads = KVH // CORES
    scale = 1.0 / DH**0.5
    steps_count, req_count = (queries.shape[0], queries.shape[1])
    pairs = steps_count * req_count
    rows = pairs * heads * group
    share = rows // chips

    def by_head(queries):
        mine = lax.dynamic_slice_in_dim(queries, core * heads * group * DH, heads * group * DH, 2)
        return mine.reshape(steps_count, req_count, heads, group, DH).transpose(2, 0, 1, 3, 4)

    have, query = project(tokens, key_down, value_down, by_head, (queries,))
    got = lax.ppermute(have, "core", SWAP)

    offsets = jnp.cumsum(prompt_lens) - prompt_lens
    bounds = jnp.stack([offsets, offsets + prompt_lens]) - chip * CORES * tok_rows
    bounds = jnp.broadcast_to(bounds[:, None, :, None], (2, steps_count, req_count, group)).reshape(2, -1)
    sending = attend(have, got, core, key_up, value_up, query.reshape(heads, -1, DH), bounds, chips)

    sending, query, new_latent = lax.optimization_barrier((sending, query, new_latent))
    flat_new = new_latent.reshape(pairs, 2 * lat_width)

    def my_heads(latent, up):
        full = lax.dynamic_slice_in_dim(mm(latent, up), core * heads * DH, heads * DH, 1)
        return full.astype(BF).reshape(steps_count, req_count, heads, DH)

    new_keys = my_heads(flat_new[:, :lat_width], key_up)
    new_values = my_heads(flat_new[:, lat_width:], value_up)
    causal = (jnp.arange(steps_count)[:, None] >= jnp.arange(steps_count)[None, :])[:, None, None, None, :]
    fresh = jnp.einsum("gsrjd,urgd->srgju", query, new_keys, preferred_element_type=F32) * scale
    fresh = jnp.where(causal, fresh, -1e30)
    fresh_top = jnp.max(fresh, -1)
    fresh_weights = jnp.where(causal, jnp.exp(fresh - fresh_top[..., None]), 0.0)
    fresh_total = jnp.sum(fresh_weights, -1)
    fresh_summed = jnp.einsum("srgju,urgd->srgjd", fresh_weights.astype(BF), new_values, preferred_element_type=F32)

    def my_share(x):
        return lax.dynamic_slice_in_dim(x, chip * share, share, 0)

    fresh_summed = my_share(fresh_summed.reshape(rows, DH))
    fresh_stats = [my_share(x.reshape(rows)).reshape(-1, group).T for x in (fresh_top, fresh_total)]
    fresh_stats = jnp.pad(jnp.concatenate(fresh_stats, 1), ((0, 0), (0, DH - 2 * share // group)))

    flat = sending.reshape(chips, -1, DH)
    arrived = lax.all_to_all(flat, "chip", split_axis=0, concat_axis=0, tiled=True).reshape(sending.shape)
    result = merge(arrived, fresh_stats, fresh_summed)

    if chips == 8:
        near = lax.ppermute(result, "chip", [(c, c ^ 1) for c in range(chips)])
        upper = chip & 1 == 1
        couple = jnp.concatenate([jnp.where(upper, near, result), jnp.where(upper, result, near)], 0)
        far = [couple] + [lax.ppermute(couple, "chip", [(c, c ^ (2 * d)) for c in range(chips)]) for d in range(1, 4)]
        odd, high = chip & 2 != 0, chip & 4 != 0

        def of(z):
            return jnp.where(high, jnp.where(odd, far[z ^ 3], far[z ^ 2]), jnp.where(odd, far[z ^ 1], far[z]))

        whole = jnp.concatenate([of(z) for z in range(4)], 0)
    else:
        whole = lax.all_gather(result, "chip", axis=0, tiled=True)
    whole = whole.reshape(pairs, 1, rows // pairs * DH)
    away = lax.ppermute(whole, "core", SWAP)
    whole = jnp.concatenate([jnp.where(first, whole, away), jnp.where(first, away, whole)], 1)
    return whole.reshape(steps_count, req_count, QH * DH)


def solution(mesh):
    groups, n_ctx = mesh.shape["groups"], mesh.shape["ctx"]
    split = Mesh(mesh.devices.reshape(groups, n_ctx // CORES, CORES), ("groups", "chip", "core"))
    ctx = ("chip", "core")
    return jax.shard_map(
        on_device,
        mesh=split,
        in_specs=(
            P(("groups",) + ctx, None),
            P(ctx, None),
            P(ctx, None),
            P(),
            P(),
            P("groups"),
            P(None, "groups", None),
            P(None, "groups", None),
        ),
        out_specs=P(None, "groups", None),
        check_vma=False,
    )
```

```python
import jax
import jax.numpy as jnp
from jax import lax
from jax.experimental import pallas as pl
from jax.experimental.pallas import tpu as pltpu
from jax.sharding import Mesh, PartitionSpec as P

QH = 64
KVH = 8
DH = 128
CORES = 2
BF = jnp.bfloat16
F32 = jnp.float32
SWAP = [(0, 1), (1, 0)]


def mm(a, b):
    return jnp.dot(a, b, preferred_element_type=F32)


def add_pieces(tokens, theirs, halves, total, part, core=None):
    tok_rows = tokens.shape[0]
    span, width = tokens.shape[1] // lax.axis_size("chip") // CORES, halves[0][1].shape[1]
    deep = span * len(halves)
    flat = [x for half in halves for x in half[1:4]]
    count = len(flat)
    last = core is not None
    places = jnp.stack([half[0] for half in halves] + [part] + ([core, 1 - core] if last else []))

    def kernel(places_ref, mine_ref, theirs_ref, *refs):
        parts = list(refs[:count])
        total_ref, out_ref, mark_ref, columns, weights, sems, loaded = (
            refs[count:] if total is not None else (None,) + refs[count:]
        )
        copies = []
        for j, source in enumerate((mine_ref, theirs_ref)):
            for h in range(len(halves)):
                start = pl.multiple_of(places_ref[h], 128)
                copy = pltpu.make_async_copy(
                    source.at[:, pl.ds(start, span)], columns.at[j, :, pl.ds(h * span, span)], sems.at[j, h]
                )
                copy.start()
                copies.append(copy)
        loads = []

        def load(source, place):
            copy = pltpu.make_async_copy(source, weights.at[pl.ds(place, source.shape[0])], loaded.at[len(loads)])
            copy.start()
            loads.append(copy)

        turn = places_ref[len(halves)]
        for h, half in enumerate(halves):
            shared = half[1].shape[0]
            load(parts.pop(0), h * span)
            if len(half) > 2:
                rest = half[2].shape[0]
                first = h * span + shared
                load(parts.pop(0), pl.multiple_of(first + turn * rest, rest))
                load(parts.pop(0).at[pl.ds(half[4] * rest, rest)], pl.multiple_of(first + (1 - turn) * rest, rest))
        mark_ref[...] = jnp.zeros_like(mark_ref)
        for copy in loads:
            copy.wait()
        for j in range(2):
            for h in range(len(halves)):
                copies[j * len(halves) + h].wait()
            rows = pl.ds(j * tok_rows, tok_rows)
            term = mm(columns[j], weights[...])
            if total is not None:
                term = total_ref[rows, :] + term
            if last:
                rows = pl.ds(pl.multiple_of(places_ref[len(halves) + 1 + j] * tok_rows, tok_rows), tok_rows)
            out_ref[rows, :] = term.astype(out_ref.dtype)

    tokens = pltpu.with_memory_space_constraint(tokens, pltpu.HBM)
    in_vmem = pl.BlockSpec(memory_space=pltpu.VMEM)
    in_any = pl.BlockSpec(memory_space=pl.ANY)
    sums = [] if total is None else [total]
    return pl.pallas_call(
        kernel,
        out_shape=(
            jax.ShapeDtypeStruct((2 * tok_rows, width), BF if last else F32),
            jax.ShapeDtypeStruct((8, 128), F32),
        ),
        in_specs=[pl.BlockSpec(memory_space=pltpu.SMEM)] + [in_any] * (2 + count) + [in_vmem] * len(sums),
        out_specs=(in_vmem, in_vmem),
        scratch_shapes=[
            pltpu.VMEM((2, tok_rows, deep), BF),
            pltpu.VMEM((deep, width), BF),
            pltpu.SemaphoreType.DMA((2, len(halves))),
            pltpu.SemaphoreType.DMA((count,)),
        ],
        input_output_aliases={} if total is None or last else {3 + count: 0},
        compiler_params=pltpu.CompilerParams(vmem_limit_bytes=20 * 2**20),
        cost_estimate=pl.CostEstimate(
            flops=4 * tok_rows * deep * width, bytes_accessed=4 * tok_rows * deep, transcendentals=0
        ),
    )(places, tokens, theirs, *flat, *sums)


def project(tokens, key_down, value_down, prepare, inputs):
    chips = lax.axis_size("chip")
    chip = lax.axis_index("chip")
    core = lax.axis_index("core")
    part = lax.axis_index("groups")
    first = core == 0
    shard = key_down.shape[0]
    rows = CORES * shard
    own = jnp.where(first, key_down, value_down)
    got = lax.ppermute(jnp.where(first, value_down, key_down), "core", SWAP)
    if chips != 8 or lax.axis_size("groups") != 2:
        theirs = lax.ppermute(tokens, "core", SWAP)
        block = jnp.concatenate([jnp.where(first, own, got), jnp.where(first, got, own)], 0)
        full = lax.all_gather(block, "chip", axis=0, tiled=True)
        mine, other = mm(tokens, full).astype(BF), mm(theirs, full).astype(BF)
        return jnp.concatenate([jnp.where(first, mine, other), jnp.where(first, other, mine)], 0), prepare(*inputs)
    cycle = list(range(0, chips, 2)) + list(range(chips - 1, 0, -2))
    last = chips - 1
    place = jnp.where(chip & 1 == 0, chip >> 1, last - (chip >> 1))
    right = [(cycle[i], cycle[(i + 1) % chips]) for i in range(chips)]
    ways = (right, [(b, a) for a, b in right])

    def start_of(way, step):
        spot = place - step if way == 0 else place + step
        spot = jnp.where(spot < 0, spot + chips, jnp.where(spot > last, spot - chips, spot))
        source = jnp.where(spot < chips // 2, 2 * spot, 2 * (last - spot) + 1)
        return source * rows + (core if way == 0 else 1 - core) * shard

    rest = shard // 4
    shared = shard - 2 * rest

    def turns(half):
        return jnp.where(part == 0, half[shared : shared + rest], half[shared + rest :])

    both, single = [own[:shared]], [turns(own)]
    got, tokens_later = lax.optimization_barrier((got, tokens))
    both.append(got[:shared])
    single.append(turns(got))
    theirs = lax.ppermute(tokens_later, "core", SWAP)
    todo = [(start_of(0, 0), own), (start_of(1, 0), got)]
    calls = {3: 4, 4: 2, 5: 2, 6: 2, 7: 2}
    total = mark = crossed = None
    for step in range(1, chips):
        if step == 2:
            both, single = lax.optimization_barrier((both, single))
        if step == last:
            _, inputs = lax.optimization_barrier((both[0], inputs))
        if mark is not None:
            both = [lax.optimization_barrier((x, mark))[0] for x in both]
            single = [lax.optimization_barrier((x, mark))[0] for x in single]
            mark = None
        passed = single
        both = [lax.ppermute(x, "chip", way) for x, way in zip(both, ways)]
        single = [lax.ppermute(x, "chip", way) for x, way in zip(single, ways)]
        if step > 1:
            crossed = lax.ppermute(jnp.concatenate(passed, 0), "groups", SWAP)
            todo += [(start_of(w, step - 1), before[w], passed[w], crossed, w) for w in range(2)]
        before = both
        if step in calls:
            ready, todo = todo[: calls[step]], todo[calls[step] :]
            total, mark = add_pieces(tokens, theirs, ready, total, part)
    crossed, _ = lax.optimization_barrier((crossed, mark))
    others = [lax.ppermute(crossed[w * rest : (w + 1) * rest], "chip", ways[w]) for w in range(2)]
    total, _ = add_pieces(tokens, theirs, todo, total, part)
    final = [(start_of(w, last), both[w], single[w], others[w], 0) for w in range(2)]
    return add_pieces(tokens, theirs, final, total, part, core)[0], prepare(*inputs)


def attend(have, got, core, key_up, value_up, query, bounds, chips):
    heads, rows = query.shape[:2]
    tokens = have.shape[0]
    pairs = rows // 8
    blocks = pairs * heads // chips
    scale = 1.0 / DH**0.5

    def kernel(core_ref, have_any, got_any, key_any, value_any, query_any, bounds_ref, out_ref, *scratch):
        latents, ups, query_ref, sems = scratch
        core = core_ref[0]
        lanes = pl.ds(pl.multiple_of(core * heads * DH, heads * DH), heads * DH)
        pairs_of = [
            (have_any, latents.at[core]),
            (got_any, latents.at[1 - core]),
            (key_any.at[:, lanes], ups.at[0]),
            (value_any.at[:, lanes], ups.at[1]),
            (query_any, query_ref),
        ]
        copies = [pltpu.make_async_copy(source, target, sems.at[k]) for k, (source, target) in enumerate(pairs_of)]
        for copy in copies:
            copy.start()
        for copy in copies[:3]:
            copy.wait()
        keys = mm(latents[0], ups[0]).astype(BF)
        for copy in copies[3:]:
            copy.wait()
        values = mm(latents[1], ups[1]).astype(BF)
        position = lax.broadcasted_iota(jnp.int32, (tokens, rows), 0)
        visible = (position >= bounds_ref[0:1, :]) & (position < bounds_ref[1:2, :])
        tops, totals = [], []
        for g in range(heads):
            lanes = slice(g * DH, (g + 1) * DH)
            scores = scale * lax.dot_general(
                keys[:, lanes], query_ref[g], (((1,), (1,)), ((), ())), preferred_element_type=F32
            )
            scores = jnp.where(visible, scores, -1e30)
            top = jnp.max(scores, 0, keepdims=True)
            weights = jnp.where(visible, jnp.exp(scores - top), 0.0)
            tops.append(top)
            totals.append(jnp.sum(weights, 0, keepdims=True))
            summed = lax.dot_general(
                weights.astype(BF), values[:, lanes], (((0,), (0,)), ((), ())), preferred_element_type=F32
            )
            for pair in range(pairs):
                block = pair * heads + g
                out_ref[block // blocks, block % blocks] = summed[pair * 8 : (pair + 1) * 8]
        stats = jnp.transpose(jnp.concatenate(tops + totals, 0))
        stride = min(blocks, heads)
        for chip in range(chips):
            spots = [divmod(b, heads) for b in range(chip * blocks, (chip + 1) * blocks, stride)]
            sides = [
                stats[pair * 8 : (pair + 1) * 8, side + g : side + g + stride] for side in (0, heads) for pair, g in spots
            ]
            out_ref[chip, blocks] = jnp.zeros((8, DH), F32)
            out_ref[chip, blocks, :, : 2 * blocks] = jnp.concatenate(sides, 1)

    ups = [pltpu.with_memory_space_constraint(x, pltpu.HBM) for x in (key_up, value_up)]
    in_vmem = pl.BlockSpec(memory_space=pltpu.VMEM)
    return pl.pallas_call(
        kernel,
        out_shape=jax.ShapeDtypeStruct((chips, blocks + 1, 8, DH), F32),
        in_specs=[pl.BlockSpec(memory_space=pltpu.SMEM)] + [pl.BlockSpec(memory_space=pl.ANY)] * 5 + [in_vmem],
        out_specs=in_vmem,
        scratch_shapes=[
            pltpu.VMEM((2,) + have.shape, BF),
            pltpu.VMEM((2, have.shape[1], heads * DH), BF),
            pltpu.VMEM(query.shape, BF),
            pltpu.SemaphoreType.DMA((5,)),
        ],
        compiler_params=pltpu.CompilerParams(vmem_limit_bytes=16 * 2**20),
        cost_estimate=pl.CostEstimate(
            flops=4 * tokens * (have.shape[1] * heads * DH + heads * rows * DH),
            bytes_accessed=4 * tokens * have.shape[1],
            transcendentals=tokens * heads * rows,
        ),
    )(core.reshape(1), have, got, *ups, query, bounds)


def merge(arrived, fresh_stats, fresh_summed):
    chips, blocks = arrived.shape[0], arrived.shape[1] - 1

    def kernel(arrived_ref, stats_ref, summed_ref, out_ref):
        results = []
        for b in range(blocks):
            top = arrived_ref[:, blocks, :, b : b + 1]
            total = arrived_ref[:, blocks, :, blocks + b : blocks + b + 1]
            fresh_top = stats_ref[:, b : b + 1]
            overall = jnp.maximum(jnp.max(top, 0), fresh_top)
            carried = jnp.exp(top - overall[None])
            fresh_carried = jnp.exp(fresh_top - overall)
            total = jnp.sum(total * carried, 0) + stats_ref[:, blocks + b : blocks + b + 1] * fresh_carried
            summed = jnp.sum(arrived_ref[:, b] * carried, 0) + summed_ref[b * 8 : (b + 1) * 8, :] * fresh_carried
            results.append(summed / total)
        out_ref[...] = jnp.concatenate(results, 0).astype(BF)

    in_vmem = pl.BlockSpec(memory_space=pltpu.VMEM)
    return pl.pallas_call(
        kernel,
        out_shape=jax.ShapeDtypeStruct((blocks * 8, DH), BF),
        in_specs=[in_vmem] * 3,
        out_specs=in_vmem,
        compiler_params=pltpu.CompilerParams(vmem_limit_bytes=8 * 2**20),
        cost_estimate=pl.CostEstimate(
            flops=2 * chips * blocks * 8 * DH, bytes_accessed=4 * arrived.size, transcendentals=chips * blocks * 8
        ),
    )(arrived, fresh_stats, fresh_summed)


def on_device(tokens, key_down, value_down, key_up, value_up, prompt_lens, queries, new_latent):
    chips = lax.axis_size("chip")
    chip = lax.axis_index("chip")
    core = lax.axis_index("core")
    first = core == 0
    tok_rows = tokens.shape[0]
    lat_width = key_down.shape[1]
    group = QH // KVH
    heads = KVH // CORES
    scale = 1.0 / DH**0.5
    steps_count, req_count = (queries.shape[0], queries.shape[1])
    pairs = steps_count * req_count
    rows = pairs * heads * group
    share = rows // chips

    def by_head(queries):
        mine = lax.dynamic_slice_in_dim(queries, core * heads * group * DH, heads * group * DH, 2)
        return mine.reshape(steps_count, req_count, heads, group, DH).transpose(2, 0, 1, 3, 4)

    have, query = project(tokens, key_down, value_down, by_head, (queries,))
    got = lax.ppermute(have, "core", SWAP)

    offsets = jnp.cumsum(prompt_lens) - prompt_lens
    bounds = jnp.stack([offsets, offsets + prompt_lens]) - chip * CORES * tok_rows
    bounds = jnp.broadcast_to(bounds[:, None, :, None], (2, steps_count, req_count, group)).reshape(2, -1)
    sending = attend(have, got, core, key_up, value_up, query.reshape(heads, -1, DH), bounds, chips)

    sending, query, new_latent = lax.optimization_barrier((sending, query, new_latent))
    flat_new = new_latent.reshape(pairs, 2 * lat_width)

    def my_heads(latent, up):
        full = lax.dynamic_slice_in_dim(mm(latent, up), core * heads * DH, heads * DH, 1)
        return full.astype(BF).reshape(steps_count, req_count, heads, DH)

    new_keys = my_heads(flat_new[:, :lat_width], key_up)
    new_values = my_heads(flat_new[:, lat_width:], value_up)
    causal = (jnp.arange(steps_count)[:, None] >= jnp.arange(steps_count)[None, :])[:, None, None, None, :]
    fresh = jnp.einsum("gsrjd,urgd->srgju", query, new_keys, preferred_element_type=F32) * scale
    fresh = jnp.where(causal, fresh, -1e30)
    fresh_top = jnp.max(fresh, -1)
    fresh_weights = jnp.where(causal, jnp.exp(fresh - fresh_top[..., None]), 0.0)
    fresh_total = jnp.sum(fresh_weights, -1)
    fresh_summed = jnp.einsum("srgju,urgd->srgjd", fresh_weights.astype(BF), new_values, preferred_element_type=F32)

    def my_share(x):
        return lax.dynamic_slice_in_dim(x, chip * share, share, 0)

    fresh_summed = my_share(fresh_summed.reshape(rows, DH))
    fresh_stats = [my_share(x.reshape(rows)).reshape(-1, group).T for x in (fresh_top, fresh_total)]
    fresh_stats = jnp.pad(jnp.concatenate(fresh_stats, 1), ((0, 0), (0, DH - 2 * share // group)))

    flat = sending.reshape(chips, -1, DH)
    arrived = lax.all_to_all(flat, "chip", split_axis=0, concat_axis=0, tiled=True).reshape(sending.shape)
    result = merge(arrived, fresh_stats, fresh_summed)

    if chips == 8:
        near = lax.ppermute(result, "chip", [(c, c ^ 1) for c in range(chips)])
        upper = chip & 1 == 1
        couple = jnp.concatenate([jnp.where(upper, near, result), jnp.where(upper, result, near)], 0)
        far = [couple] + [lax.ppermute(couple, "chip", [(c, c ^ (2 * d)) for c in range(chips)]) for d in range(1, 4)]
        odd, high = chip & 2 != 0, chip & 4 != 0

        def of(z):
            return jnp.where(high, jnp.where(odd, far[z ^ 3], far[z ^ 2]), jnp.where(odd, far[z ^ 1], far[z]))

        whole = jnp.concatenate([of(z) for z in range(4)], 0)
    else:
        whole = lax.all_gather(result, "chip", axis=0, tiled=True)
    whole = whole.reshape(pairs, 1, rows // pairs * DH)
    away = lax.ppermute(whole, "core", SWAP)
    whole = jnp.concatenate([jnp.where(first, whole, away), jnp.where(first, away, whole)], 1)
    return whole.reshape(steps_count, req_count, QH * DH)


def solution(mesh):
    groups, n_ctx = mesh.shape["groups"], mesh.shape["ctx"]
    split = Mesh(mesh.devices.reshape(groups, n_ctx // CORES, CORES), ("groups", "chip", "core"))
    ctx = ("chip", "core")
    return jax.shard_map(
        on_device,
        mesh=split,
        in_specs=(
            P(("groups",) + ctx, None),
            P(ctx, None),
            P(ctx, None),
            P(),
            P(),
            P("groups"),
            P(None, "groups", None),
            P(None, "groups", None),
        ),
        out_specs=P(None, "groups", None),
        check_vma=False,
    )
```

```python
import jax
import jax.numpy as jnp
from jax import lax
from jax.experimental import pallas as pl
from jax.experimental.pallas import tpu as pltpu
from jax.sharding import Mesh, PartitionSpec as P

QH = 64
KVH = 8
DH = 128
CORES = 2
BF = jnp.bfloat16
F32 = jnp.float32
SWAP = [(0, 1), (1, 0)]


def mm(a, b):
    return jnp.dot(a, b, preferred_element_type=F32)


def add_pieces(tokens, theirs, groups, total, core=None):
    tok_rows = tokens.shape[0]
    width = groups[0][1][0].shape[1]
    depths = [[part.shape[0] for part in parts] for _, parts in groups]
    span = sum(depths[0])
    deep = span * len(groups)
    flat = [part for _, parts in groups for part in parts]
    count = len(flat)
    last = core is not None
    places = jnp.stack([start for start, _ in groups] + ([core * tok_rows, (1 - core) * tok_rows] if last else []))

    def kernel(places_ref, mine_ref, theirs_ref, *refs):
        parts = refs[:count]
        total_ref, out_ref, mark_ref, columns, weights, sems, loaded = (
            refs[count:] if total is not None else (None,) + refs[count:]
        )
        copies = []
        for j, source in enumerate((mine_ref, theirs_ref)):
            for g in range(len(groups)):
                start = pl.multiple_of(places_ref[g], 128)
                copy = pltpu.make_async_copy(
                    source.at[:, pl.ds(start, span)], columns.at[j, :, pl.ds(g * span, span)], sems.at[j, g]
                )
                copy.start()
                copies.append(copy)
        at = 0
        loads = []
        for k, part in enumerate(parts):
            load = pltpu.make_async_copy(part, weights.at[pl.ds(at, part.shape[0])], loaded.at[k])
            load.start()
            loads.append(load)
            at += part.shape[0]
        mark_ref[...] = jnp.zeros_like(mark_ref)
        for load in loads:
            load.wait()
        for j in range(2):
            for g in range(len(groups)):
                copies[j * len(groups) + g].wait()
            rows = pl.ds(j * tok_rows, tok_rows)
            term = mm(columns[j], weights[...])
            if total is not None:
                term = total_ref[rows, :] + term
            if last:
                rows = pl.ds(pl.multiple_of(places_ref[len(groups) + j], tok_rows), tok_rows)
            out_ref[rows, :] = term.astype(out_ref.dtype)

    tokens = pltpu.with_memory_space_constraint(tokens, pltpu.HBM)
    in_vmem = pl.BlockSpec(memory_space=pltpu.VMEM)
    in_any = pl.BlockSpec(memory_space=pl.ANY)
    sums = [] if total is None else [total]
    return pl.pallas_call(
        kernel,
        out_shape=(
            jax.ShapeDtypeStruct((2 * tok_rows, width), BF if last else F32),
            jax.ShapeDtypeStruct((8, 128), F32),
        ),
        in_specs=[pl.BlockSpec(memory_space=pltpu.SMEM)] + [in_any] * (2 + count) + [in_vmem] * len(sums),
        out_specs=(in_vmem, in_vmem),
        scratch_shapes=[
            pltpu.VMEM((2, tok_rows, deep), BF),
            pltpu.VMEM((deep, width), BF),
            pltpu.SemaphoreType.DMA((2, len(groups))),
            pltpu.SemaphoreType.DMA((count,)),
        ],
        input_output_aliases={} if total is None or last else {3 + count: 0},
        compiler_params=pltpu.CompilerParams(vmem_limit_bytes=20 * 2**20),
        cost_estimate=pl.CostEstimate(
            flops=4 * tok_rows * deep * width, bytes_accessed=4 * tok_rows * deep, transcendentals=0
        ),
    )(places, tokens, theirs, *flat, *sums)


def project(tokens, key_down, value_down, prepare, inputs):
    chips = lax.axis_size("chip")
    chip = lax.axis_index("chip")
    core = lax.axis_index("core")
    first = core == 0
    shard = key_down.shape[0]
    rows = CORES * shard
    own = jnp.where(first, key_down, value_down)
    got = lax.ppermute(jnp.where(first, value_down, key_down), "core", SWAP)
    if chips > 8:
        theirs = lax.ppermute(tokens, "core", SWAP)
        block = jnp.concatenate([jnp.where(first, own, got), jnp.where(first, got, own)], 0)
        full = lax.all_gather(block, "chip", axis=0, tiled=True)
        mine, other = mm(tokens, full).astype(BF), mm(theirs, full).astype(BF)
        return jnp.concatenate([jnp.where(first, mine, other), jnp.where(first, other, mine)], 0), prepare(*inputs)
    cycle = list(range(0, chips, 2)) + list(range(chips - 1, 0, -2))
    last = chips - 1
    place = jnp.where(chip & 1 == 0, chip >> 1, last - (chip >> 1))
    chains = 2
    piece = shard // chains
    right = [(cycle[i], cycle[(i + 1) % chips]) for i in range(chips)]
    left = [(b, a) for a, b in right]
    ways = [right] * chains + [left] * chains

    def start_of(way, step):
        spot = place - step if way == 0 else place + step
        spot = jnp.where(spot < 0, spot + chips, jnp.where(spot > last, spot - chips, spot))
        source = jnp.where(spot < chips // 2, 2 * spot, 2 * (last - spot) + 1)
        return source * rows + (core if way == 0 else 1 - core) * shard

    held = [own[k * piece : (k + 1) * piece] for k in range(chains)]
    got, tokens_later = lax.optimization_barrier((got, tokens))
    held += [got[k * piece : (k + 1) * piece] for k in range(chains)]
    theirs = lax.ppermute(tokens_later, "core", SWAP)
    todo = [(start_of(0, 0), [own]), (start_of(1, 0), [got])]
    total = None
    mark = None
    for step in range(1, chips):
        ready = todo
        if step == 2:
            held = lax.optimization_barrier(held)
        if step == last:
            _, inputs = lax.optimization_barrier((held[0], inputs))
        for k in range(2 * chains):
            if mark is not None:
                held[k], _ = lax.optimization_barrier((held[k], mark))
            held[k] = lax.ppermute(held[k], "chip", ways[k])
        arriving = [(start_of(w, step), held[w * chains : (w + 1) * chains]) for w in range(2)]
        if step == 1:
            todo = todo + arriving
        else:
            total, mark = add_pieces(tokens, theirs, ready, total)
            todo = arriving
    return add_pieces(tokens, theirs, todo, total, core)[0], prepare(*inputs)


def attend(have, got, core, key_up, value_up, query, bounds, chips):
    heads, rows = query.shape[:2]
    tokens = have.shape[0]
    pairs = rows // 8
    blocks = pairs * heads // chips
    scale = 1.0 / DH**0.5

    split = chips == 8

    def kernel(core_ref, have_any, got_any, key_any, value_any, query_any, bounds_ref, *refs):
        outs = refs[:-4]
        latents, ups, query_ref, sems = refs[-4:]
        core = core_ref[0]

        def put(chip, block, value):
            if not split:
                outs[0][chip, block, :, : value.shape[1]] = value
                return
            same = core_ref[1] == chip % 2

            @pl.when(same)
            def _():
                outs[0][chip // 2, block, :, : value.shape[1]] = value

            @pl.when(jnp.logical_not(same))
            def _():
                outs[1][chip // 2, block, :, : value.shape[1]] = value

        lanes = pl.ds(pl.multiple_of(core * heads * DH, heads * DH), heads * DH)
        pairs_of = [
            (have_any, latents.at[core]),
            (got_any, latents.at[1 - core]),
            (key_any.at[:, lanes], ups.at[0]),
            (value_any.at[:, lanes], ups.at[1]),
            (query_any, query_ref),
        ]
        copies = [pltpu.make_async_copy(source, target, sems.at[k]) for k, (source, target) in enumerate(pairs_of)]
        for copy in copies:
            copy.start()
        for copy in copies[:3]:
            copy.wait()
        keys = mm(latents[0], ups[0]).astype(BF)
        for copy in copies[3:]:
            copy.wait()
        values = mm(latents[1], ups[1]).astype(BF)
        position = lax.broadcasted_iota(jnp.int32, (tokens, rows), 0)
        visible = (position >= bounds_ref[0:1, :]) & (position < bounds_ref[1:2, :])
        tops, totals = [], []
        for g in range(heads):
            lanes = slice(g * DH, (g + 1) * DH)
            scores = scale * lax.dot_general(
                keys[:, lanes], query_ref[g], (((1,), (1,)), ((), ())), preferred_element_type=F32
            )
            scores = jnp.where(visible, scores, -1e30)
            top = jnp.max(scores, 0, keepdims=True)
            weights = jnp.where(visible, jnp.exp(scores - top), 0.0)
            tops.append(top)
            totals.append(jnp.sum(weights, 0, keepdims=True))
            summed = lax.dot_general(
                weights.astype(BF), values[:, lanes], (((0,), (0,)), ((), ())), preferred_element_type=F32
            )
            for pair in range(pairs):
                block = pair * heads + g
                put(block // blocks, block % blocks, summed[pair * 8 : (pair + 1) * 8])
        stats = jnp.transpose(jnp.concatenate(tops + totals, 0))
        stride = min(blocks, heads)
        for chip in range(chips):
            spots = [divmod(b, heads) for b in range(chip * blocks, (chip + 1) * blocks, stride)]
            sides = [
                stats[pair * 8 : (pair + 1) * 8, side + g : side + g + stride] for side in (0, heads) for pair, g in spots
            ]
            put(chip, blocks, jnp.concatenate(sides + [jnp.zeros((8, DH - 2 * blocks), F32)], 1))

    ups = [pltpu.with_memory_space_constraint(x, pltpu.HBM) for x in (key_up, value_up)]
    in_vmem = pl.BlockSpec(memory_space=pltpu.VMEM)
    return pl.pallas_call(
        kernel,
        out_shape=[jax.ShapeDtypeStruct((chips // (1 + split), blocks + 1, 8, DH), F32)] * (1 + split),
        in_specs=[pl.BlockSpec(memory_space=pltpu.SMEM)] + [pl.BlockSpec(memory_space=pl.ANY)] * 5 + [in_vmem],
        out_specs=[in_vmem] * (1 + split),
        scratch_shapes=[
            pltpu.VMEM((2,) + have.shape, BF),
            pltpu.VMEM((2, have.shape[1], heads * DH), BF),
            pltpu.VMEM(query.shape, BF),
            pltpu.SemaphoreType.DMA((5,)),
        ],
        compiler_params=pltpu.CompilerParams(vmem_limit_bytes=16 * 2**20),
        cost_estimate=pl.CostEstimate(
            flops=4 * tokens * (have.shape[1] * heads * DH + heads * rows * DH),
            bytes_accessed=4 * tokens * have.shape[1],
            transcendentals=tokens * heads * rows,
        ),
    )(jnp.stack([core, lax.axis_index("chip") & 1]), have, got, *ups, query, bounds)


def merge(sources, fresh_stats, fresh_summed):
    count = len(sources)
    blocks = sources[0].shape[-3] - 1

    def kernel(*refs):
        stats_ref, summed_ref, out_ref = refs[count:]
        parts = refs[:count]
        if len(parts[0].shape) == 4:
            parts = [parts[0].at[i] for i in range(parts[0].shape[0])]
        results = []
        for b in range(blocks):
            tops = [part[blocks, :, b : b + 1] for part in parts]
            totals = [part[blocks, :, blocks + b : blocks + b + 1] for part in parts]
            fresh_top = stats_ref[:, b : b + 1]
            overall = fresh_top
            for top in tops:
                overall = jnp.maximum(overall, top)
            carried = jnp.exp(fresh_top - overall)
            total = stats_ref[:, blocks + b : blocks + b + 1] * carried
            summed = summed_ref[b * 8 : (b + 1) * 8, :] * carried
            for part, top, more in zip(parts, tops, totals):
                carried = jnp.exp(top - overall)
                total = total + more * carried
                summed = summed + part[b] * carried
            results.append(summed / total)
        out_ref[...] = jnp.concatenate(results, 0).astype(BF)

    in_vmem = pl.BlockSpec(memory_space=pltpu.VMEM)
    return pl.pallas_call(
        kernel,
        out_shape=jax.ShapeDtypeStruct((blocks * 8, DH), BF),
        in_specs=[in_vmem] * (count + 2),
        out_specs=in_vmem,
        compiler_params=pltpu.CompilerParams(vmem_limit_bytes=8 * 2**20),
    )(*sources, fresh_stats, fresh_summed)


def pair_up(mine, other, place):
    count, blocks = mine.shape[0], mine.shape[1] - 1

    def kernel(place_ref, mine_ref, other_ref, *outs):
        for d in range(count):
            at = place_ref[0] ^ d
            stats, more = mine_ref[at, blocks], other_ref[at, blocks]
            tops, totals = [], []
            for b in range(blocks):
                one, two = stats[:, b : b + 1], more[:, b : b + 1]
                top = jnp.maximum(one, two)
                one, two = jnp.exp(one - top), jnp.exp(two - top)
                tops.append(top)
                totals.append(stats[:, blocks + b : blocks + b + 1] * one + more[:, blocks + b : blocks + b + 1] * two)
                outs[d][b] = mine_ref[at, b] * one + other_ref[at, b] * two
            outs[d][blocks] = jnp.concatenate(tops + totals + [jnp.zeros((8, DH - 2 * blocks), F32)], 1)

    in_vmem = pl.BlockSpec(memory_space=pltpu.VMEM)
    return pl.pallas_call(
        kernel,
        out_shape=[jax.ShapeDtypeStruct(mine.shape[1:], F32)] * count,
        in_specs=[pl.BlockSpec(memory_space=pltpu.SMEM), in_vmem, in_vmem],
        out_specs=[in_vmem] * count,
        compiler_params=pltpu.CompilerParams(vmem_limit_bytes=8 * 2**20),
    )(place.reshape(1), mine, other)


def on_device(tokens, key_down, value_down, key_up, value_up, prompt_lens, queries, new_latent):
    chips = lax.axis_size("chip")
    chip = lax.axis_index("chip")
    core = lax.axis_index("core")
    first = core == 0
    tok_rows = tokens.shape[0]
    lat_width = key_down.shape[1]
    group = QH // KVH
    heads = KVH // CORES
    scale = 1.0 / DH**0.5
    steps_count, req_count = (queries.shape[0], queries.shape[1])
    pairs = steps_count * req_count
    rows = pairs * heads * group
    share = rows // chips

    def by_head(queries):
        mine = lax.dynamic_slice_in_dim(queries, core * heads * group * DH, heads * group * DH, 2)
        return mine.reshape(steps_count, req_count, heads, group, DH).transpose(2, 0, 1, 3, 4)

    have, query = project(tokens, key_down, value_down, by_head, (queries,))
    got = lax.ppermute(have, "core", SWAP)

    offsets = jnp.cumsum(prompt_lens) - prompt_lens
    bounds = jnp.stack([offsets, offsets + prompt_lens]) - chip * CORES * tok_rows
    bounds = jnp.broadcast_to(bounds[:, None, :, None], (2, steps_count, req_count, group)).reshape(2, -1)
    sending = attend(have, got, core, key_up, value_up, query.reshape(heads, -1, DH), bounds, chips)

    _, new_latent = lax.optimization_barrier((have, new_latent))
    flat_new = new_latent.reshape(pairs, 2 * lat_width)

    def my_heads(latent, up):
        full = lax.dynamic_slice_in_dim(mm(latent, up), core * heads * DH, heads * DH, 1)
        return full.astype(BF).reshape(steps_count, req_count, heads, DH)

    new_keys = my_heads(flat_new[:, :lat_width], key_up)
    new_values = my_heads(flat_new[:, lat_width:], value_up)
    causal = (jnp.arange(steps_count)[:, None] >= jnp.arange(steps_count)[None, :])[:, None, None, None, :]
    fresh = jnp.einsum("gsrjd,urgd->srgju", query, new_keys, preferred_element_type=F32) * scale
    fresh = jnp.where(causal, fresh, -1e30)
    fresh_top = jnp.max(fresh, -1)
    fresh_weights = jnp.where(causal, jnp.exp(fresh - fresh_top[..., None]), 0.0)
    fresh_total = jnp.sum(fresh_weights, -1)
    fresh_summed = jnp.einsum("srgju,urgd->srgjd", fresh_weights.astype(BF), new_values, preferred_element_type=F32)

    def my_share(x):
        return lax.dynamic_slice_in_dim(x, chip * share, share, 0)

    fresh_summed = my_share(fresh_summed.reshape(rows, DH))
    fresh_stats = [my_share(x.reshape(rows)).reshape(-1, group).T for x in (fresh_top, fresh_total)]
    fresh_stats = jnp.pad(jnp.concatenate(fresh_stats, 1), ((0, 0), (0, DH - 2 * share // group)))

    if chips == 8:
        near = [(c, c ^ 1) for c in range(chips)]
        joined = pair_up(sending[0], lax.ppermute(sending[1], "chip", near), chip >> 1)
        far = [lax.ppermute(joined[d], "chip", [(c, c ^ (2 * d)) for c in range(chips)]) for d in range(1, 4)]
        result = merge([joined[0]] + far, fresh_stats, fresh_summed)
    else:
        flat = sending[0].reshape(chips, -1, DH)
        arrived = lax.all_to_all(flat, "chip", split_axis=0, concat_axis=0, tiled=True).reshape(sending[0].shape)
        result = merge([arrived], fresh_stats, fresh_summed)

    if chips == 8:
        near = lax.ppermute(result, "chip", [(c, c ^ 1) for c in range(chips)])
        upper = chip & 1 == 1
        couple = jnp.concatenate([jnp.where(upper, near, result), jnp.where(upper, result, near)], 0)
        far = [couple] + [lax.ppermute(couple, "chip", [(c, c ^ (2 * d)) for c in range(chips)]) for d in range(1, 4)]
        odd, high = chip & 2 != 0, chip & 4 != 0

        def of(z):
            return jnp.where(high, jnp.where(odd, far[z ^ 3], far[z ^ 2]), jnp.where(odd, far[z ^ 1], far[z]))

        whole = jnp.concatenate([of(z) for z in range(4)], 0)
    else:
        whole = lax.all_gather(result, "chip", axis=0, tiled=True)
    whole = whole.reshape(pairs, 1, rows // pairs * DH)
    away = lax.ppermute(whole, "core", SWAP)
    whole = jnp.concatenate([jnp.where(first, whole, away), jnp.where(first, away, whole)], 1)
    return whole.reshape(steps_count, req_count, QH * DH)


def solution(mesh):
    groups, n_ctx = mesh.shape["groups"], mesh.shape["ctx"]
    split = Mesh(mesh.devices.reshape(groups, n_ctx // CORES, CORES), ("groups", "chip", "core"))
    ctx = ("chip", "core")
    return jax.shard_map(
        on_device,
        mesh=split,
        in_specs=(
            P(("groups",) + ctx, None),
            P(ctx, None),
            P(ctx, None),
            P(),
            P(),
            P("groups"),
            P(None, "groups", None),
            P(None, "groups", None),
        ),
        out_specs=P(None, "groups", None),
        check_vma=False,
    )
```

```python
import jax
import jax.numpy as jnp
from jax import lax
from jax.experimental import pallas as pl
from jax.experimental.pallas import tpu as pltpu
from jax.sharding import Mesh, PartitionSpec as P

QH = 64
KVH = 8
DH = 128
CORES = 2
BF = jnp.bfloat16
F32 = jnp.float32
SWAP = [(0, 1), (1, 0)]


def mm(a, b):
    return jnp.dot(a, b, preferred_element_type=F32)


def add_pieces(tokens, theirs, groups, total, core=None):
    tok_rows = tokens.shape[0]
    width = groups[0][1][0].shape[1]
    depths = [[part.shape[0] for part in parts] for _, parts in groups]
    span = sum(depths[0])
    deep = span * len(groups)
    flat = [part for _, parts in groups for part in parts]
    count = len(flat)
    last = core is not None
    places = jnp.stack([start for start, _ in groups] + ([core * tok_rows, (1 - core) * tok_rows] if last else []))

    def kernel(places_ref, mine_ref, theirs_ref, *refs):
        parts = refs[:count]
        total_ref, out_ref, mark_ref, columns, weights, sems, loaded = (
            refs[count:] if total is not None else (None,) + refs[count:]
        )
        copies = []
        for j, source in enumerate((mine_ref, theirs_ref)):
            for g in range(len(groups)):
                start = pl.multiple_of(places_ref[g], 128)
                copy = pltpu.make_async_copy(
                    source.at[:, pl.ds(start, span)], columns.at[j, :, pl.ds(g * span, span)], sems.at[j, g]
                )
                copy.start()
                copies.append(copy)
        at = 0
        loads = []
        for k, part in enumerate(parts):
            load = pltpu.make_async_copy(part, weights.at[pl.ds(at, part.shape[0])], loaded.at[k])
            load.start()
            loads.append(load)
            at += part.shape[0]
        mark_ref[...] = jnp.zeros_like(mark_ref)
        for load in loads:
            load.wait()
        for j in range(2):
            for g in range(len(groups)):
                copies[j * len(groups) + g].wait()
            rows = pl.ds(j * tok_rows, tok_rows)
            term = mm(columns[j], weights[...])
            if total is not None:
                term = total_ref[rows, :] + term
            if last:
                rows = pl.ds(pl.multiple_of(places_ref[len(groups) + j], tok_rows), tok_rows)
            out_ref[rows, :] = term.astype(out_ref.dtype)

    tokens = pltpu.with_memory_space_constraint(tokens, pltpu.HBM)
    in_vmem = pl.BlockSpec(memory_space=pltpu.VMEM)
    in_any = pl.BlockSpec(memory_space=pl.ANY)
    sums = [] if total is None else [total]
    return pl.pallas_call(
        kernel,
        out_shape=(
            jax.ShapeDtypeStruct((2 * tok_rows, width), BF if last else F32),
            jax.ShapeDtypeStruct((8, 128), F32),
        ),
        in_specs=[pl.BlockSpec(memory_space=pltpu.SMEM)] + [in_any] * (2 + count) + [in_vmem] * len(sums),
        out_specs=(in_vmem, in_vmem),
        scratch_shapes=[
            pltpu.VMEM((2, tok_rows, deep), BF),
            pltpu.VMEM((deep, width), BF),
            pltpu.SemaphoreType.DMA((2, len(groups))),
            pltpu.SemaphoreType.DMA((count,)),
        ],
        input_output_aliases={} if total is None or last else {3 + count: 0},
        compiler_params=pltpu.CompilerParams(vmem_limit_bytes=20 * 2**20),
        cost_estimate=pl.CostEstimate(
            flops=4 * tok_rows * deep * width, bytes_accessed=4 * tok_rows * deep, transcendentals=0
        ),
    )(places, tokens, theirs, *flat, *sums)


def project(tokens, key_down, value_down, prepare, inputs):
    chips = lax.axis_size("chip")
    chip = lax.axis_index("chip")
    core = lax.axis_index("core")
    first = core == 0
    shard = key_down.shape[0]
    rows = CORES * shard
    own = jnp.where(first, key_down, value_down)
    got = lax.ppermute(jnp.where(first, value_down, key_down), "core", SWAP)
    if chips > 8:
        theirs = lax.ppermute(tokens, "core", SWAP)
        block = jnp.concatenate([jnp.where(first, own, got), jnp.where(first, got, own)], 0)
        full = lax.all_gather(block, "chip", axis=0, tiled=True)
        mine, other = mm(tokens, full).astype(BF), mm(theirs, full).astype(BF)
        return jnp.concatenate([jnp.where(first, mine, other), jnp.where(first, other, mine)], 0), prepare(*inputs)
    cycle = list(range(0, chips, 2)) + list(range(chips - 1, 0, -2))
    last = chips - 1
    place = jnp.where(chip & 1 == 0, chip >> 1, last - (chip >> 1))
    chains = 2
    piece = shard // chains
    right = [(cycle[i], cycle[(i + 1) % chips]) for i in range(chips)]
    left = [(b, a) for a, b in right]
    ways = [right] * chains + [left] * chains

    def start_of(way, step):
        spot = place - step if way == 0 else place + step
        spot = jnp.where(spot < 0, spot + chips, jnp.where(spot > last, spot - chips, spot))
        source = jnp.where(spot < chips // 2, 2 * spot, 2 * (last - spot) + 1)
        return source * rows + (core if way == 0 else 1 - core) * shard

    held = [own[k * piece : (k + 1) * piece] for k in range(chains)]
    got, tokens_later = lax.optimization_barrier((got, tokens))
    held += [got[k * piece : (k + 1) * piece] for k in range(chains)]
    theirs = lax.ppermute(tokens_later, "core", SWAP)
    todo = [(start_of(0, 0), [own]), (start_of(1, 0), [got])]
    total = None
    mark = None
    for step in range(1, chips):
        ready = todo
        if step == 2:
            held = lax.optimization_barrier(held)
        if step == 3:
            _, inputs = lax.optimization_barrier((held[0], inputs))
            early = prepare(*inputs)
        if step == 5:
            held[0], early = lax.optimization_barrier((held[0], early))
        for k in range(2 * chains):
            if mark is not None:
                held[k], _ = lax.optimization_barrier((held[k], mark))
            held[k] = lax.ppermute(held[k], "chip", ways[k])
        arriving = [(start_of(w, step), held[w * chains : (w + 1) * chains]) for w in range(2)]
        if step == 1:
            todo = todo + arriving
        else:
            total, mark = add_pieces(tokens, theirs, ready, total)
            todo = arriving
    return add_pieces(tokens, theirs, todo, total, core)[0], early


def attend(have, got, core, key_up, value_up, query, bounds, chips):
    heads, rows = query.shape[:2]
    tokens = have.shape[0]
    pairs = rows // 8
    blocks = pairs * heads // chips
    scale = 1.0 / DH**0.5

    def kernel(core_ref, have_ref, got_ref, key_up_ref, value_up_ref, query_ref, bounds_ref, out_ref):
        first = core_ref[0] == 0
        have, got = have_ref[...], got_ref[...]
        keys = mm(jnp.where(first, have, got), key_up_ref[...]).astype(BF)
        values = mm(jnp.where(first, got, have), value_up_ref[...]).astype(BF)
        position = lax.broadcasted_iota(jnp.int32, (tokens, rows), 0)
        visible = (position >= bounds_ref[0:1, :]) & (position < bounds_ref[1:2, :])
        tops, totals = [], []
        for g in range(heads):
            lanes = slice(g * DH, (g + 1) * DH)
            scores = scale * lax.dot_general(
                keys[:, lanes], query_ref[g], (((1,), (1,)), ((), ())), preferred_element_type=F32
            )
            scores = jnp.where(visible, scores, -1e30)
            top = jnp.max(scores, 0, keepdims=True)
            weights = jnp.where(visible, jnp.exp(scores - top), 0.0)
            tops.append(top)
            totals.append(jnp.sum(weights, 0, keepdims=True))
            summed = lax.dot_general(
                weights.astype(BF), values[:, lanes], (((0,), (0,)), ((), ())), preferred_element_type=F32
            )
            for pair in range(pairs):
                block = pair * heads + g
                out_ref[block // blocks, block % blocks] = summed[pair * 8 : (pair + 1) * 8]
        stats = jnp.transpose(jnp.concatenate(tops + totals, 0))
        stride = min(blocks, heads)
        for chip in range(chips):
            spots = [divmod(b, heads) for b in range(chip * blocks, (chip + 1) * blocks, stride)]
            sides = [
                stats[pair * 8 : (pair + 1) * 8, side + g : side + g + stride] for side in (0, heads) for pair, g in spots
            ]
            out_ref[chip, blocks] = jnp.zeros((8, DH), F32)
            out_ref[chip, blocks, :, : 2 * blocks] = jnp.concatenate(sides, 1)

    in_vmem = pl.BlockSpec(memory_space=pltpu.VMEM)
    return pl.pallas_call(
        kernel,
        out_shape=jax.ShapeDtypeStruct((chips, blocks + 1, 8, DH), F32),
        in_specs=[pl.BlockSpec(memory_space=pltpu.SMEM)] + [in_vmem] * 6,
        out_specs=in_vmem,
        compiler_params=pltpu.CompilerParams(vmem_limit_bytes=16 * 2**20),
        cost_estimate=pl.CostEstimate(
            flops=4 * tokens * (have.shape[1] * heads * DH + heads * rows * DH),
            bytes_accessed=4 * tokens * have.shape[1],
            transcendentals=tokens * heads * rows,
        ),
    )(core.reshape(1), have, got, key_up, value_up, query, bounds)


def merge(arrived, fresh_stats, fresh_summed):
    chips, blocks = arrived.shape[0], arrived.shape[1] - 1

    def kernel(arrived_ref, stats_ref, summed_ref, out_ref):
        results = []
        for b in range(blocks):
            top = arrived_ref[:, blocks, :, b : b + 1]
            total = arrived_ref[:, blocks, :, blocks + b : blocks + b + 1]
            fresh_top = stats_ref[:, b : b + 1]
            overall = jnp.maximum(jnp.max(top, 0), fresh_top)
            carried = jnp.exp(top - overall[None])
            fresh_carried = jnp.exp(fresh_top - overall)
            total = jnp.sum(total * carried, 0) + stats_ref[:, blocks + b : blocks + b + 1] * fresh_carried
            summed = jnp.sum(arrived_ref[:, b] * carried, 0) + summed_ref[b * 8 : (b + 1) * 8, :] * fresh_carried
            results.append(summed / total)
        out_ref[...] = jnp.concatenate(results, 0).astype(BF)

    in_vmem = pl.BlockSpec(memory_space=pltpu.VMEM)
    return pl.pallas_call(
        kernel,
        out_shape=jax.ShapeDtypeStruct((blocks * 8, DH), BF),
        in_specs=[in_vmem] * 3,
        out_specs=in_vmem,
        compiler_params=pltpu.CompilerParams(vmem_limit_bytes=8 * 2**20),
        cost_estimate=pl.CostEstimate(
            flops=2 * chips * blocks * 8 * DH, bytes_accessed=4 * arrived.size, transcendentals=chips * blocks * 8
        ),
    )(arrived, fresh_stats, fresh_summed)


def on_device(tokens, key_down, value_down, key_up, value_up, prompt_lens, queries, new_latent):
    chips = lax.axis_size("chip")
    chip = lax.axis_index("chip")
    core = lax.axis_index("core")
    first = core == 0
    tok_rows = tokens.shape[0]
    lat_width = key_down.shape[1]
    group = QH // KVH
    heads = KVH // CORES
    scale = 1.0 / DH**0.5
    steps_count, req_count = (queries.shape[0], queries.shape[1])
    pairs = steps_count * req_count
    rows = pairs * heads * group
    share = rows // chips

    def my_heads(queries, key_up, value_up):
        mine = lax.dynamic_slice_in_dim(queries, core * heads * group * DH, heads * group * DH, 2)
        mine = mine.reshape(steps_count, req_count, heads, group, DH).transpose(2, 0, 1, 3, 4)
        ups = [lax.dynamic_slice_in_dim(x, core * heads * DH, heads * DH, 1) for x in (key_up, value_up)]
        return mine, *ups

    have, early = project(tokens, key_down, value_down, my_heads, (queries, key_up, value_up))
    query, key_up, value_up = early
    got = lax.ppermute(have, "core", SWAP)

    offsets = jnp.cumsum(prompt_lens) - prompt_lens
    bounds = jnp.stack([offsets, offsets + prompt_lens]) - chip * CORES * tok_rows
    bounds = jnp.broadcast_to(bounds[:, None, :, None], (2, steps_count, req_count, group)).reshape(2, -1)
    sending = attend(have, got, core, key_up, value_up, query.reshape(heads, -1, DH), bounds, chips)

    _, new_latent = lax.optimization_barrier((have, new_latent))
    flat_new = new_latent.reshape(pairs, 2 * lat_width)
    new_keys = mm(flat_new[:, :lat_width], key_up).astype(BF).reshape(steps_count, req_count, heads, DH)
    new_values = mm(flat_new[:, lat_width:], value_up).astype(BF).reshape(steps_count, req_count, heads, DH)
    causal = (jnp.arange(steps_count)[:, None] >= jnp.arange(steps_count)[None, :])[:, None, None, None, :]
    fresh = jnp.einsum("gsrjd,urgd->srgju", query, new_keys, preferred_element_type=F32) * scale
    fresh = jnp.where(causal, fresh, -1e30)
    fresh_top = jnp.max(fresh, -1)
    fresh_weights = jnp.where(causal, jnp.exp(fresh - fresh_top[..., None]), 0.0)
    fresh_total = jnp.sum(fresh_weights, -1)
    fresh_summed = jnp.einsum("srgju,urgd->srgjd", fresh_weights.astype(BF), new_values, preferred_element_type=F32)

    def my_share(x):
        return lax.dynamic_slice_in_dim(x, chip * share, share, 0)

    fresh_summed = my_share(fresh_summed.reshape(rows, DH))
    fresh_stats = [my_share(x.reshape(rows)).reshape(-1, group).T for x in (fresh_top, fresh_total)]
    fresh_stats = jnp.pad(jnp.concatenate(fresh_stats, 1), ((0, 0), (0, DH - 2 * share // group)))

    flat = sending.reshape(chips, -1, DH)
    arrived = lax.all_to_all(flat, "chip", split_axis=0, concat_axis=0, tiled=True).reshape(sending.shape)
    result = merge(arrived, fresh_stats, fresh_summed)

    if chips == 8:
        near = lax.ppermute(result, "chip", [(c, c ^ 1) for c in range(chips)])
        upper = chip & 1 == 1
        couple = jnp.concatenate([jnp.where(upper, near, result), jnp.where(upper, result, near)], 0)
        far = [couple] + [lax.ppermute(couple, "chip", [(c, c ^ (2 * d)) for c in range(chips)]) for d in range(1, 4)]
        odd, high = chip & 2 != 0, chip & 4 != 0

        def of(z):
            return jnp.where(high, jnp.where(odd, far[z ^ 3], far[z ^ 2]), jnp.where(odd, far[z ^ 1], far[z]))

        whole = jnp.concatenate([of(z) for z in range(4)], 0)
    else:
        whole = lax.all_gather(result, "chip", axis=0, tiled=True)
    whole = whole.reshape(pairs, 1, rows // pairs * DH)
    away = lax.ppermute(whole, "core", SWAP)
    whole = jnp.concatenate([jnp.where(first, whole, away), jnp.where(first, away, whole)], 1)
    return whole.reshape(steps_count, req_count, QH * DH)


def solution(mesh):
    groups, n_ctx = mesh.shape["groups"], mesh.shape["ctx"]
    split = Mesh(mesh.devices.reshape(groups, n_ctx // CORES, CORES), ("groups", "chip", "core"))
    ctx = ("chip", "core")
    return jax.shard_map(
        on_device,
        mesh=split,
        in_specs=(
            P(("groups",) + ctx, None),
            P(ctx, None),
            P(ctx, None),
            P(),
            P(),
            P("groups"),
            P(None, "groups", None),
            P(None, "groups", None),
        ),
        out_specs=P(None, "groups", None),
        check_vma=False,
    )
```

```python
import jax
import jax.numpy as jnp
from jax import lax
from jax.experimental import pallas as pl
from jax.experimental.pallas import tpu as pltpu
from jax.sharding import Mesh, PartitionSpec as P

QH = 64
KVH = 8
DH = 128
CORES = 2
BF = jnp.bfloat16
F32 = jnp.float32
SWAP = [(0, 1), (1, 0)]


def mm(a, b):
    return jnp.dot(a, b, preferred_element_type=F32)


def add_pieces(tokens, theirs, groups, total, core=None):
    tok_rows = tokens.shape[0]
    width = groups[0][1][0].shape[1]
    depths = [[part.shape[0] for part in parts] for _, parts in groups]
    span = sum(depths[0])
    deep = span * len(groups)
    flat = [part for _, parts in groups for part in parts]
    count = len(flat)
    last = core is not None
    places = jnp.stack([start for start, _ in groups] + ([core * tok_rows, (1 - core) * tok_rows] if last else []))

    def kernel(places_ref, mine_ref, theirs_ref, *refs):
        parts = refs[:count]
        total_ref, out_ref, mark_ref, columns, weights, sems, loaded = (
            refs[count:] if total is not None else (None,) + refs[count:]
        )
        copies = []
        for j, source in enumerate((mine_ref, theirs_ref)):
            for g in range(len(groups)):
                start = pl.multiple_of(places_ref[g], 128)
                copy = pltpu.make_async_copy(
                    source.at[:, pl.ds(start, span)], columns.at[j, :, pl.ds(g * span, span)], sems.at[j, g]
                )
                copy.start()
                copies.append(copy)
        at = 0
        loads = []
        for k, part in enumerate(parts):
            load = pltpu.make_async_copy(part, weights.at[pl.ds(at, part.shape[0])], loaded.at[k])
            load.start()
            loads.append(load)
            at += part.shape[0]
        mark_ref[...] = jnp.zeros_like(mark_ref)
        for load in loads:
            load.wait()
        for j in range(2):
            for g in range(len(groups)):
                copies[j * len(groups) + g].wait()
            rows = pl.ds(j * tok_rows, tok_rows)
            term = mm(columns[j], weights[...])
            if total is not None:
                term = total_ref[rows, :] + term
            if last:
                rows = pl.ds(pl.multiple_of(places_ref[len(groups) + j], tok_rows), tok_rows)
            out_ref[rows, :] = term.astype(out_ref.dtype)

    tokens = pltpu.with_memory_space_constraint(tokens, pltpu.HBM)
    in_vmem = pl.BlockSpec(memory_space=pltpu.VMEM)
    in_any = pl.BlockSpec(memory_space=pl.ANY)
    sums = [] if total is None else [total]
    return pl.pallas_call(
        kernel,
        out_shape=(
            jax.ShapeDtypeStruct((2 * tok_rows, width), BF if last else F32),
            jax.ShapeDtypeStruct((8, 128), F32),
        ),
        in_specs=[pl.BlockSpec(memory_space=pltpu.SMEM)] + [in_any] * (2 + count) + [in_vmem] * len(sums),
        out_specs=(in_vmem, in_vmem),
        scratch_shapes=[
            pltpu.VMEM((2, tok_rows, deep), BF),
            pltpu.VMEM((deep, width), BF),
            pltpu.SemaphoreType.DMA((2, len(groups))),
            pltpu.SemaphoreType.DMA((count,)),
        ],
        input_output_aliases={} if total is None or last else {3 + count: 0},
        compiler_params=pltpu.CompilerParams(vmem_limit_bytes=20 * 2**20),
        cost_estimate=pl.CostEstimate(
            flops=4 * tok_rows * deep * width, bytes_accessed=4 * tok_rows * deep, transcendentals=0
        ),
    )(places, tokens, theirs, *flat, *sums)


def project(tokens, key_down, value_down, prepare, inputs):
    chips = lax.axis_size("chip")
    chip = lax.axis_index("chip")
    core = lax.axis_index("core")
    first = core == 0
    shard = key_down.shape[0]
    rows = CORES * shard
    own = jnp.where(first, key_down, value_down)
    got = lax.ppermute(jnp.where(first, value_down, key_down), "core", SWAP)
    if chips > 8:
        theirs = lax.ppermute(tokens, "core", SWAP)
        block = jnp.concatenate([jnp.where(first, own, got), jnp.where(first, got, own)], 0)
        full = lax.all_gather(block, "chip", axis=0, tiled=True)
        mine, other = mm(tokens, full).astype(BF), mm(theirs, full).astype(BF)
        return jnp.concatenate([jnp.where(first, mine, other), jnp.where(first, other, mine)], 0), prepare(*inputs)
    cycle = list(range(0, chips, 2)) + list(range(chips - 1, 0, -2))
    last = chips - 1
    place = jnp.where(chip & 1 == 0, chip >> 1, last - (chip >> 1))
    chains = 2
    piece = shard // chains
    right = [(cycle[i], cycle[(i + 1) % chips]) for i in range(chips)]
    left = [(b, a) for a, b in right]
    ways = [right] * chains + [left] * chains

    def start_of(way, step):
        spot = place - step if way == 0 else place + step
        spot = jnp.where(spot < 0, spot + chips, jnp.where(spot > last, spot - chips, spot))
        source = jnp.where(spot < chips // 2, 2 * spot, 2 * (last - spot) + 1)
        return source * rows + (core if way == 0 else 1 - core) * shard

    held = [own[k * piece : (k + 1) * piece] for k in range(chains)]
    held += [got[k * piece : (k + 1) * piece] for k in range(chains)]
    todo = [(start_of(0, 0), [own]), (start_of(1, 0), [got])]
    total = None
    mark = None
    for step in range(1, chips):
        if step == 2:
            held, tokens_later = lax.optimization_barrier((held, tokens))
            theirs = lax.ppermute(tokens_later, "core", SWAP)
        if step == 3:
            _, inputs = lax.optimization_barrier((held[0], inputs))
            early = prepare(*inputs)
        if step == 5:
            held[0], early = lax.optimization_barrier((held[0], early))
        for k in range(2 * chains):
            if mark is not None:
                held[k], _ = lax.optimization_barrier((held[k], mark))
            held[k] = lax.ppermute(held[k], "chip", ways[k])
        arriving = [(start_of(w, step), held[w * chains : (w + 1) * chains]) for w in range(2)]
        todo += arriving
        if step >= 3:
            ready, todo = (todo[:4], todo[4:]) if total is None else (todo[:2], todo[2:])
            total, mark = add_pieces(tokens, theirs, ready, total)
    total, _ = add_pieces(tokens, theirs, todo[:2], total)
    return add_pieces(tokens, theirs, todo[2:], total, core)[0], early


def attend(have, got, core, key_up, value_up, query, bounds, chips):
    heads, rows = query.shape[:2]
    tokens = have.shape[0]
    pairs = rows // 8
    blocks = pairs * heads // chips
    scale = 1.0 / DH**0.5

    def kernel(core_ref, have_ref, got_ref, key_up_ref, value_up_ref, query_ref, bounds_ref, out_ref):
        first = core_ref[0] == 0
        have, got = have_ref[...], got_ref[...]
        keys = mm(jnp.where(first, have, got), key_up_ref[...]).astype(BF)
        values = mm(jnp.where(first, got, have), value_up_ref[...]).astype(BF)
        position = lax.broadcasted_iota(jnp.int32, (tokens, rows), 0)
        visible = (position >= bounds_ref[0:1, :]) & (position < bounds_ref[1:2, :])
        tops, totals = [], []
        for g in range(heads):
            lanes = slice(g * DH, (g + 1) * DH)
            scores = scale * lax.dot_general(
                keys[:, lanes], query_ref[g], (((1,), (1,)), ((), ())), preferred_element_type=F32
            )
            scores = jnp.where(visible, scores, -1e30)
            top = jnp.max(scores, 0, keepdims=True)
            weights = jnp.where(visible, jnp.exp(scores - top), 0.0)
            tops.append(top)
            totals.append(jnp.sum(weights, 0, keepdims=True))
            summed = lax.dot_general(
                weights.astype(BF), values[:, lanes], (((0,), (0,)), ((), ())), preferred_element_type=F32
            )
            for pair in range(pairs):
                block = pair * heads + g
                out_ref[block // blocks, block % blocks] = summed[pair * 8 : (pair + 1) * 8]
        stats = jnp.transpose(jnp.concatenate(tops + totals, 0))
        stride = min(blocks, heads)
        for chip in range(chips):
            spots = [divmod(b, heads) for b in range(chip * blocks, (chip + 1) * blocks, stride)]
            sides = [
                stats[pair * 8 : (pair + 1) * 8, side + g : side + g + stride] for side in (0, heads) for pair, g in spots
            ]
            out_ref[chip, blocks] = jnp.zeros((8, DH), F32)
            out_ref[chip, blocks, :, : 2 * blocks] = jnp.concatenate(sides, 1)

    in_vmem = pl.BlockSpec(memory_space=pltpu.VMEM)
    return pl.pallas_call(
        kernel,
        out_shape=jax.ShapeDtypeStruct((chips, blocks + 1, 8, DH), F32),
        in_specs=[pl.BlockSpec(memory_space=pltpu.SMEM)] + [in_vmem] * 6,
        out_specs=in_vmem,
        compiler_params=pltpu.CompilerParams(vmem_limit_bytes=16 * 2**20),
        cost_estimate=pl.CostEstimate(
            flops=4 * tokens * (have.shape[1] * heads * DH + heads * rows * DH),
            bytes_accessed=4 * tokens * have.shape[1],
            transcendentals=tokens * heads * rows,
        ),
    )(core.reshape(1), have, got, key_up, value_up, query, bounds)


def merge(arrived, fresh_stats, fresh_summed):
    chips, blocks = arrived.shape[0], arrived.shape[1] - 1

    def kernel(arrived_ref, stats_ref, summed_ref, out_ref):
        results = []
        for b in range(blocks):
            top = arrived_ref[:, blocks, :, b : b + 1]
            total = arrived_ref[:, blocks, :, blocks + b : blocks + b + 1]
            fresh_top = stats_ref[:, b : b + 1]
            overall = jnp.maximum(jnp.max(top, 0), fresh_top)
            carried = jnp.exp(top - overall[None])
            fresh_carried = jnp.exp(fresh_top - overall)
            total = jnp.sum(total * carried, 0) + stats_ref[:, blocks + b : blocks + b + 1] * fresh_carried
            summed = jnp.sum(arrived_ref[:, b] * carried, 0) + summed_ref[b * 8 : (b + 1) * 8, :] * fresh_carried
            results.append(summed / total)
        out_ref[...] = jnp.concatenate(results, 0).astype(BF)

    in_vmem = pl.BlockSpec(memory_space=pltpu.VMEM)
    return pl.pallas_call(
        kernel,
        out_shape=jax.ShapeDtypeStruct((blocks * 8, DH), BF),
        in_specs=[in_vmem] * 3,
        out_specs=in_vmem,
        compiler_params=pltpu.CompilerParams(vmem_limit_bytes=8 * 2**20),
        cost_estimate=pl.CostEstimate(
            flops=2 * chips * blocks * 8 * DH, bytes_accessed=4 * arrived.size, transcendentals=chips * blocks * 8
        ),
    )(arrived, fresh_stats, fresh_summed)


def on_device(tokens, key_down, value_down, key_up, value_up, prompt_lens, queries, new_latent):
    chips = lax.axis_size("chip")
    chip = lax.axis_index("chip")
    core = lax.axis_index("core")
    first = core == 0
    tok_rows = tokens.shape[0]
    lat_width = key_down.shape[1]
    group = QH // KVH
    heads = KVH // CORES
    scale = 1.0 / DH**0.5
    steps_count, req_count = (queries.shape[0], queries.shape[1])
    pairs = steps_count * req_count
    rows = pairs * heads * group
    share = rows // chips

    def my_heads(queries, key_up, value_up):
        mine = lax.dynamic_slice_in_dim(queries, core * heads * group * DH, heads * group * DH, 2)
        mine = mine.reshape(steps_count, req_count, heads, group, DH).transpose(2, 0, 1, 3, 4)
        ups = [lax.dynamic_slice_in_dim(x, core * heads * DH, heads * DH, 1) for x in (key_up, value_up)]
        return mine, *ups

    have, early = project(tokens, key_down, value_down, my_heads, (queries, key_up, value_up))
    query, key_up, value_up = early
    got = lax.ppermute(have, "core", SWAP)

    offsets = jnp.cumsum(prompt_lens) - prompt_lens
    bounds = jnp.stack([offsets, offsets + prompt_lens]) - chip * CORES * tok_rows
    bounds = jnp.broadcast_to(bounds[:, None, :, None], (2, steps_count, req_count, group)).reshape(2, -1)
    sending = attend(have, got, core, key_up, value_up, query.reshape(heads, -1, DH), bounds, chips)

    _, new_latent = lax.optimization_barrier((have, new_latent))
    flat_new = new_latent.reshape(pairs, 2 * lat_width)
    new_keys = mm(flat_new[:, :lat_width], key_up).astype(BF).reshape(steps_count, req_count, heads, DH)
    new_values = mm(flat_new[:, lat_width:], value_up).astype(BF).reshape(steps_count, req_count, heads, DH)
    causal = (jnp.arange(steps_count)[:, None] >= jnp.arange(steps_count)[None, :])[:, None, None, None, :]
    fresh = jnp.einsum("gsrjd,urgd->srgju", query, new_keys, preferred_element_type=F32) * scale
    fresh = jnp.where(causal, fresh, -1e30)
    fresh_top = jnp.max(fresh, -1)
    fresh_weights = jnp.where(causal, jnp.exp(fresh - fresh_top[..., None]), 0.0)
    fresh_total = jnp.sum(fresh_weights, -1)
    fresh_summed = jnp.einsum("srgju,urgd->srgjd", fresh_weights.astype(BF), new_values, preferred_element_type=F32)

    def my_share(x):
        return lax.dynamic_slice_in_dim(x, chip * share, share, 0)

    fresh_summed = my_share(fresh_summed.reshape(rows, DH))
    fresh_stats = [my_share(x.reshape(rows)).reshape(-1, group).T for x in (fresh_top, fresh_total)]
    fresh_stats = jnp.pad(jnp.concatenate(fresh_stats, 1), ((0, 0), (0, DH - 2 * share // group)))

    flat = sending.reshape(chips, -1, DH)
    arrived = lax.all_to_all(flat, "chip", split_axis=0, concat_axis=0, tiled=True).reshape(sending.shape)
    result = merge(arrived, fresh_stats, fresh_summed)

    if chips == 8:
        near = lax.ppermute(result, "chip", [(c, c ^ 1) for c in range(chips)])
        upper = chip & 1 == 1
        couple = jnp.concatenate([jnp.where(upper, near, result), jnp.where(upper, result, near)], 0)
        far = [couple] + [lax.ppermute(couple, "chip", [(c, c ^ (2 * d)) for c in range(chips)]) for d in range(1, 4)]
        odd, high = chip & 2 != 0, chip & 4 != 0

        def of(z):
            return jnp.where(high, jnp.where(odd, far[z ^ 3], far[z ^ 2]), jnp.where(odd, far[z ^ 1], far[z]))

        whole = jnp.concatenate([of(z) for z in range(4)], 0)
    else:
        whole = lax.all_gather(result, "chip", axis=0, tiled=True)
    whole = whole.reshape(pairs, 1, rows // pairs * DH)
    away = lax.ppermute(whole, "core", SWAP)
    whole = jnp.concatenate([jnp.where(first, whole, away), jnp.where(first, away, whole)], 1)
    return whole.reshape(steps_count, req_count, QH * DH)


def solution(mesh):
    groups, n_ctx = mesh.shape["groups"], mesh.shape["ctx"]
    split = Mesh(mesh.devices.reshape(groups, n_ctx // CORES, CORES), ("groups", "chip", "core"))
    ctx = ("chip", "core")
    return jax.shard_map(
        on_device,
        mesh=split,
        in_specs=(
            P(("groups",) + ctx, None),
            P(ctx, None),
            P(ctx, None),
            P(),
            P(),
            P("groups"),
            P(None, "groups", None),
            P(None, "groups", None),
        ),
        out_specs=P(None, "groups", None),
        check_vma=False,
    )
```

```python
import jax
import jax.numpy as jnp
from jax import lax
from jax.experimental import pallas as pl
from jax.experimental.pallas import tpu as pltpu
from jax.sharding import Mesh, PartitionSpec as P

QH = 64
KVH = 8
DH = 128
CORES = 2
BF = jnp.bfloat16
F32 = jnp.float32
SWAP = [(0, 1), (1, 0)]


def mm(a, b):
    return jnp.dot(a, b, preferred_element_type=F32)


def add_pieces(tokens, theirs, groups, total, core=None):
    tok_rows = tokens.shape[0]
    width = groups[0][1][0].shape[1]
    depths = [[part.shape[0] for part in parts] for _, parts in groups]
    span = sum(depths[0])
    deep = span * len(groups)
    flat = [part for _, parts in groups for part in parts]
    count = len(flat)
    last = core is not None
    places = jnp.stack([start for start, _ in groups] + ([core * tok_rows, (1 - core) * tok_rows] if last else []))

    def kernel(places_ref, mine_ref, theirs_ref, *refs):
        parts = refs[:count]
        total_ref, out_ref, mark_ref, columns, weights, sems, loaded = (
            refs[count:] if total is not None else (None,) + refs[count:]
        )
        copies = []
        for j, source in enumerate((mine_ref, theirs_ref)):
            for g in range(len(groups)):
                start = pl.multiple_of(places_ref[g], 128)
                copy = pltpu.make_async_copy(
                    source.at[:, pl.ds(start, span)], columns.at[j, :, pl.ds(g * span, span)], sems.at[j, g]
                )
                copy.start()
                copies.append(copy)
        at = 0
        loads = []
        for k, part in enumerate(parts):
            load = pltpu.make_async_copy(part, weights.at[pl.ds(at, part.shape[0])], loaded.at[k])
            load.start()
            loads.append(load)
            at += part.shape[0]
        mark_ref[...] = jnp.zeros_like(mark_ref)
        for load in loads:
            load.wait()
        for j in range(2):
            for g in range(len(groups)):
                copies[j * len(groups) + g].wait()
            rows = pl.ds(j * tok_rows, tok_rows)
            term = mm(columns[j], weights[...])
            if total is not None:
                term = total_ref[rows, :] + term
            if last:
                rows = pl.ds(pl.multiple_of(places_ref[len(groups) + j], tok_rows), tok_rows)
            out_ref[rows, :] = term.astype(out_ref.dtype)

    tokens = pltpu.with_memory_space_constraint(tokens, pltpu.HBM)
    if total is None:
        flat = flat[:2] + [pltpu.with_memory_space_constraint(x, pltpu.HBM) for x in flat[2:]]
    in_vmem = pl.BlockSpec(memory_space=pltpu.VMEM)
    in_any = pl.BlockSpec(memory_space=pl.ANY)
    sums = [] if total is None else [total]
    return pl.pallas_call(
        kernel,
        out_shape=(
            jax.ShapeDtypeStruct((2 * tok_rows, width), BF if last else F32),
            jax.ShapeDtypeStruct((8, 128), F32),
        ),
        in_specs=[pl.BlockSpec(memory_space=pltpu.SMEM)] + [in_any] * (2 + count) + [in_vmem] * len(sums),
        out_specs=(in_vmem, in_vmem),
        scratch_shapes=[
            pltpu.VMEM((2, tok_rows, deep), BF),
            pltpu.VMEM((deep, width), BF),
            pltpu.SemaphoreType.DMA((2, len(groups))),
            pltpu.SemaphoreType.DMA((count,)),
        ],
        input_output_aliases={} if total is None or last else {3 + count: 0},
        compiler_params=pltpu.CompilerParams(vmem_limit_bytes=20 * 2**20),
        cost_estimate=pl.CostEstimate(
            flops=4 * tok_rows * deep * width, bytes_accessed=4 * tok_rows * deep, transcendentals=0
        ),
    )(places, tokens, theirs, *flat, *sums)


def project(tokens, key_down, value_down, prepare, inputs):
    chips = lax.axis_size("chip")
    chip = lax.axis_index("chip")
    core = lax.axis_index("core")
    first = core == 0
    shard = key_down.shape[0]
    rows = CORES * shard
    own = jnp.where(first, key_down, value_down)
    got = lax.ppermute(jnp.where(first, value_down, key_down), "core", SWAP)
    if chips > 8:
        theirs = lax.ppermute(tokens, "core", SWAP)
        block = jnp.concatenate([jnp.where(first, own, got), jnp.where(first, got, own)], 0)
        full = lax.all_gather(block, "chip", axis=0, tiled=True)
        mine, other = mm(tokens, full).astype(BF), mm(theirs, full).astype(BF)
        return jnp.concatenate([jnp.where(first, mine, other), jnp.where(first, other, mine)], 0), prepare(*inputs)
    cycle = list(range(0, chips, 2)) + list(range(chips - 1, 0, -2))
    last = chips - 1
    place = jnp.where(chip & 1 == 0, chip >> 1, last - (chip >> 1))
    chains = 2
    piece = shard // chains
    right = [(cycle[i], cycle[(i + 1) % chips]) for i in range(chips)]
    left = [(b, a) for a, b in right]
    ways = [right] * chains + [left] * chains

    def start_of(way, step):
        spot = place - step if way == 0 else place + step
        spot = jnp.where(spot < 0, spot + chips, jnp.where(spot > last, spot - chips, spot))
        source = jnp.where(spot < chips // 2, 2 * spot, 2 * (last - spot) + 1)
        return source * rows + (core if way == 0 else 1 - core) * shard

    held = [own[k * piece : (k + 1) * piece] for k in range(chains)]
    held += [got[k * piece : (k + 1) * piece] for k in range(chains)]
    todo = [(start_of(0, 0), [own]), (start_of(1, 0), [got])]
    total = None
    mark = None
    for step in range(1, chips):
        if step == 2:
            held, tokens_later = lax.optimization_barrier((held, tokens))
            theirs = lax.ppermute(tokens_later, "core", SWAP)
        if step == 3:
            _, inputs = lax.optimization_barrier((held[0], inputs))
            early = prepare(*inputs)
        if step == 5:
            held[0], early = lax.optimization_barrier((held[0], early))
        for k in range(2 * chains):
            if mark is not None:
                held[k], _ = lax.optimization_barrier((held[k], mark))
            held[k] = lax.ppermute(held[k], "chip", ways[k])
        arriving = [(start_of(w, step), held[w * chains : (w + 1) * chains]) for w in range(2)]
        todo += arriving
        if step >= 3:
            ready, todo = (todo[:4], todo[4:]) if total is None else (todo[:2], todo[2:])
            total, mark = add_pieces(tokens, theirs, ready, total)
    total, _ = add_pieces(tokens, theirs, todo[:2], total)
    return add_pieces(tokens, theirs, todo[2:], total, core)[0], early


def attend(have, got, core, key_up, value_up, query, bounds, chips):
    heads, rows = query.shape[:2]
    tokens = have.shape[0]
    pairs = rows // 8
    blocks = pairs * heads // chips
    scale = 1.0 / DH**0.5

    def kernel(core_ref, have_ref, got_ref, key_up_ref, value_up_ref, query_ref, bounds_ref, out_ref):
        first = core_ref[0] == 0
        have, got = have_ref[...], got_ref[...]
        keys = mm(jnp.where(first, have, got), key_up_ref[...]).astype(BF)
        values = mm(jnp.where(first, got, have), value_up_ref[...]).astype(BF)
        position = lax.broadcasted_iota(jnp.int32, (tokens, rows), 0)
        visible = (position >= bounds_ref[0:1, :]) & (position < bounds_ref[1:2, :])
        tops, totals = [], []
        for g in range(heads):
            lanes = slice(g * DH, (g + 1) * DH)
            scores = scale * lax.dot_general(
                keys[:, lanes], query_ref[g], (((1,), (1,)), ((), ())), preferred_element_type=F32
            )
            scores = jnp.where(visible, scores, -1e30)
            top = jnp.max(scores, 0, keepdims=True)
            weights = jnp.where(visible, jnp.exp(scores - top), 0.0)
            tops.append(top)
            totals.append(jnp.sum(weights, 0, keepdims=True))
            summed = lax.dot_general(
                weights.astype(BF), values[:, lanes], (((0,), (0,)), ((), ())), preferred_element_type=F32
            )
            for pair in range(pairs):
                block = pair * heads + g
                out_ref[block // blocks, block % blocks] = summed[pair * 8 : (pair + 1) * 8]
        stats = jnp.transpose(jnp.concatenate(tops + totals, 0))
        stride = min(blocks, heads)
        for chip in range(chips):
            spots = [divmod(b, heads) for b in range(chip * blocks, (chip + 1) * blocks, stride)]
            sides = [
                stats[pair * 8 : (pair + 1) * 8, side + g : side + g + stride] for side in (0, heads) for pair, g in spots
            ]
            out_ref[chip, blocks] = jnp.zeros((8, DH), F32)
            out_ref[chip, blocks, :, : 2 * blocks] = jnp.concatenate(sides, 1)

    in_vmem = pl.BlockSpec(memory_space=pltpu.VMEM)
    return pl.pallas_call(
        kernel,
        out_shape=jax.ShapeDtypeStruct((chips, blocks + 1, 8, DH), F32),
        in_specs=[pl.BlockSpec(memory_space=pltpu.SMEM)] + [in_vmem] * 6,
        out_specs=in_vmem,
        compiler_params=pltpu.CompilerParams(vmem_limit_bytes=16 * 2**20),
        cost_estimate=pl.CostEstimate(
            flops=4 * tokens * (have.shape[1] * heads * DH + heads * rows * DH),
            bytes_accessed=4 * tokens * have.shape[1],
            transcendentals=tokens * heads * rows,
        ),
    )(core.reshape(1), have, got, key_up, value_up, query, bounds)


def merge(arrived, fresh_stats, fresh_summed):
    chips, blocks = arrived.shape[0], arrived.shape[1] - 1

    def kernel(arrived_ref, stats_ref, summed_ref, out_ref):
        results = []
        for b in range(blocks):
            top = arrived_ref[:, blocks, :, b : b + 1]
            total = arrived_ref[:, blocks, :, blocks + b : blocks + b + 1]
            fresh_top = stats_ref[:, b : b + 1]
            overall = jnp.maximum(jnp.max(top, 0), fresh_top)
            carried = jnp.exp(top - overall[None])
            fresh_carried = jnp.exp(fresh_top - overall)
            total = jnp.sum(total * carried, 0) + stats_ref[:, blocks + b : blocks + b + 1] * fresh_carried
            summed = jnp.sum(arrived_ref[:, b] * carried, 0) + summed_ref[b * 8 : (b + 1) * 8, :] * fresh_carried
            results.append(summed / total)
        out_ref[...] = jnp.concatenate(results, 0).astype(BF)

    in_vmem = pl.BlockSpec(memory_space=pltpu.VMEM)
    return pl.pallas_call(
        kernel,
        out_shape=jax.ShapeDtypeStruct((blocks * 8, DH), BF),
        in_specs=[in_vmem] * 3,
        out_specs=in_vmem,
        compiler_params=pltpu.CompilerParams(vmem_limit_bytes=8 * 2**20),
        cost_estimate=pl.CostEstimate(
            flops=2 * chips * blocks * 8 * DH, bytes_accessed=4 * arrived.size, transcendentals=chips * blocks * 8
        ),
    )(arrived, fresh_stats, fresh_summed)


def on_device(tokens, key_down, value_down, key_up, value_up, prompt_lens, queries, new_latent):
    chips = lax.axis_size("chip")
    chip = lax.axis_index("chip")
    core = lax.axis_index("core")
    first = core == 0
    tok_rows = tokens.shape[0]
    lat_width = key_down.shape[1]
    group = QH // KVH
    heads = KVH // CORES
    scale = 1.0 / DH**0.5
    steps_count, req_count = (queries.shape[0], queries.shape[1])
    pairs = steps_count * req_count
    rows = pairs * heads * group
    share = rows // chips

    def my_heads(queries, key_up, value_up):
        mine = lax.dynamic_slice_in_dim(queries, core * heads * group * DH, heads * group * DH, 2)
        mine = mine.reshape(steps_count, req_count, heads, group, DH).transpose(2, 0, 1, 3, 4)
        ups = [lax.dynamic_slice_in_dim(x, core * heads * DH, heads * DH, 1) for x in (key_up, value_up)]
        return mine, *ups

    have, early = project(tokens, key_down, value_down, my_heads, (queries, key_up, value_up))
    query, key_up, value_up = early
    got = lax.ppermute(have, "core", SWAP)

    offsets = jnp.cumsum(prompt_lens) - prompt_lens
    bounds = jnp.stack([offsets, offsets + prompt_lens]) - chip * CORES * tok_rows
    bounds = jnp.broadcast_to(bounds[:, None, :, None], (2, steps_count, req_count, group)).reshape(2, -1)
    sending = attend(have, got, core, key_up, value_up, query.reshape(heads, -1, DH), bounds, chips)

    _, new_latent = lax.optimization_barrier((have, new_latent))
    flat_new = new_latent.reshape(pairs, 2 * lat_width)
    new_keys = mm(flat_new[:, :lat_width], key_up).astype(BF).reshape(steps_count, req_count, heads, DH)
    new_values = mm(flat_new[:, lat_width:], value_up).astype(BF).reshape(steps_count, req_count, heads, DH)
    causal = (jnp.arange(steps_count)[:, None] >= jnp.arange(steps_count)[None, :])[:, None, None, None, :]
    fresh = jnp.einsum("gsrjd,urgd->srgju", query, new_keys, preferred_element_type=F32) * scale
    fresh = jnp.where(causal, fresh, -1e30)
    fresh_top = jnp.max(fresh, -1)
    fresh_weights = jnp.where(causal, jnp.exp(fresh - fresh_top[..., None]), 0.0)
    fresh_total = jnp.sum(fresh_weights, -1)
    fresh_summed = jnp.einsum("srgju,urgd->srgjd", fresh_weights.astype(BF), new_values, preferred_element_type=F32)

    def my_share(x):
        return lax.dynamic_slice_in_dim(x, chip * share, share, 0)

    fresh_summed = my_share(fresh_summed.reshape(rows, DH))
    fresh_stats = [my_share(x.reshape(rows)).reshape(-1, group).T for x in (fresh_top, fresh_total)]
    fresh_stats = jnp.pad(jnp.concatenate(fresh_stats, 1), ((0, 0), (0, DH - 2 * share // group)))

    flat = sending.reshape(chips, -1, DH)
    arrived = lax.all_to_all(flat, "chip", split_axis=0, concat_axis=0, tiled=True).reshape(sending.shape)
    result = merge(arrived, fresh_stats, fresh_summed)

    if chips == 8:
        near = lax.ppermute(result, "chip", [(c, c ^ 1) for c in range(chips)])
        upper = chip & 1 == 1
        couple = jnp.concatenate([jnp.where(upper, near, result), jnp.where(upper, result, near)], 0)
        far = [couple] + [lax.ppermute(couple, "chip", [(c, c ^ (2 * d)) for c in range(chips)]) for d in range(1, 4)]
        odd, high = chip & 2 != 0, chip & 4 != 0

        def of(z):
            return jnp.where(high, jnp.where(odd, far[z ^ 3], far[z ^ 2]), jnp.where(odd, far[z ^ 1], far[z]))

        whole = jnp.concatenate([of(z) for z in range(4)], 0)
    else:
        whole = lax.all_gather(result, "chip", axis=0, tiled=True)
    whole = whole.reshape(pairs, 1, rows // pairs * DH)
    away = lax.ppermute(whole, "core", SWAP)
    whole = jnp.concatenate([jnp.where(first, whole, away), jnp.where(first, away, whole)], 1)
    return whole.reshape(steps_count, req_count, QH * DH)


def solution(mesh):
    groups, n_ctx = mesh.shape["groups"], mesh.shape["ctx"]
    split = Mesh(mesh.devices.reshape(groups, n_ctx // CORES, CORES), ("groups", "chip", "core"))
    ctx = ("chip", "core")
    return jax.shard_map(
        on_device,
        mesh=split,
        in_specs=(
            P(("groups",) + ctx, None),
            P(ctx, None),
            P(ctx, None),
            P(),
            P(),
            P("groups"),
            P(None, "groups", None),
            P(None, "groups", None),
        ),
        out_specs=P(None, "groups", None),
        check_vma=False,
    )
```

```python
import jax
import jax.numpy as jnp
from jax import lax
from jax.experimental import pallas as pl
from jax.experimental.pallas import tpu as pltpu
from jax.sharding import Mesh, PartitionSpec as P

QH = 64
KVH = 8
DH = 128
CORES = 2
BF = jnp.bfloat16
F32 = jnp.float32
SWAP = [(0, 1), (1, 0)]


def mm(a, b):
    return jnp.dot(a, b, preferred_element_type=F32)


def add_pieces(tokens, theirs, groups, total, core=None):
    tok_rows = tokens.shape[0]
    width = groups[0][1][0].shape[1]
    depths = [[part.shape[0] for part in parts] for _, parts in groups]
    span = sum(depths[0])
    deep = span * len(groups)
    flat = [part for _, parts in groups for part in parts]
    count = len(flat)
    last = core is not None
    places = jnp.stack([start for start, _ in groups] + ([core * tok_rows, (1 - core) * tok_rows] if last else []))

    def kernel(places_ref, mine_ref, theirs_ref, *refs):
        parts = refs[:count]
        total_ref, out_ref, mark_ref, columns, weights, sems, loaded = (
            refs[count:] if total is not None else (None,) + refs[count:]
        )
        copies = []
        for j, source in enumerate((mine_ref, theirs_ref)):
            for g in range(len(groups)):
                start = pl.multiple_of(places_ref[g], 128)
                copy = pltpu.make_async_copy(
                    source.at[:, pl.ds(start, span)], columns.at[j, :, pl.ds(g * span, span)], sems.at[j, g]
                )
                copy.start()
                copies.append(copy)
        at = 0
        loads = []
        for k, part in enumerate(parts):
            load = pltpu.make_async_copy(part, weights.at[pl.ds(at, part.shape[0])], loaded.at[k])
            load.start()
            loads.append(load)
            at += part.shape[0]
        mark_ref[...] = jnp.zeros_like(mark_ref)
        for load in loads:
            load.wait()
        for j in range(2):
            for g in range(len(groups)):
                copies[j * len(groups) + g].wait()
            rows = pl.ds(j * tok_rows, tok_rows)
            term = mm(columns[j], weights[...])
            if total is not None:
                term = total_ref[rows, :] + term
            if last:
                rows = pl.ds(pl.multiple_of(places_ref[len(groups) + j], tok_rows), tok_rows)
            out_ref[rows, :] = term.astype(out_ref.dtype)

    tokens = pltpu.with_memory_space_constraint(tokens, pltpu.HBM)
    if total is None:
        flat = flat[:2] + [pltpu.with_memory_space_constraint(x, pltpu.HBM) for x in flat[2:]]
    in_vmem = pl.BlockSpec(memory_space=pltpu.VMEM)
    in_any = pl.BlockSpec(memory_space=pl.ANY)
    sums = [] if total is None else [total]
    return pl.pallas_call(
        kernel,
        out_shape=(
            jax.ShapeDtypeStruct((2 * tok_rows, width), BF if last else F32),
            jax.ShapeDtypeStruct((8, 128), F32),
        ),
        in_specs=[pl.BlockSpec(memory_space=pltpu.SMEM)] + [in_any] * (2 + count) + [in_vmem] * len(sums),
        out_specs=(in_vmem, in_vmem),
        scratch_shapes=[
            pltpu.VMEM((2, tok_rows, deep), BF),
            pltpu.VMEM((deep, width), BF),
            pltpu.SemaphoreType.DMA((2, len(groups))),
            pltpu.SemaphoreType.DMA((count,)),
        ],
        input_output_aliases={} if total is None or last else {3 + count: 0},
        compiler_params=pltpu.CompilerParams(vmem_limit_bytes=20 * 2**20),
        cost_estimate=pl.CostEstimate(
            flops=4 * tok_rows * deep * width, bytes_accessed=4 * tok_rows * deep, transcendentals=0
        ),
    )(places, tokens, theirs, *flat, *sums)


def project(tokens, key_down, value_down, prepare, inputs):
    chips = lax.axis_size("chip")
    chip = lax.axis_index("chip")
    core = lax.axis_index("core")
    first = core == 0
    shard = key_down.shape[0]
    rows = CORES * shard
    own = jnp.where(first, key_down, value_down)
    got = lax.ppermute(jnp.where(first, value_down, key_down), "core", SWAP)
    if chips > 8:
        theirs = lax.ppermute(tokens, "core", SWAP)
        block = jnp.concatenate([jnp.where(first, own, got), jnp.where(first, got, own)], 0)
        full = lax.all_gather(block, "chip", axis=0, tiled=True)
        mine, other = mm(tokens, full).astype(BF), mm(theirs, full).astype(BF)
        return jnp.concatenate([jnp.where(first, mine, other), jnp.where(first, other, mine)], 0), prepare(*inputs)
    cycle = list(range(0, chips, 2)) + list(range(chips - 1, 0, -2))
    last = chips - 1
    place = jnp.where(chip & 1 == 0, chip >> 1, last - (chip >> 1))
    chains = 2
    piece = shard // chains
    right = [(cycle[i], cycle[(i + 1) % chips]) for i in range(chips)]
    left = [(b, a) for a, b in right]
    ways = [right] * chains + [left] * chains

    def start_of(way, step):
        spot = place - step if way == 0 else place + step
        spot = jnp.where(spot < 0, spot + chips, jnp.where(spot > last, spot - chips, spot))
        source = jnp.where(spot < chips // 2, 2 * spot, 2 * (last - spot) + 1)
        return source * rows + (core if way == 0 else 1 - core) * shard

    held = [own[k * piece : (k + 1) * piece] for k in range(chains)]
    held += [got[k * piece : (k + 1) * piece] for k in range(chains)]
    todo = [(start_of(0, 0), [own]), (start_of(1, 0), [got])]
    total = None
    mark = None
    for step in range(1, chips):
        if step == 2:
            held, tokens_later = lax.optimization_barrier((held, tokens))
            theirs = lax.ppermute(tokens_later, "core", SWAP)
        if step == 3:
            _, inputs = lax.optimization_barrier((held[0], inputs))
            early = prepare(*inputs)
        if step == 5:
            held[0], early = lax.optimization_barrier((held[0], early))
        for k in range(2 * chains):
            if mark is not None:
                held[k], _ = lax.optimization_barrier((held[k], mark))
            held[k] = lax.ppermute(held[k], "chip", ways[k])
        arriving = [(start_of(w, step), held[w * chains : (w + 1) * chains]) for w in range(2)]
        todo += arriving
        if step >= 3:
            taken = 4 if step in (3, 4) else 2
            ready, todo = todo[:taken], todo[taken:]
            total, mark = add_pieces(tokens, theirs, ready, total)
    return add_pieces(tokens, theirs, todo, total, core)[0], early


def attend(have, got, core, key_up, value_up, query, bounds, chips):
    heads, rows = query.shape[:2]
    tokens = have.shape[0]
    pairs = rows // 8
    blocks = pairs * heads // chips
    scale = 1.0 / DH**0.5

    def kernel(core_ref, have_ref, got_ref, key_up_ref, value_up_ref, query_ref, bounds_ref, out_ref):
        first = core_ref[0] == 0
        have, got = have_ref[...], got_ref[...]
        keys = mm(jnp.where(first, have, got), key_up_ref[...]).astype(BF)
        values = mm(jnp.where(first, got, have), value_up_ref[...]).astype(BF)
        position = lax.broadcasted_iota(jnp.int32, (tokens, rows), 0)
        visible = (position >= bounds_ref[0:1, :]) & (position < bounds_ref[1:2, :])
        tops, totals = [], []
        for g in range(heads):
            lanes = slice(g * DH, (g + 1) * DH)
            scores = scale * lax.dot_general(
                keys[:, lanes], query_ref[g], (((1,), (1,)), ((), ())), preferred_element_type=F32
            )
            scores = jnp.where(visible, scores, -1e30)
            top = jnp.max(scores, 0, keepdims=True)
            weights = jnp.where(visible, jnp.exp(scores - top), 0.0)
            tops.append(top)
            totals.append(jnp.sum(weights, 0, keepdims=True))
            summed = lax.dot_general(
                weights.astype(BF), values[:, lanes], (((0,), (0,)), ((), ())), preferred_element_type=F32
            )
            for pair in range(pairs):
                block = pair * heads + g
                out_ref[block // blocks, block % blocks] = summed[pair * 8 : (pair + 1) * 8]
        stats = jnp.transpose(jnp.concatenate(tops + totals, 0))
        stride = min(blocks, heads)
        for chip in range(chips):
            spots = [divmod(b, heads) for b in range(chip * blocks, (chip + 1) * blocks, stride)]
            sides = [
                stats[pair * 8 : (pair + 1) * 8, side + g : side + g + stride] for side in (0, heads) for pair, g in spots
            ]
            out_ref[chip, blocks] = jnp.zeros((8, DH), F32)
            out_ref[chip, blocks, :, : 2 * blocks] = jnp.concatenate(sides, 1)

    in_vmem = pl.BlockSpec(memory_space=pltpu.VMEM)
    return pl.pallas_call(
        kernel,
        out_shape=jax.ShapeDtypeStruct((chips, blocks + 1, 8, DH), F32),
        in_specs=[pl.BlockSpec(memory_space=pltpu.SMEM)] + [in_vmem] * 6,
        out_specs=in_vmem,
        compiler_params=pltpu.CompilerParams(vmem_limit_bytes=16 * 2**20),
        cost_estimate=pl.CostEstimate(
            flops=4 * tokens * (have.shape[1] * heads * DH + heads * rows * DH),
            bytes_accessed=4 * tokens * have.shape[1],
            transcendentals=tokens * heads * rows,
        ),
    )(core.reshape(1), have, got, key_up, value_up, query, bounds)


def merge(arrived, fresh_stats, fresh_summed):
    chips, blocks = arrived.shape[0], arrived.shape[1] - 1

    def kernel(arrived_ref, stats_ref, summed_ref, out_ref):
        results = []
        for b in range(blocks):
            top = arrived_ref[:, blocks, :, b : b + 1]
            total = arrived_ref[:, blocks, :, blocks + b : blocks + b + 1]
            fresh_top = stats_ref[:, b : b + 1]
            overall = jnp.maximum(jnp.max(top, 0), fresh_top)
            carried = jnp.exp(top - overall[None])
            fresh_carried = jnp.exp(fresh_top - overall)
            total = jnp.sum(total * carried, 0) + stats_ref[:, blocks + b : blocks + b + 1] * fresh_carried
            summed = jnp.sum(arrived_ref[:, b] * carried, 0) + summed_ref[b * 8 : (b + 1) * 8, :] * fresh_carried
            results.append(summed / total)
        out_ref[...] = jnp.concatenate(results, 0).astype(BF)

    in_vmem = pl.BlockSpec(memory_space=pltpu.VMEM)
    return pl.pallas_call(
        kernel,
        out_shape=jax.ShapeDtypeStruct((blocks * 8, DH), BF),
        in_specs=[in_vmem] * 3,
        out_specs=in_vmem,
        compiler_params=pltpu.CompilerParams(vmem_limit_bytes=8 * 2**20),
        cost_estimate=pl.CostEstimate(
            flops=2 * chips * blocks * 8 * DH, bytes_accessed=4 * arrived.size, transcendentals=chips * blocks * 8
        ),
    )(arrived, fresh_stats, fresh_summed)


def on_device(tokens, key_down, value_down, key_up, value_up, prompt_lens, queries, new_latent):
    chips = lax.axis_size("chip")
    chip = lax.axis_index("chip")
    core = lax.axis_index("core")
    first = core == 0
    tok_rows = tokens.shape[0]
    lat_width = key_down.shape[1]
    group = QH // KVH
    heads = KVH // CORES
    scale = 1.0 / DH**0.5
    steps_count, req_count = (queries.shape[0], queries.shape[1])
    pairs = steps_count * req_count
    rows = pairs * heads * group
    share = rows // chips

    def my_heads(queries, key_up, value_up):
        mine = lax.dynamic_slice_in_dim(queries, core * heads * group * DH, heads * group * DH, 2)
        mine = mine.reshape(steps_count, req_count, heads, group, DH).transpose(2, 0, 1, 3, 4)
        ups = [lax.dynamic_slice_in_dim(x, core * heads * DH, heads * DH, 1) for x in (key_up, value_up)]
        return mine, *ups

    have, early = project(tokens, key_down, value_down, my_heads, (queries, key_up, value_up))
    query, key_up, value_up = early
    got = lax.ppermute(have, "core", SWAP)

    offsets = jnp.cumsum(prompt_lens) - prompt_lens
    bounds = jnp.stack([offsets, offsets + prompt_lens]) - chip * CORES * tok_rows
    bounds = jnp.broadcast_to(bounds[:, None, :, None], (2, steps_count, req_count, group)).reshape(2, -1)
    sending = attend(have, got, core, key_up, value_up, query.reshape(heads, -1, DH), bounds, chips)

    _, new_latent = lax.optimization_barrier((have, new_latent))
    flat_new = new_latent.reshape(pairs, 2 * lat_width)
    new_keys = mm(flat_new[:, :lat_width], key_up).astype(BF).reshape(steps_count, req_count, heads, DH)
    new_values = mm(flat_new[:, lat_width:], value_up).astype(BF).reshape(steps_count, req_count, heads, DH)
    causal = (jnp.arange(steps_count)[:, None] >= jnp.arange(steps_count)[None, :])[:, None, None, None, :]
    fresh = jnp.einsum("gsrjd,urgd->srgju", query, new_keys, preferred_element_type=F32) * scale
    fresh = jnp.where(causal, fresh, -1e30)
    fresh_top = jnp.max(fresh, -1)
    fresh_weights = jnp.where(causal, jnp.exp(fresh - fresh_top[..., None]), 0.0)
    fresh_total = jnp.sum(fresh_weights, -1)
    fresh_summed = jnp.einsum("srgju,urgd->srgjd", fresh_weights.astype(BF), new_values, preferred_element_type=F32)

    def my_share(x):
        return lax.dynamic_slice_in_dim(x, chip * share, share, 0)

    fresh_summed = my_share(fresh_summed.reshape(rows, DH))
    fresh_stats = [my_share(x.reshape(rows)).reshape(-1, group).T for x in (fresh_top, fresh_total)]
    fresh_stats = jnp.pad(jnp.concatenate(fresh_stats, 1), ((0, 0), (0, DH - 2 * share // group)))

    flat = sending.reshape(chips, -1, DH)
    arrived = lax.all_to_all(flat, "chip", split_axis=0, concat_axis=0, tiled=True).reshape(sending.shape)
    result = merge(arrived, fresh_stats, fresh_summed)

    if chips == 8:
        near = lax.ppermute(result, "chip", [(c, c ^ 1) for c in range(chips)])
        upper = chip & 1 == 1
        couple = jnp.concatenate([jnp.where(upper, near, result), jnp.where(upper, result, near)], 0)
        far = [couple] + [lax.ppermute(couple, "chip", [(c, c ^ (2 * d)) for c in range(chips)]) for d in range(1, 4)]
        odd, high = chip & 2 != 0, chip & 4 != 0

        def of(z):
            return jnp.where(high, jnp.where(odd, far[z ^ 3], far[z ^ 2]), jnp.where(odd, far[z ^ 1], far[z]))

        whole = jnp.concatenate([of(z) for z in range(4)], 0)
    else:
        whole = lax.all_gather(result, "chip", axis=0, tiled=True)
    whole = whole.reshape(pairs, 1, rows // pairs * DH)
    away = lax.ppermute(whole, "core", SWAP)
    whole = jnp.concatenate([jnp.where(first, whole, away), jnp.where(first, away, whole)], 1)
    return whole.reshape(steps_count, req_count, QH * DH)


def solution(mesh):
    groups, n_ctx = mesh.shape["groups"], mesh.shape["ctx"]
    split = Mesh(mesh.devices.reshape(groups, n_ctx // CORES, CORES), ("groups", "chip", "core"))
    ctx = ("chip", "core")
    return jax.shard_map(
        on_device,
        mesh=split,
        in_specs=(
            P(("groups",) + ctx, None),
            P(ctx, None),
            P(ctx, None),
            P(),
            P(),
            P("groups"),
            P(None, "groups", None),
            P(None, "groups", None),
        ),
        out_specs=P(None, "groups", None),
        check_vma=False,
    )
```

```python
import jax
import jax.numpy as jnp
from jax import lax
from jax.experimental import pallas as pl
from jax.experimental.pallas import tpu as pltpu
from jax.sharding import Mesh, PartitionSpec as P

QH = 64
KVH = 8
DH = 128
CORES = 2
BF = jnp.bfloat16
F32 = jnp.float32
SWAP = [(0, 1), (1, 0)]


def mm(a, b):
    return jnp.dot(a, b, preferred_element_type=F32)


def add_pieces(tokens, theirs, groups, total, core=None):
    tok_rows = tokens.shape[0]
    width = groups[0][1][0].shape[1]
    depths = [[part.shape[0] for part in parts] for _, parts in groups]
    span = sum(depths[0])
    deep = span * len(groups)
    flat = [part for _, parts in groups for part in parts]
    count = len(flat)
    last = core is not None
    places = jnp.stack([start for start, _ in groups] + ([core * tok_rows, (1 - core) * tok_rows] if last else []))

    def kernel(places_ref, mine_ref, theirs_ref, *refs):
        parts = refs[:count]
        total_ref, out_ref, mark_ref, columns, weights, sems, loaded = (
            refs[count:] if total is not None else (None,) + refs[count:]
        )
        copies = []
        for j, source in enumerate((mine_ref, theirs_ref)):
            for g in range(len(groups)):
                start = pl.multiple_of(places_ref[g], 128)
                copy = pltpu.make_async_copy(
                    source.at[:, pl.ds(start, span)], columns.at[j, :, pl.ds(g * span, span)], sems.at[j, g]
                )
                copy.start()
                copies.append(copy)
        at = 0
        loads = []
        for k, part in enumerate(parts):
            load = pltpu.make_async_copy(part, weights.at[pl.ds(at, part.shape[0])], loaded.at[k])
            load.start()
            loads.append(load)
            at += part.shape[0]
        mark_ref[...] = jnp.zeros_like(mark_ref)
        for load in loads:
            load.wait()
        for j in range(2):
            for g in range(len(groups)):
                copies[j * len(groups) + g].wait()
            rows = pl.ds(j * tok_rows, tok_rows)
            term = mm(columns[j], weights[...])
            if total is not None:
                term = total_ref[rows, :] + term
            if last:
                rows = pl.ds(pl.multiple_of(places_ref[len(groups) + j], tok_rows), tok_rows)
            out_ref[rows, :] = term.astype(out_ref.dtype)

    tokens = pltpu.with_memory_space_constraint(tokens, pltpu.HBM)
    if total is None:
        flat = flat[:2] + [pltpu.with_memory_space_constraint(x, pltpu.HBM) for x in flat[2:]]
    in_vmem = pl.BlockSpec(memory_space=pltpu.VMEM)
    in_any = pl.BlockSpec(memory_space=pl.ANY)
    sums = [] if total is None else [total]
    return pl.pallas_call(
        kernel,
        out_shape=(
            jax.ShapeDtypeStruct((2 * tok_rows, width), BF if last else F32),
            jax.ShapeDtypeStruct((8, 128), F32),
        ),
        in_specs=[pl.BlockSpec(memory_space=pltpu.SMEM)] + [in_any] * (2 + count) + [in_vmem] * len(sums),
        out_specs=(in_vmem, in_vmem),
        scratch_shapes=[
            pltpu.VMEM((2, tok_rows, deep), BF),
            pltpu.VMEM((deep, width), BF),
            pltpu.SemaphoreType.DMA((2, len(groups))),
            pltpu.SemaphoreType.DMA((count,)),
        ],
        input_output_aliases={} if total is None or last else {3 + count: 0},
        compiler_params=pltpu.CompilerParams(vmem_limit_bytes=20 * 2**20),
        cost_estimate=pl.CostEstimate(
            flops=4 * tok_rows * deep * width, bytes_accessed=4 * tok_rows * deep, transcendentals=0
        ),
    )(places, tokens, theirs, *flat, *sums)


def project(tokens, key_down, value_down, prepare, inputs):
    chips = lax.axis_size("chip")
    chip = lax.axis_index("chip")
    core = lax.axis_index("core")
    first = core == 0
    shard = key_down.shape[0]
    rows = CORES * shard
    own = jnp.where(first, key_down, value_down)
    got = lax.ppermute(jnp.where(first, value_down, key_down), "core", SWAP)
    if chips > 8:
        theirs = lax.ppermute(tokens, "core", SWAP)
        block = jnp.concatenate([jnp.where(first, own, got), jnp.where(first, got, own)], 0)
        full = lax.all_gather(block, "chip", axis=0, tiled=True)
        mine, other = mm(tokens, full).astype(BF), mm(theirs, full).astype(BF)
        return jnp.concatenate([jnp.where(first, mine, other), jnp.where(first, other, mine)], 0), prepare(*inputs)
    cycle = list(range(0, chips, 2)) + list(range(chips - 1, 0, -2))
    last = chips - 1
    place = jnp.where(chip & 1 == 0, chip >> 1, last - (chip >> 1))
    chains = 2
    piece = shard // chains
    right = [(cycle[i], cycle[(i + 1) % chips]) for i in range(chips)]
    left = [(b, a) for a, b in right]
    ways = [right] * chains + [left] * chains

    def start_of(way, step):
        spot = place - step if way == 0 else place + step
        spot = jnp.where(spot < 0, spot + chips, jnp.where(spot > last, spot - chips, spot))
        source = jnp.where(spot < chips // 2, 2 * spot, 2 * (last - spot) + 1)
        return source * rows + (core if way == 0 else 1 - core) * shard

    held = [own[k * piece : (k + 1) * piece] for k in range(chains)]
    held += [got[k * piece : (k + 1) * piece] for k in range(chains)]
    todo = [(start_of(0, 0), [own]), (start_of(1, 0), [got])]
    total = None
    mark = None
    for step in range(1, chips):
        if step == 2:
            held, tokens_later = lax.optimization_barrier((held, tokens))
            theirs = lax.ppermute(tokens_later, "core", SWAP)
        if step == 3:
            _, inputs = lax.optimization_barrier((held[0], inputs))
            early = prepare(*inputs)
        if step == 5:
            held[0], early = lax.optimization_barrier((held[0], early))
        for k in range(2 * chains):
            if mark is not None:
                held[k], _ = lax.optimization_barrier((held[k], mark))
            held[k] = lax.ppermute(held[k], "chip", ways[k])
        arriving = [(start_of(w, step), held[w * chains : (w + 1) * chains]) for w in range(2)]
        todo += arriving
        if step >= 3:
            taken = 4 if step in (3, last) else 2
            ready, todo = todo[:taken], todo[taken:]
            total, mark = add_pieces(tokens, theirs, ready, total)
    return add_pieces(tokens, theirs, todo, total, core)[0], early


def attend(have, got, core, key_up, value_up, query, bounds, chips):
    heads, rows = query.shape[:2]
    tokens = have.shape[0]
    pairs = rows // 8
    blocks = pairs * heads // chips
    scale = 1.0 / DH**0.5

    def kernel(core_ref, have_ref, got_ref, key_up_ref, value_up_ref, query_ref, bounds_ref, out_ref):
        first = core_ref[0] == 0
        have, got = have_ref[...], got_ref[...]
        keys = mm(jnp.where(first, have, got), key_up_ref[...]).astype(BF)
        values = mm(jnp.where(first, got, have), value_up_ref[...]).astype(BF)
        position = lax.broadcasted_iota(jnp.int32, (tokens, rows), 0)
        visible = (position >= bounds_ref[0:1, :]) & (position < bounds_ref[1:2, :])
        tops, totals = [], []
        for g in range(heads):
            lanes = slice(g * DH, (g + 1) * DH)
            scores = scale * lax.dot_general(
                keys[:, lanes], query_ref[g], (((1,), (1,)), ((), ())), preferred_element_type=F32
            )
            scores = jnp.where(visible, scores, -1e30)
            top = jnp.max(scores, 0, keepdims=True)
            weights = jnp.where(visible, jnp.exp(scores - top), 0.0)
            tops.append(top)
            totals.append(jnp.sum(weights, 0, keepdims=True))
            summed = lax.dot_general(
                weights.astype(BF), values[:, lanes], (((0,), (0,)), ((), ())), preferred_element_type=F32
            )
            for pair in range(pairs):
                block = pair * heads + g
                out_ref[block // blocks, block % blocks] = summed[pair * 8 : (pair + 1) * 8]
        stats = jnp.transpose(jnp.concatenate(tops + totals, 0))
        stride = min(blocks, heads)
        for chip in range(chips):
            spots = [divmod(b, heads) for b in range(chip * blocks, (chip + 1) * blocks, stride)]
            sides = [
                stats[pair * 8 : (pair + 1) * 8, side + g : side + g + stride] for side in (0, heads) for pair, g in spots
            ]
            out_ref[chip, blocks] = jnp.zeros((8, DH), F32)
            out_ref[chip, blocks, :, : 2 * blocks] = jnp.concatenate(sides, 1)

    in_vmem = pl.BlockSpec(memory_space=pltpu.VMEM)
    return pl.pallas_call(
        kernel,
        out_shape=jax.ShapeDtypeStruct((chips, blocks + 1, 8, DH), F32),
        in_specs=[pl.BlockSpec(memory_space=pltpu.SMEM)] + [in_vmem] * 6,
        out_specs=in_vmem,
        compiler_params=pltpu.CompilerParams(vmem_limit_bytes=16 * 2**20),
        cost_estimate=pl.CostEstimate(
            flops=4 * tokens * (have.shape[1] * heads * DH + heads * rows * DH),
            bytes_accessed=4 * tokens * have.shape[1],
            transcendentals=tokens * heads * rows,
        ),
    )(core.reshape(1), have, got, key_up, value_up, query, bounds)


def merge(arrived, fresh_stats, fresh_summed):
    chips, blocks = arrived.shape[0], arrived.shape[1] - 1

    def kernel(arrived_ref, stats_ref, summed_ref, out_ref):
        results = []
        for b in range(blocks):
            top = arrived_ref[:, blocks, :, b : b + 1]
            total = arrived_ref[:, blocks, :, blocks + b : blocks + b + 1]
            fresh_top = stats_ref[:, b : b + 1]
            overall = jnp.maximum(jnp.max(top, 0), fresh_top)
            carried = jnp.exp(top - overall[None])
            fresh_carried = jnp.exp(fresh_top - overall)
            total = jnp.sum(total * carried, 0) + stats_ref[:, blocks + b : blocks + b + 1] * fresh_carried
            summed = jnp.sum(arrived_ref[:, b] * carried, 0) + summed_ref[b * 8 : (b + 1) * 8, :] * fresh_carried
            results.append(summed / total)
        out_ref[...] = jnp.concatenate(results, 0).astype(BF)

    in_vmem = pl.BlockSpec(memory_space=pltpu.VMEM)
    return pl.pallas_call(
        kernel,
        out_shape=jax.ShapeDtypeStruct((blocks * 8, DH), BF),
        in_specs=[in_vmem] * 3,
        out_specs=in_vmem,
        compiler_params=pltpu.CompilerParams(vmem_limit_bytes=8 * 2**20),
        cost_estimate=pl.CostEstimate(
            flops=2 * chips * blocks * 8 * DH, bytes_accessed=4 * arrived.size, transcendentals=chips * blocks * 8
        ),
    )(arrived, fresh_stats, fresh_summed)


def on_device(tokens, key_down, value_down, key_up, value_up, prompt_lens, queries, new_latent):
    chips = lax.axis_size("chip")
    chip = lax.axis_index("chip")
    core = lax.axis_index("core")
    first = core == 0
    tok_rows = tokens.shape[0]
    lat_width = key_down.shape[1]
    group = QH // KVH
    heads = KVH // CORES
    scale = 1.0 / DH**0.5
    steps_count, req_count = (queries.shape[0], queries.shape[1])
    pairs = steps_count * req_count
    rows = pairs * heads * group
    share = rows // chips

    def my_heads(queries, key_up, value_up):
        mine = lax.dynamic_slice_in_dim(queries, core * heads * group * DH, heads * group * DH, 2)
        mine = mine.reshape(steps_count, req_count, heads, group, DH).transpose(2, 0, 1, 3, 4)
        ups = [lax.dynamic_slice_in_dim(x, core * heads * DH, heads * DH, 1) for x in (key_up, value_up)]
        return mine, *ups

    have, early = project(tokens, key_down, value_down, my_heads, (queries, key_up, value_up))
    query, key_up, value_up = early
    got = lax.ppermute(have, "core", SWAP)

    offsets = jnp.cumsum(prompt_lens) - prompt_lens
    bounds = jnp.stack([offsets, offsets + prompt_lens]) - chip * CORES * tok_rows
    bounds = jnp.broadcast_to(bounds[:, None, :, None], (2, steps_count, req_count, group)).reshape(2, -1)
    sending = attend(have, got, core, key_up, value_up, query.reshape(heads, -1, DH), bounds, chips)

    _, new_latent = lax.optimization_barrier((have, new_latent))
    flat_new = new_latent.reshape(pairs, 2 * lat_width)
    new_keys = mm(flat_new[:, :lat_width], key_up).astype(BF).reshape(steps_count, req_count, heads, DH)
    new_values = mm(flat_new[:, lat_width:], value_up).astype(BF).reshape(steps_count, req_count, heads, DH)
    causal = (jnp.arange(steps_count)[:, None] >= jnp.arange(steps_count)[None, :])[:, None, None, None, :]
    fresh = jnp.einsum("gsrjd,urgd->srgju", query, new_keys, preferred_element_type=F32) * scale
    fresh = jnp.where(causal, fresh, -1e30)
    fresh_top = jnp.max(fresh, -1)
    fresh_weights = jnp.where(causal, jnp.exp(fresh - fresh_top[..., None]), 0.0)
    fresh_total = jnp.sum(fresh_weights, -1)
    fresh_summed = jnp.einsum("srgju,urgd->srgjd", fresh_weights.astype(BF), new_values, preferred_element_type=F32)

    def my_share(x):
        return lax.dynamic_slice_in_dim(x, chip * share, share, 0)

    fresh_summed = my_share(fresh_summed.reshape(rows, DH))
    fresh_stats = [my_share(x.reshape(rows)).reshape(-1, group).T for x in (fresh_top, fresh_total)]
    fresh_stats = jnp.pad(jnp.concatenate(fresh_stats, 1), ((0, 0), (0, DH - 2 * share // group)))

    flat = sending.reshape(chips, -1, DH)
    arrived = lax.all_to_all(flat, "chip", split_axis=0, concat_axis=0, tiled=True).reshape(sending.shape)
    result = merge(arrived, fresh_stats, fresh_summed)

    if chips == 8:
        near = lax.ppermute(result, "chip", [(c, c ^ 1) for c in range(chips)])
        upper = chip & 1 == 1
        couple = jnp.concatenate([jnp.where(upper, near, result), jnp.where(upper, result, near)], 0)
        far = [couple] + [lax.ppermute(couple, "chip", [(c, c ^ (2 * d)) for c in range(chips)]) for d in range(1, 4)]
        odd, high = chip & 2 != 0, chip & 4 != 0

        def of(z):
            return jnp.where(high, jnp.where(odd, far[z ^ 3], far[z ^ 2]), jnp.where(odd, far[z ^ 1], far[z]))

        whole = jnp.concatenate([of(z) for z in range(4)], 0)
    else:
        whole = lax.all_gather(result, "chip", axis=0, tiled=True)
    whole = whole.reshape(pairs, 1, rows // pairs * DH)
    away = lax.ppermute(whole, "core", SWAP)
    whole = jnp.concatenate([jnp.where(first, whole, away), jnp.where(first, away, whole)], 1)
    return whole.reshape(steps_count, req_count, QH * DH)


def solution(mesh):
    groups, n_ctx = mesh.shape["groups"], mesh.shape["ctx"]
    split = Mesh(mesh.devices.reshape(groups, n_ctx // CORES, CORES), ("groups", "chip", "core"))
    ctx = ("chip", "core")
    return jax.shard_map(
        on_device,
        mesh=split,
        in_specs=(
            P(("groups",) + ctx, None),
            P(ctx, None),
            P(ctx, None),
            P(),
            P(),
            P("groups"),
            P(None, "groups", None),
            P(None, "groups", None),
        ),
        out_specs=P(None, "groups", None),
        check_vma=False,
    )
```

```python
import jax
import jax.numpy as jnp
from jax import lax
from jax.experimental import pallas as pl
from jax.experimental.pallas import tpu as pltpu
from jax.sharding import Mesh, PartitionSpec as P

QH = 64
KVH = 8
DH = 128
CORES = 2
BF = jnp.bfloat16
F32 = jnp.float32
SWAP = [(0, 1), (1, 0)]


def mm(a, b):
    return jnp.dot(a, b, preferred_element_type=F32)


def add_pieces(tokens, theirs, groups, total, core=None):
    tok_rows = tokens.shape[0]
    width = groups[0][1][0].shape[1]
    depths = [[part.shape[0] for part in parts] for _, parts in groups]
    span = sum(depths[0])
    deep = span * len(groups)
    flat = [part for _, parts in groups for part in parts]
    count = len(flat)
    last = core is not None
    places = jnp.stack([start for start, _ in groups] + ([core * tok_rows, (1 - core) * tok_rows] if last else []))

    def kernel(places_ref, mine_ref, theirs_ref, *refs):
        parts = refs[:count]
        total_ref, out_ref, mark_ref, columns, weights, sems, loaded = (
            refs[count:] if total is not None else (None,) + refs[count:]
        )
        copies = []
        for j, source in enumerate((mine_ref, theirs_ref)):
            for g in range(len(groups)):
                start = pl.multiple_of(places_ref[g], 128)
                copy = pltpu.make_async_copy(
                    source.at[:, pl.ds(start, span)], columns.at[j, :, pl.ds(g * span, span)], sems.at[j, g]
                )
                copy.start()
                copies.append(copy)
        at = 0
        loads = []
        for k, part in enumerate(parts):
            load = pltpu.make_async_copy(part, weights.at[pl.ds(at, part.shape[0])], loaded.at[k])
            load.start()
            loads.append(load)
            at += part.shape[0]
        mark_ref[...] = jnp.zeros_like(mark_ref)
        for load in loads:
            load.wait()
        for j in range(2):
            for g in range(len(groups)):
                copies[j * len(groups) + g].wait()
            rows = pl.ds(j * tok_rows, tok_rows)
            term = mm(columns[j], weights[...])
            if total is not None:
                term = total_ref[rows, :] + term
            if last:
                rows = pl.ds(pl.multiple_of(places_ref[len(groups) + j], tok_rows), tok_rows)
            out_ref[rows, :] = term.astype(out_ref.dtype)

    tokens = pltpu.with_memory_space_constraint(tokens, pltpu.HBM)
    if total is None:
        flat = flat[:2] + [pltpu.with_memory_space_constraint(x, pltpu.HBM) for x in flat[2:]]
    in_vmem = pl.BlockSpec(memory_space=pltpu.VMEM)
    in_any = pl.BlockSpec(memory_space=pl.ANY)
    sums = [] if total is None else [total]
    return pl.pallas_call(
        kernel,
        out_shape=(
            jax.ShapeDtypeStruct((2 * tok_rows, width), BF if last else F32),
            jax.ShapeDtypeStruct((8, 128), F32),
        ),
        in_specs=[pl.BlockSpec(memory_space=pltpu.SMEM)] + [in_any] * (2 + count) + [in_vmem] * len(sums),
        out_specs=(in_vmem, in_vmem),
        scratch_shapes=[
            pltpu.VMEM((2, tok_rows, deep), BF),
            pltpu.VMEM((deep, width), BF),
            pltpu.SemaphoreType.DMA((2, len(groups))),
            pltpu.SemaphoreType.DMA((count,)),
        ],
        input_output_aliases={} if total is None or last else {3 + count: 0},
        compiler_params=pltpu.CompilerParams(vmem_limit_bytes=20 * 2**20),
        cost_estimate=pl.CostEstimate(
            flops=4 * tok_rows * deep * width, bytes_accessed=4 * tok_rows * deep, transcendentals=0
        ),
    )(places, tokens, theirs, *flat, *sums)


def project(tokens, key_down, value_down, prepare, inputs):
    chips = lax.axis_size("chip")
    chip = lax.axis_index("chip")
    core = lax.axis_index("core")
    first = core == 0
    shard = key_down.shape[0]
    rows = CORES * shard
    own = jnp.where(first, key_down, value_down)
    got = lax.ppermute(jnp.where(first, value_down, key_down), "core", SWAP)
    if chips > 8:
        theirs = lax.ppermute(tokens, "core", SWAP)
        block = jnp.concatenate([jnp.where(first, own, got), jnp.where(first, got, own)], 0)
        full = lax.all_gather(block, "chip", axis=0, tiled=True)
        mine, other = mm(tokens, full).astype(BF), mm(theirs, full).astype(BF)
        return jnp.concatenate([jnp.where(first, mine, other), jnp.where(first, other, mine)], 0), prepare(*inputs)
    cycle = list(range(0, chips, 2)) + list(range(chips - 1, 0, -2))
    last = chips - 1
    place = jnp.where(chip & 1 == 0, chip >> 1, last - (chip >> 1))
    chains = 2
    piece = shard // chains
    right = [(cycle[i], cycle[(i + 1) % chips]) for i in range(chips)]
    left = [(b, a) for a, b in right]
    ways = [right] * chains + [left] * chains

    def start_of(way, step):
        spot = place - step if way == 0 else place + step
        spot = jnp.where(spot < 0, spot + chips, jnp.where(spot > last, spot - chips, spot))
        source = jnp.where(spot < chips // 2, 2 * spot, 2 * (last - spot) + 1)
        return source * rows + (core if way == 0 else 1 - core) * shard

    held = [own[k * piece : (k + 1) * piece] for k in range(chains)]
    held += [got[k * piece : (k + 1) * piece] for k in range(chains)]
    todo = [(start_of(0, 0), [own]), (start_of(1, 0), [got])]
    total = None
    mark = None
    for step in range(1, chips):
        if step == 2:
            held, tokens_later = lax.optimization_barrier((held, tokens))
            theirs = lax.ppermute(tokens_later, "core", SWAP)
        if step == 3:
            _, inputs = lax.optimization_barrier((held[0], inputs))
            early = prepare(*inputs)
        if step == 5:
            held[0], early = lax.optimization_barrier((held[0], early))
        for k in range(2 * chains):
            if mark is not None:
                held[k], _ = lax.optimization_barrier((held[k], mark))
            held[k] = lax.ppermute(held[k], "chip", ways[k])
        arriving = [(start_of(w, step), held[w * chains : (w + 1) * chains]) for w in range(2)]
        todo += arriving
        if step >= 3:
            taken = 4 if step in (3, last) else 2
            ready, todo = todo[:taken], todo[taken:]
            total, mark = add_pieces(tokens, theirs, ready, total)
    return add_pieces(tokens, theirs, todo, total, core)[0], early


def attend(have, got, core, key_up, value_up, query, bounds, chips):
    heads, rows = query.shape[:2]
    tokens = have.shape[0]
    pairs = rows // 8
    blocks = pairs * heads // chips
    scale = 1.0 / DH**0.5

    def kernel(core_ref, have_ref, got_ref, key_up_ref, value_up_ref, query_ref, bounds_ref, out_ref):
        first = core_ref[0] == 0
        have, got = have_ref[...], got_ref[...]
        keys = mm(jnp.where(first, have, got), key_up_ref[...]).astype(BF)
        values = mm(jnp.where(first, got, have), value_up_ref[...]).astype(BF)
        position = lax.broadcasted_iota(jnp.int32, (tokens, rows), 0)
        visible = (position >= bounds_ref[0:1, :]) & (position < bounds_ref[1:2, :])
        tops, totals = [], []
        for g in range(heads):
            lanes = slice(g * DH, (g + 1) * DH)
            scores = scale * lax.dot_general(
                keys[:, lanes], query_ref[g], (((1,), (1,)), ((), ())), preferred_element_type=F32
            )
            scores = jnp.where(visible, scores, -1e30)
            top = jnp.max(scores, 0, keepdims=True)
            weights = jnp.where(visible, jnp.exp(scores - top), 0.0)
            tops.append(top)
            totals.append(jnp.sum(weights, 0, keepdims=True))
            summed = lax.dot_general(
                weights.astype(BF), values[:, lanes], (((0,), (0,)), ((), ())), preferred_element_type=F32
            )
            for pair in range(pairs):
                block = pair * heads + g
                out_ref[block // blocks, block % blocks] = summed[pair * 8 : (pair + 1) * 8]
        stats = jnp.transpose(jnp.concatenate(tops + totals, 0))
        stride = min(blocks, heads)
        for chip in range(chips):
            spots = [divmod(b, heads) for b in range(chip * blocks, (chip + 1) * blocks, stride)]
            sides = [
                stats[pair * 8 : (pair + 1) * 8, side + g : side + g + stride] for side in (0, heads) for pair, g in spots
            ]
            out_ref[chip, blocks] = jnp.zeros((8, DH), F32)
            out_ref[chip, blocks, :, : 2 * blocks] = jnp.concatenate(sides, 1)

    in_vmem = pl.BlockSpec(memory_space=pltpu.VMEM)
    return pl.pallas_call(
        kernel,
        out_shape=jax.ShapeDtypeStruct((chips, blocks + 1, 8, DH), F32),
        in_specs=[pl.BlockSpec(memory_space=pltpu.SMEM)] + [in_vmem] * 6,
        out_specs=in_vmem,
        compiler_params=pltpu.CompilerParams(vmem_limit_bytes=16 * 2**20),
        cost_estimate=pl.CostEstimate(
            flops=4 * tokens * (have.shape[1] * heads * DH + heads * rows * DH),
            bytes_accessed=4 * tokens * have.shape[1],
            transcendentals=tokens * heads * rows,
        ),
    )(core.reshape(1), have, got, key_up, value_up, query, bounds)


def merge(arrived, fresh_stats, fresh_summed):
    chips, blocks = arrived.shape[0], arrived.shape[1] - 1

    def kernel(arrived_ref, stats_ref, summed_ref, out_ref):
        results = []
        for b in range(blocks):
            top = arrived_ref[:, blocks, :, b : b + 1]
            total = arrived_ref[:, blocks, :, blocks + b : blocks + b + 1]
            fresh_top = stats_ref[:, b : b + 1]
            overall = jnp.maximum(jnp.max(top, 0), fresh_top)
            carried = jnp.exp(top - overall[None])
            fresh_carried = jnp.exp(fresh_top - overall)
            total = jnp.sum(total * carried, 0) + stats_ref[:, blocks + b : blocks + b + 1] * fresh_carried
            summed = jnp.sum(arrived_ref[:, b] * carried, 0) + summed_ref[b * 8 : (b + 1) * 8, :] * fresh_carried
            results.append(summed / total)
        out_ref[...] = jnp.concatenate(results, 0).astype(BF)

    in_vmem = pl.BlockSpec(memory_space=pltpu.VMEM)
    return pl.pallas_call(
        kernel,
        out_shape=jax.ShapeDtypeStruct((blocks * 8, DH), BF),
        in_specs=[in_vmem] * 3,
        out_specs=in_vmem,
        compiler_params=pltpu.CompilerParams(vmem_limit_bytes=8 * 2**20),
        cost_estimate=pl.CostEstimate(
            flops=2 * chips * blocks * 8 * DH, bytes_accessed=4 * arrived.size, transcendentals=chips * blocks * 8
        ),
    )(arrived, fresh_stats, fresh_summed)


def on_device(tokens, key_down, value_down, key_up, value_up, prompt_lens, queries, new_latent):
    chips = lax.axis_size("chip")
    chip = lax.axis_index("chip")
    core = lax.axis_index("core")
    first = core == 0
    tok_rows = tokens.shape[0]
    lat_width = key_down.shape[1]
    group = QH // KVH
    heads = KVH // CORES
    scale = 1.0 / DH**0.5
    steps_count, req_count = (queries.shape[0], queries.shape[1])
    pairs = steps_count * req_count
    rows = pairs * heads * group
    share = rows // chips

    def my_heads(queries, key_up, value_up):
        mine = lax.dynamic_slice_in_dim(queries, core * heads * group * DH, heads * group * DH, 2)
        mine = mine.reshape(steps_count, req_count, heads, group, DH).transpose(2, 0, 1, 3, 4)
        ups = [lax.dynamic_slice_in_dim(x, core * heads * DH, heads * DH, 1) for x in (key_up, value_up)]
        return mine, *ups

    have, early = project(tokens, key_down, value_down, my_heads, (queries, key_up, value_up))
    query, key_up, value_up = early
    got = lax.ppermute(have, "core", SWAP)

    offsets = jnp.cumsum(prompt_lens) - prompt_lens
    bounds = jnp.stack([offsets, offsets + prompt_lens]) - chip * CORES * tok_rows
    bounds = jnp.broadcast_to(bounds[:, None, :, None], (2, steps_count, req_count, group)).reshape(2, -1)
    sending = attend(have, got, core, key_up, value_up, query.reshape(heads, -1, DH), bounds, chips)

    _, new_latent = lax.optimization_barrier((have, new_latent))
    flat_new = new_latent.reshape(pairs, 2 * lat_width)
    new_keys = mm(flat_new[:, :lat_width], key_up).astype(BF).reshape(steps_count, req_count, heads, DH)
    new_values = mm(flat_new[:, lat_width:], value_up).astype(BF).reshape(steps_count, req_count, heads, DH)
    causal = (jnp.arange(steps_count)[:, None] >= jnp.arange(steps_count)[None, :])[:, None, None, None, :]
    fresh = jnp.einsum("gsrjd,urgd->srgju", query, new_keys, preferred_element_type=F32) * scale
    fresh = jnp.where(causal, fresh, -1e30)
    fresh_top = jnp.max(fresh, -1)
    fresh_weights = jnp.where(causal, jnp.exp(fresh - fresh_top[..., None]), 0.0)
    fresh_total = jnp.sum(fresh_weights, -1)
    fresh_summed = jnp.einsum("srgju,urgd->srgjd", fresh_weights.astype(BF), new_values, preferred_element_type=F32)

    def my_share(x):
        return lax.dynamic_slice_in_dim(x, chip * share, share, 0)

    fresh_summed = my_share(fresh_summed.reshape(rows, DH))
    fresh_stats = [my_share(x.reshape(rows)).reshape(-1, group).T for x in (fresh_top, fresh_total)]
    fresh_stats = jnp.pad(jnp.concatenate(fresh_stats, 1), ((0, 0), (0, DH - 2 * share // group)))

    arrived = lax.all_to_all(sending, "chip", split_axis=0, concat_axis=0, tiled=True)
    result = merge(arrived, fresh_stats, fresh_summed)

    if chips == 8:
        near = lax.ppermute(result, "chip", [(c, c ^ 1) for c in range(chips)])
        upper = chip & 1 == 1
        couple = jnp.concatenate([jnp.where(upper, near, result), jnp.where(upper, result, near)], 0)
        far = [couple] + [lax.ppermute(couple, "chip", [(c, c ^ (2 * d)) for c in range(chips)]) for d in range(1, 4)]
        odd, high = chip & 2 != 0, chip & 4 != 0

        def of(z):
            return jnp.where(high, jnp.where(odd, far[z ^ 3], far[z ^ 2]), jnp.where(odd, far[z ^ 1], far[z]))

        whole = jnp.concatenate([of(z) for z in range(4)], 0)
    else:
        whole = lax.all_gather(result, "chip", axis=0, tiled=True)
    whole = whole.reshape(pairs, 1, rows // pairs * DH)
    away = lax.ppermute(whole, "core", SWAP)
    whole = jnp.concatenate([jnp.where(first, whole, away), jnp.where(first, away, whole)], 1)
    return whole.reshape(steps_count, req_count, QH * DH)


def solution(mesh):
    groups, n_ctx = mesh.shape["groups"], mesh.shape["ctx"]
    split = Mesh(mesh.devices.reshape(groups, n_ctx // CORES, CORES), ("groups", "chip", "core"))
    ctx = ("chip", "core")
    return jax.shard_map(
        on_device,
        mesh=split,
        in_specs=(
            P(("groups",) + ctx, None),
            P(ctx, None),
            P(ctx, None),
            P(),
            P(),
            P("groups"),
            P(None, "groups", None),
            P(None, "groups", None),
        ),
        out_specs=P(None, "groups", None),
        check_vma=False,
    )
```

```python
import jax
import jax.numpy as jnp
from jax import lax
from jax.experimental import pallas as pl
from jax.experimental.pallas import tpu as pltpu
from jax.sharding import Mesh, PartitionSpec as P

QH = 64
KVH = 8
DH = 128
CORES = 2
BF = jnp.bfloat16
F32 = jnp.float32
SWAP = [(0, 1), (1, 0)]


def mm(a, b):
    return jnp.dot(a, b, preferred_element_type=F32)


def add_pieces(tokens, theirs, groups, total, core=None):
    tok_rows = tokens.shape[0]
    width = groups[0][1][0].shape[1]
    depths = [[part.shape[0] for part in parts] for _, parts in groups]
    span = sum(depths[0])
    deep = span * len(groups)
    flat = [part for _, parts in groups for part in parts]
    count = len(flat)
    last = core is not None
    places = jnp.stack([start for start, _ in groups] + ([core * tok_rows, (1 - core) * tok_rows] if last else []))

    def kernel(places_ref, mine_ref, theirs_ref, *refs):
        parts = refs[:count]
        total_ref, out_ref, mark_ref, columns, weights, sems, loaded = (
            refs[count:] if total is not None else (None,) + refs[count:]
        )
        copies = []
        for j, source in enumerate((mine_ref, theirs_ref)):
            for g in range(len(groups)):
                start = pl.multiple_of(places_ref[g], 128)
                copy = pltpu.make_async_copy(
                    source.at[:, pl.ds(start, span)], columns.at[j, :, pl.ds(g * span, span)], sems.at[j, g]
                )
                copy.start()
                copies.append(copy)
        at = 0
        loads = []
        for k, part in enumerate(parts):
            load = pltpu.make_async_copy(part, weights.at[pl.ds(at, part.shape[0])], loaded.at[k])
            load.start()
            loads.append(load)
            at += part.shape[0]
        mark_ref[...] = jnp.zeros_like(mark_ref)
        for load in loads:
            load.wait()
        for j in range(2):
            for g in range(len(groups)):
                copies[j * len(groups) + g].wait()
            rows = pl.ds(j * tok_rows, tok_rows)
            term = mm(columns[j], weights[...])
            if total is not None:
                term = total_ref[rows, :] + term
            if last:
                rows = pl.ds(pl.multiple_of(places_ref[len(groups) + j], tok_rows), tok_rows)
            out_ref[rows, :] = term.astype(out_ref.dtype)

    tokens = pltpu.with_memory_space_constraint(tokens, pltpu.HBM)
    if total is None:
        flat = flat[:2] + [pltpu.with_memory_space_constraint(x, pltpu.HBM) for x in flat[2:]]
    in_vmem = pl.BlockSpec(memory_space=pltpu.VMEM)
    in_any = pl.BlockSpec(memory_space=pl.ANY)
    sums = [] if total is None else [total]
    return pl.pallas_call(
        kernel,
        out_shape=(
            jax.ShapeDtypeStruct((2 * tok_rows, width), BF if last else F32),
            jax.ShapeDtypeStruct((8, 128), F32),
        ),
        in_specs=[pl.BlockSpec(memory_space=pltpu.SMEM)] + [in_any] * (2 + count) + [in_vmem] * len(sums),
        out_specs=(in_vmem, in_vmem),
        scratch_shapes=[
            pltpu.VMEM((2, tok_rows, deep), BF),
            pltpu.VMEM((deep, width), BF),
            pltpu.SemaphoreType.DMA((2, len(groups))),
            pltpu.SemaphoreType.DMA((count,)),
        ],
        input_output_aliases={} if total is None or last else {3 + count: 0},
        compiler_params=pltpu.CompilerParams(vmem_limit_bytes=20 * 2**20),
        cost_estimate=pl.CostEstimate(
            flops=4 * tok_rows * deep * width, bytes_accessed=4 * tok_rows * deep, transcendentals=0
        ),
    )(places, tokens, theirs, *flat, *sums)


def project(tokens, key_down, value_down, prepare, inputs):
    chips = lax.axis_size("chip")
    chip = lax.axis_index("chip")
    core = lax.axis_index("core")
    first = core == 0
    shard = key_down.shape[0]
    rows = CORES * shard
    own = jnp.where(first, key_down, value_down)
    got = lax.ppermute(jnp.where(first, value_down, key_down), "core", SWAP)
    if chips > 8:
        theirs = lax.ppermute(tokens, "core", SWAP)
        block = jnp.concatenate([jnp.where(first, own, got), jnp.where(first, got, own)], 0)
        full = lax.all_gather(block, "chip", axis=0, tiled=True)
        mine, other = mm(tokens, full).astype(BF), mm(theirs, full).astype(BF)
        return jnp.concatenate([jnp.where(first, mine, other), jnp.where(first, other, mine)], 0), prepare(*inputs)
    cycle = list(range(0, chips, 2)) + list(range(chips - 1, 0, -2))
    last = chips - 1
    place = jnp.where(chip & 1 == 0, chip >> 1, last - (chip >> 1))
    chains = 2
    piece = shard // chains
    right = [(cycle[i], cycle[(i + 1) % chips]) for i in range(chips)]
    left = [(b, a) for a, b in right]
    ways = [right] * chains + [left] * chains

    def start_of(way, step):
        spot = place - step if way == 0 else place + step
        spot = jnp.where(spot < 0, spot + chips, jnp.where(spot > last, spot - chips, spot))
        source = jnp.where(spot < chips // 2, 2 * spot, 2 * (last - spot) + 1)
        return source * rows + (core if way == 0 else 1 - core) * shard

    held = [own[k * piece : (k + 1) * piece] for k in range(chains)]
    held += [got[k * piece : (k + 1) * piece] for k in range(chains)]
    todo = [(start_of(0, 0), [own]), (start_of(1, 0), [got])]
    total = None
    mark = None
    for step in range(1, chips):
        if step == 2:
            held, tokens_later = lax.optimization_barrier((held, tokens))
            theirs = lax.ppermute(tokens_later, "core", SWAP)
        if step == 3:
            _, inputs = lax.optimization_barrier((held[0], inputs))
            early = prepare(*inputs)
        if step == 5:
            held[0], early = lax.optimization_barrier((held[0], early))
        for k in range(2 * chains):
            if mark is not None:
                held[k], _ = lax.optimization_barrier((held[k], mark))
            held[k] = lax.ppermute(held[k], "chip", ways[k])
        arriving = [(start_of(w, step), held[w * chains : (w + 1) * chains]) for w in range(2)]
        todo += arriving
        if step >= 3:
            taken = 4 if step in (3, last) else 2
            ready, todo = todo[:taken], todo[taken:]
            total, mark = add_pieces(tokens, theirs, ready, total)
    return add_pieces(tokens, theirs, todo, total, core)[0], early


def attend(have, got, core, key_up, value_up, query, bounds, chips):
    heads, rows = query.shape[:2]
    tokens = have.shape[0]
    pairs = rows // 8
    blocks = pairs * heads // chips
    scale = 1.0 / DH**0.5

    def kernel(core_ref, have_ref, got_ref, key_up_ref, value_up_ref, query_ref, bounds_ref, out_ref):
        first = core_ref[0] == 0
        have, got = have_ref[...], got_ref[...]
        keys = mm(jnp.where(first, have, got), key_up_ref[...]).astype(BF)
        values = mm(jnp.where(first, got, have), value_up_ref[...]).astype(BF)
        position = lax.broadcasted_iota(jnp.int32, (tokens, rows), 0)
        visible = (position >= bounds_ref[0:1, :]) & (position < bounds_ref[1:2, :])
        tops, totals = [], []
        for g in range(heads):
            lanes = slice(g * DH, (g + 1) * DH)
            scores = scale * lax.dot_general(
                keys[:, lanes], query_ref[g], (((1,), (1,)), ((), ())), preferred_element_type=F32
            )
            scores = jnp.where(visible, scores, -1e30)
            top = jnp.max(scores, 0, keepdims=True)
            weights = jnp.where(visible, jnp.exp(scores - top), 0.0)
            tops.append(top)
            totals.append(jnp.sum(weights, 0, keepdims=True))
            summed = lax.dot_general(
                weights.astype(BF), values[:, lanes], (((0,), (0,)), ((), ())), preferred_element_type=F32
            )
            for pair in range(pairs):
                block = pair * heads + g
                out_ref[block // blocks, block % blocks] = summed[pair * 8 : (pair + 1) * 8]
        stats = jnp.transpose(jnp.concatenate(tops + totals, 0))
        stride = min(blocks, heads)
        for chip in range(chips):
            spots = [divmod(b, heads) for b in range(chip * blocks, (chip + 1) * blocks, stride)]
            sides = [
                stats[pair * 8 : (pair + 1) * 8, side + g : side + g + stride] for side in (0, heads) for pair, g in spots
            ]
            out_ref[chip, blocks] = jnp.zeros((8, DH), F32)
            out_ref[chip, blocks, :, : 2 * blocks] = jnp.concatenate(sides, 1)

    in_vmem = pl.BlockSpec(memory_space=pltpu.VMEM)
    return pl.pallas_call(
        kernel,
        out_shape=jax.ShapeDtypeStruct((chips, blocks + 1, 8, DH), F32),
        in_specs=[pl.BlockSpec(memory_space=pltpu.SMEM)] + [in_vmem] * 6,
        out_specs=in_vmem,
        compiler_params=pltpu.CompilerParams(vmem_limit_bytes=16 * 2**20),
        cost_estimate=pl.CostEstimate(
            flops=4 * tokens * (have.shape[1] * heads * DH + heads * rows * DH),
            bytes_accessed=4 * tokens * have.shape[1],
            transcendentals=tokens * heads * rows,
        ),
    )(core.reshape(1), have, got, key_up, value_up, query, bounds)


def merge(arrived, fresh_stats, fresh_summed):
    chips, blocks = arrived.shape[0], arrived.shape[1] - 1

    def kernel(arrived_ref, stats_ref, summed_ref, out_ref):
        results = []
        for b in range(blocks):
            top = arrived_ref[:, blocks, :, b : b + 1]
            total = arrived_ref[:, blocks, :, blocks + b : blocks + b + 1]
            fresh_top = stats_ref[:, b : b + 1]
            overall = jnp.maximum(jnp.max(top, 0), fresh_top)
            carried = jnp.exp(top - overall[None])
            fresh_carried = jnp.exp(fresh_top - overall)
            total = jnp.sum(total * carried, 0) + stats_ref[:, blocks + b : blocks + b + 1] * fresh_carried
            summed = jnp.sum(arrived_ref[:, b] * carried, 0) + summed_ref[b * 8 : (b + 1) * 8, :] * fresh_carried
            results.append(summed / total)
        out_ref[...] = jnp.concatenate(results, 0).astype(BF)

    in_vmem = pl.BlockSpec(memory_space=pltpu.VMEM)
    return pl.pallas_call(
        kernel,
        out_shape=jax.ShapeDtypeStruct((blocks * 8, DH), BF),
        in_specs=[in_vmem] * 3,
        out_specs=in_vmem,
        compiler_params=pltpu.CompilerParams(vmem_limit_bytes=8 * 2**20),
        cost_estimate=pl.CostEstimate(
            flops=2 * chips * blocks * 8 * DH, bytes_accessed=4 * arrived.size, transcendentals=chips * blocks * 8
        ),
    )(arrived, fresh_stats, fresh_summed)


def on_device(tokens, key_down, value_down, key_up, value_up, prompt_lens, queries, new_latent):
    chips = lax.axis_size("chip")
    chip = lax.axis_index("chip")
    core = lax.axis_index("core")
    first = core == 0
    tok_rows = tokens.shape[0]
    lat_width = key_down.shape[1]
    group = QH // KVH
    heads = KVH // CORES
    scale = 1.0 / DH**0.5
    steps_count, req_count = (queries.shape[0], queries.shape[1])
    pairs = steps_count * req_count
    rows = pairs * heads * group
    share = rows // chips

    def my_heads(queries, key_up, value_up):
        mine = lax.dynamic_slice_in_dim(queries, core * heads * group * DH, heads * group * DH, 2)
        mine = mine.reshape(steps_count, req_count, heads, group, DH).transpose(2, 0, 1, 3, 4)
        ups = [lax.dynamic_slice_in_dim(x, core * heads * DH, heads * DH, 1) for x in (key_up, value_up)]
        return mine, *ups

    have, early = project(tokens, key_down, value_down, my_heads, (queries, key_up, value_up))
    query, key_up, value_up = early
    got = lax.ppermute(have, "core", SWAP)

    offsets = jnp.cumsum(prompt_lens) - prompt_lens
    bounds = jnp.stack([offsets, offsets + prompt_lens]) - chip * CORES * tok_rows
    bounds = jnp.broadcast_to(bounds[:, None, :, None], (2, steps_count, req_count, group)).reshape(2, -1)
    sending = attend(have, got, core, key_up, value_up, query.reshape(heads, -1, DH), bounds, chips)

    _, new_latent = lax.optimization_barrier((have, new_latent))
    flat_new = new_latent.reshape(pairs, 2 * lat_width)
    new_keys = mm(flat_new[:, :lat_width], key_up).astype(BF).reshape(steps_count, req_count, heads, DH)
    new_values = mm(flat_new[:, lat_width:], value_up).astype(BF).reshape(steps_count, req_count, heads, DH)
    causal = (jnp.arange(steps_count)[:, None] >= jnp.arange(steps_count)[None, :])[:, None, None, None, :]
    fresh = jnp.einsum("gsrjd,urgd->srgju", query, new_keys, preferred_element_type=F32) * scale
    fresh = jnp.where(causal, fresh, -1e30)
    fresh_top = jnp.max(fresh, -1)
    fresh_weights = jnp.where(causal, jnp.exp(fresh - fresh_top[..., None]), 0.0)
    fresh_total = jnp.sum(fresh_weights, -1)
    fresh_summed = jnp.einsum("srgju,urgd->srgjd", fresh_weights.astype(BF), new_values, preferred_element_type=F32)

    def my_share(x):
        return lax.dynamic_slice_in_dim(x, chip * share, share, 0)

    fresh_summed = my_share(fresh_summed.reshape(rows, DH))
    fresh_stats = [my_share(x.reshape(rows)).reshape(-1, group).T for x in (fresh_top, fresh_total)]
    fresh_stats = jnp.pad(jnp.concatenate(fresh_stats, 1), ((0, 0), (0, DH - 2 * share // group)))

    arrived = lax.all_to_all(sending, "chip", split_axis=0, concat_axis=0, tiled=True)
    result = merge(arrived, fresh_stats, fresh_summed)

    if chips == 8:
        near = lax.ppermute(result, "chip", [(c, c ^ 1) for c in range(chips)])
        upper = chip & 1 == 1
        couple = jnp.concatenate([jnp.where(upper, near, result), jnp.where(upper, result, near)], 0)
        far = [couple] + [lax.ppermute(couple, "chip", [(c, c ^ (2 * d)) for c in range(chips)]) for d in range(1, 4)]
        odd, high = chip & 2 != 0, chip & 4 != 0

        def of(z):
            return jnp.where(high, jnp.where(odd, far[z ^ 3], far[z ^ 2]), jnp.where(odd, far[z ^ 1], far[z]))

        whole = jnp.concatenate([of(z) for z in range(4)], 0)
    else:
        whole = lax.all_gather(result, "chip", axis=0, tiled=True)
    whole = whole.reshape(pairs, 1, rows // pairs, DH)
    away = lax.ppermute(whole, "core", SWAP)
    whole = jnp.concatenate([jnp.where(first, whole, away), jnp.where(first, away, whole)], 1)
    return whole.reshape(steps_count, req_count, QH * DH)


def solution(mesh):
    groups, n_ctx = mesh.shape["groups"], mesh.shape["ctx"]
    split = Mesh(mesh.devices.reshape(groups, n_ctx // CORES, CORES), ("groups", "chip", "core"))
    ctx = ("chip", "core")
    return jax.shard_map(
        on_device,
        mesh=split,
        in_specs=(
            P(("groups",) + ctx, None),
            P(ctx, None),
            P(ctx, None),
            P(),
            P(),
            P("groups"),
            P(None, "groups", None),
            P(None, "groups", None),
        ),
        out_specs=P(None, "groups", None),
        check_vma=False,
    )
```
